32 devices in a mesh: lat: 4 (over y, x), lon: 8 (over z, core).
Axes of the slice: x: 2, y: 2, z: 4, core: 2. Of those that a mesh axis runs over, the one named last changes fastest.
Arguments:
- state: bfloat16 [32, 128, 256], P('lat', 'lon'), may hold values from -6 to 6
- weight_first: bfloat16 [9, 256, 256], replicated, may hold values from -0.125 to 0.125
- weight_second: bfloat16 [9, 256, 256], replicated, may hold values from -0.125 to 0.125
- obs_owner: int32 [4096, 1], P(('lat', 'lon')), may hold values from 0 to 31; in each aligned block of 128 rows (0 to 127, 128 to 255, ...) at most 6 rows name the same one
- obs_cell: int32 [4096, 32], P(('lat', 'lon')), may hold values from 0 to 110, as said below
- obs_level: int32 [4096, 32], P(('lat', 'lon')), may hold values from 0 to 255
- obs_count: int32 [4096], P(('lat', 'lon')), may hold values from 1 to 32
- obs_frac: float32 [4096, 2, 32], P(('lat', 'lon')), may hold values from 0 to 1
- obs_value: float32 [4096, 32], P(('lat', 'lon')), may hold values from -6 to 6
- obs_weight: float32 [4096, 32], P(('lat', 'lon')), may hold values from 0.1 to 1
Outputs:
- state_grad: float32 [32, 128, 256], P('lat', 'lon')
- grad_first: float32 [9, 256, 256], replicated
- grad_second: float32 [9, 256, 256], replicated
The draws below stay inside these ranges and needn't reach their ends.
Inputs may be any that keep to these rules, and one draw needn't show every extreme that they name: `obs_owner`: in the blocks of one device no owner is named more than 6 times; some owner is named exactly 6 times. `obs_cell`: Row-major index over the owner's 8 x 16 tile; the cell's row is below 7 and its column below 15.
All inputs are finite; a program needn't handle non-finite values.
Results may differ from the reference program's by a relative error of at most 0.0039.
Values may be sent and summed in bfloat16 or wider, within the bound.
No kernel may reach another device: no remote copies, remote signals or barrier semaphores. Data moves between devices by JAX's collectives and lax.ppermute only.
A program may use at most 64 MiB of HBM per device.

```python
import math
import jax
import jax.numpy as jnp
import numpy as np
from jax import lax

C = 256
LAT_DEV = 8
LON_DEV = 16
BLK_DEV = 128
ROWS = 32
CAP = 6
NLAT = 32
NLON = 128
BLOCKS = 4096
N_LON = 8
DEVICES = 32


def draw_obs_cell(key, part):
    key = jax.random.fold_in(key, 11)
    key_row, key_col = jax.random.split(key)
    row = jax.random.randint(key_row, (BLOCKS, ROWS), 0, LAT_DEV - 1)
    col = jax.random.randint(key_col, (BLOCKS, ROWS), 0, LON_DEV - 1)
    cell = row * LON_DEV + col
    cell = cell.at[0, 0].set((LAT_DEV - 2) * LON_DEV + LON_DEV - 2)
    return cell.at[0, 1].set(0).astype(jnp.int32)


def draw_obs_count(key, part):
    key = jax.random.fold_in(key, 23)
    count = jax.random.randint(key, (BLOCKS,), 1, ROWS + 1)
    count = count.at[0].set(ROWS)
    return count.at[1].set(1).astype(jnp.int32)


def plant(drawn, stream_key, least, top_value):
    longest = drawn.shape.index(max(drawn.shape))
    spots = []
    for shift in (0, 1):
        where = [jax.random.randint(jax.random.fold_in(stream_key, axis), (), 0, length) for axis, length in enumerate(drawn.shape)]
        where[longest] = (where[longest] + shift) % drawn.shape[longest]
        spots.append(tuple(where))
    return drawn.at[spots[0]].set(least).at[spots[1]].set(top_value)


def block_levels(rng, dims, pieces, smallest, largest):
    factor_of = 1.0
    for axis_at, blocks in pieces:
        heights = jax.random.uniform(jax.random.fold_in(jax.random.fold_in(rng, 6), axis_at), (blocks,), jnp.float32, smallest / len(pieces), largest / len(pieces))
        factor_of = factor_of * jnp.repeat(jnp.exp(heights), dims[axis_at] // blocks).reshape((-1,) + (1,) * (len(dims) - 1 - axis_at))
    return factor_of


def routed_block(key, own, number, rows, count, top, reach, slope):
    order = jax.random.permutation(key, count)
    packed, usual = shares(count, rows * top, reach, slope, True), shares(count, rows * top, reach, slope, False)
    places = jnp.arange(count)

    def named(tallies, offset_by):
        used = int((tallies > 0).sum())
        fixed = max(1, used // 4)
        moved = fixed + (places - fixed + offset_by * (used - fixed)) % max(1, count - fixed)
        return jnp.zeros((count,), jnp.int32).at[order[jnp.where(places < fixed, places, moved)]].set(jnp.asarray(tallies, jnp.int32))

    tallies = jnp.where(number % 4 == 0, named(packed, number // 4), named(usual, number - number // 4 - 1))
    mixed = jax.random.permutation(jax.random.fold_in(own, 3), count)
    giver, sink = mixed[0:count // 2 * 2:2], mixed[1:count // 2 * 2:2]
    slack = jnp.minimum(tallies[giver] - 1, reach - tallies[sink]) // 2
    slack = jnp.where((giver == order[0]) | (sink == order[0]) | (tallies[sink] == 0), 0, jnp.maximum(slack, 0))
    moved = jax.random.randint(jax.random.fold_in(own, 4), (count // 2,), 0, 1 << 20) % (slack + 1)
    tallies = tallies.at[giver].add(-moved).at[sink].add(moved)
    labels = jnp.searchsorted(jnp.cumsum(tallies), jnp.arange(rows * top), side="right").astype(jnp.int32)
    grid = labels.reshape(top, rows).T
    grid = grid[jax.random.permutation(jax.random.fold_in(own, 1), rows)]
    offset_by = jax.random.randint(jax.random.fold_in(own, 2), (rows, 1), 0, top)
    return jnp.take_along_axis(grid, (jnp.arange(top)[None, :] + offset_by) % top, axis=1)


def shares(amount, total, most, lean, full):
    portions = [(1 << 20) // math.isqrt(standing ** lean) + 1 for standing in range(1, amount + 1)]
    largest = most if full else min(most, max(-(-total // amount), total * portions[0] // sum(portions)))
    least = 1 if total - largest >= amount - 1 else 0
    holding, surplus = [largest] + [least] * (amount - 1), total - largest - least * (amount - 1)
    while surplus > 0:
        candidates = [i for i in range(1, amount) if holding[i] < largest] or [i for i in range(1, amount) if holding[i] < most]
        whole, budget = sum([portions[i] for i in candidates]), surplus
        for i in candidates:
            addition = min(most - holding[i], max(1, budget * portions[i] // whole), surplus)
            holding[i] = holding[i] + addition
            surplus = surplus - addition
    return np.array(holding)


def gaussian(rng, extent, scale, bound, shards=(), held_as=jnp.bfloat16):
    drawn = scale * jax.random.normal(rng, extent, jnp.float32)
    if shards:
        drawn = drawn * block_levels(rng, extent, shards, -0.22, 0.18)
    return jnp.clip(drawn, -bound, bound).astype(held_as)


def setup_inputs(seed: int = 0) -> dict:
    key_of = jax.random.split(jax.random.key(seed), 11)
    state = gaussian(key_of[0], (NLAT, NLON, C), 1.0, 6.0, ((0, 4), (1, 8)))
    weight_first = gaussian(key_of[1], (9, C, C), (9 * C) ** -0.5, 0.125)
    weight_second = gaussian(key_of[2], (9, C, C), (9 * C) ** -0.5, 0.125)
    obs_owner_keys = jax.random.split(jax.random.fold_in(key_of[3], 1), BLOCKS // BLK_DEV)
    obs_owner_turns = jax.random.permutation(jax.random.fold_in(key_of[3], 3), BLOCKS // BLK_DEV)
    obs_owner = jax.vmap(lambda own, number: routed_block(jax.random.fold_in(key_of[3], 2), own, number, BLK_DEV, DEVICES, 1, CAP, 2))(obs_owner_keys, obs_owner_turns).reshape((BLOCKS, 1))
    obs_cell = draw_obs_cell(jax.random.fold_in(key_of[10], 71), 0)
    obs_level = plant(jax.random.randint(key_of[5], (BLOCKS, ROWS), 0, C), jax.random.fold_in(key_of[5], 1), 0, C - 1).astype(jnp.int32)
    obs_count = draw_obs_count(jax.random.fold_in(key_of[10], 71), 0)
    obs_frac = jnp.clip(1.0 * jax.random.uniform(key_of[7], (BLOCKS, 2, ROWS), jnp.float32) ** block_levels(key_of[7], (BLOCKS, 2, ROWS), ((0, 32),), -0.2, 0.2), 0.0, 1.0)
    obs_value = gaussian(key_of[8], (BLOCKS, ROWS), 1.0, 6.0, ((0, 32),), jnp.float32)
    obs_weight = jnp.clip(jnp.exp(math.log(1.0) - 2.3025851 * jax.random.uniform(key_of[9], (BLOCKS, ROWS), jnp.float32) ** block_levels(key_of[9], (BLOCKS, ROWS), ((0, 32),), -0.2, 0.2)), 0.1, 1.0)
    return dict(state=state, weight_first=weight_first, weight_second=weight_second, obs_owner=obs_owner, obs_cell=obs_cell, obs_level=obs_level, obs_count=obs_count, obs_frac=obs_frac, obs_value=obs_value, obs_weight=obs_weight)


def widen_grid(field):
    padded = jnp.pad(field, ((1, 1), (0, 0), (0, 0)))
    return jnp.concatenate([padded[:, -1:], padded, padded[:, :1]], axis=1)


def conv_taps(padded, weight, rows, cols, flipped):
    total = jnp.zeros((rows * cols, weight.shape[2]), jnp.float32)
    for first_tap in range(3):
        for second_tap in range(3):
            if flipped:
                piece = padded[2 - first_tap:2 - first_tap + rows, 2 - second_tap:2 - second_tap + cols]
                matrix = weight[3 * first_tap + second_tap].T
            else:
                piece = padded[first_tap:first_tap + rows, second_tap:second_tap + cols]
                matrix = weight[3 * first_tap + second_tap]
            total = total + jnp.dot(piece.reshape(rows * cols, -1), matrix, preferred_element_type=jnp.float32)
    return total.reshape(rows, cols, -1)


def tap_grads(padded, pullback, rows, cols):
    flat_pull = pullback.reshape(rows * cols, -1)
    result = []
    for first_tap in range(3):
        for second_tap in range(3):
            piece = padded[first_tap:first_tap + rows, second_tap:second_tap + cols].reshape(rows * cols, -1)
            result.append(lax.dot_general(piece, flat_pull, (((0,), (0,)), ((), ())), preferred_element_type=jnp.float32))
    return jnp.stack(result)


def reference(state, weight_first, weight_second, obs_owner, obs_cell, obs_level, obs_count, obs_frac, obs_value, obs_weight):
    rows, cols = state.shape[0], state.shape[1]
    wide_state = widen_grid(state)
    first = conv_taps(wide_state, weight_first, rows, cols, False)
    hidden = jax.nn.silu(first).astype(jnp.bfloat16)
    wide_hidden = widen_grid(hidden)
    corrected = state.astype(jnp.float32) + conv_taps(wide_hidden, weight_second, rows, cols, False)

    owner = obs_owner[:, 0]
    lat_row = (owner // N_LON)[:, None] * LAT_DEV + obs_cell // LON_DEV
    lon_col = (owner % N_LON)[:, None] * LON_DEV + obs_cell % LON_DEV
    base = ((lat_row * NLON + lon_col) * C + obs_level).astype(jnp.int32)
    flat = corrected.reshape(-1)
    frac_lat = obs_frac[:, 0, :]
    frac_lon = obs_frac[:, 1, :]
    coeffs = [(1.0 - frac_lat) * (1.0 - frac_lon), (1.0 - frac_lat) * frac_lon, frac_lat * (1.0 - frac_lon), frac_lat * frac_lon]
    offsets = [0, C, NLON * C, NLON * C + C]
    predicted = jnp.zeros(obs_value.shape, jnp.float32)
    for coeff, offset in zip(coeffs, offsets):
        predicted = predicted + coeff * flat[base + offset]
    valid = (lax.broadcasted_iota(jnp.int32, obs_value.shape, 1) < obs_count[:, None]).astype(jnp.float32)
    misfit = valid * obs_weight * (predicted - obs_value)
    adjoint_flat = jnp.zeros(flat.shape, jnp.float32)
    for coeff, offset in zip(coeffs, offsets):
        adjoint_flat = adjoint_flat.at[base + offset].add(coeff * misfit)
    adjoint = adjoint_flat.reshape(corrected.shape)

    pullback = adjoint.astype(jnp.bfloat16)
    wide_pull = widen_grid(pullback)
    grad_second = tap_grads(wide_hidden, pullback, rows, cols)
    back = conv_taps(wide_pull, weight_second, rows, cols, True)
    sig = jax.nn.sigmoid(first)
    pull_first = (back * sig * (1.0 + first * (1.0 - sig))).astype(jnp.bfloat16)
    grad_first = tap_grads(wide_state, pull_first, rows, cols)
    state_grad = adjoint + conv_taps(widen_grid(pull_first), weight_first, rows, cols, True)
    return state_grad, grad_first, grad_second
```

```python
import functools

import jax
import jax.numpy as jnp
from jax import lax
from jax.experimental import pallas as pl
from jax.experimental.pallas import tpu as pltpu
from jax.sharding import PartitionSpec as P

F32 = jnp.float32
BF16 = jnp.bfloat16
FIELDS = 5
VMEM_LIMIT = 60 * 1024 * 1024


def params(limit=VMEM_LIMIT):
    return pltpu.CompilerParams(vmem_limit_bytes=limit)


def vmem():
    return pl.BlockSpec(memory_space=pltpu.VMEM)


def iota(shape, dim, dtype=jnp.int32):
    return lax.broadcasted_iota(jnp.int32, shape, dim).astype(dtype)


def dot(x, y, precision=None):
    return jnp.dot(x, y, precision=precision, preferred_element_type=F32)


def dot_nt(x, y, precision=None):
    return lax.dot_general(
        x, y, (((1,), (1,)), ((), ())), precision=precision, preferred_element_type=F32
    )


def slot_layout(slots):
    full, rest = divmod(slots, 4)
    rows = full * FIELDS + (0 if rest == 0 else -(-FIELDS // 2))
    return full, rest, -(-rows // 8) * 8


def route_kernel(
    devices, slots, chans, owner_ref, count_ref, cell_ref, level_ref, frac_ref, value_ref,
    weight_ref, out_ref
):
    width, blocks = value_ref.shape
    owner = owner_ref[...].astype(F32)
    across = jnp.broadcast_to(owner, (blocks, blocks))
    down = across.T
    earlier = iota((blocks, blocks), 0) < iota((blocks, blocks), 1)
    hits = jnp.where(jnp.logical_and(across == down, earlier), 1.0, 0.0)
    rank = jnp.sum(hits, axis=0, keepdims=True)
    target = rank * float(devices) + owner
    places = iota((slots * devices, blocks), 0, F32) == target
    onehot = jnp.where(places, 1.0, 0.0)
    valid = iota((width, blocks), 0) < count_ref[...]
    fields = jnp.concatenate(
        [
            frac_ref[0],
            frac_ref[1],
            value_ref[...],
            jnp.where(valid, weight_ref[...], 0.0),
            (cell_ref[...] * chans + level_ref[...]).astype(F32),
        ],
        axis=0,
    )
    placed = dot_nt(onehot, fields, lax.Precision.HIGHEST)
    full, rest, rows = slot_layout(slots)
    out_ref[...] = jnp.zeros(out_ref.shape, F32)
    for slot in range(slots):
        for field in range(FIELDS):
            piece = placed[
                slot * devices : (slot + 1) * devices, field * width : (field + 1) * width
            ]
            if slot < 4 * full:
                row, lane = (slot // 4) * FIELDS + field, (slot % 4) * width
            else:
                row = full * FIELDS + field // 2
                lane = (field % 2) * 2 * width + (slot - 4 * full) * width
            out_ref[:, row, lane : lane + width] = piece


def route(devices, slots, chans, obs_owner, obs_cell, obs_level, obs_count, obs_frac, obs_value,
          obs_weight):
    blocks = obs_value.shape[0]
    rows = slot_layout(slots)[2]
    return pl.pallas_call(
        functools.partial(route_kernel, devices, slots, chans),
        out_shape=jax.ShapeDtypeStruct((devices, rows, 128), F32),
        in_specs=[vmem()] * 7,
        out_specs=vmem(),
        compiler_params=params(),
        name="route",
    )(
        obs_owner.reshape(1, blocks),
        obs_count.reshape(1, blocks),
        obs_cell.T,
        obs_level.T,
        jnp.transpose(obs_frac, (1, 2, 0)),
        obs_value.T,
        obs_weight.T,
    )


def silu_parts(first):
    sig = 1.0 / (1.0 + jnp.exp(-first))
    return sig, first * sig


def forward_kernel(slots, tiles, group, wide_ref, w1_ref, w2_ref, got_ref, adj_ref, pull_ref,
                   line_ref, shift_ref, hid_ref, obs_ref):
    rows, cols, chans = (wide_ref.shape[0] - 4, wide_ref.shape[1] - 4, wide_ref.shape[2])
    span = 32
    line_ref[:, 0 : cols + 4, :] = wide_ref[...].astype(F32)
    line_ref[:, cols + 4 :, :] = jnp.zeros(
        (rows + 4, line_ref.shape[1] - cols - 4, chans), F32
    )
    first = jnp.zeros(((rows + 2) * span, chans), F32)
    for b in range(3):
        shift_ref[...] = (
            line_ref[:, b : b + span, :].astype(BF16).reshape((rows + 4) * span, chans)
        )
        for a in range(3):
            first = first + dot(
                shift_ref[a * span : a * span + (rows + 2) * span, :], w1_ref[3 * a + b]
            )
    hidden = silu_parts(first)[1].astype(BF16).astype(F32).reshape(rows + 2, span, chans)
    lat = lax.axis_index("lat") * rows + iota((rows + 2, span, chans), 0) - 1
    hidden = jnp.where(jnp.logical_and(lat >= 0, lat < tiles * rows), hidden, 0.0)
    hid_ref[...] = hidden
    total = line_ref[2 : 2 + rows, 2 : 2 + cols, :].reshape(rows * cols, chans)
    for b in range(3):
        shift_ref[0 : (rows + 2) * cols, :] = (
            hid_ref[:, b : b + cols, :].astype(BF16).reshape((rows + 2) * cols, chans)
        )
        for a in range(3):
            total = total + dot(
                shift_ref[a * cols : a * cols + rows * cols, :], w2_ref[3 * a + b]
            )
    cells = rows * cols
    turned = total.T
    grid_high = turned.astype(BF16)
    grid_low = (turned - grid_high.astype(F32)).astype(BF16)
    grid_both = jnp.concatenate([grid_high, grid_low], axis=1)

    devices = got_ref.shape[0]
    full, rest, _ = slot_layout(slots)
    half = devices // 2
    for field in range(FIELDS):
        for part in range(full):
            obs_ref[field, part * devices : (part + 1) * devices, :] = got_ref[
                :, part * FIELDS + field, :
            ]
        if rest:
            tail = got_ref[:, full * FIELDS + field // 2, :]
            low, high = tail[:half], tail[half:]
            if field % 2 == 0:
                high = pltpu.roll(high, 64, 1)
            else:
                low = pltpu.roll(low, 64, 1)
            obs_ref[field, full * devices : full * devices + half, :] = jnp.where(
                iota((half, 128), 1) < 64, low, high
            )
    code = obs_ref[4].astype(jnp.int32)
    shift = chans.bit_length() - 1
    cell = lax.shift_right_logical(code, shift)
    obs_ref[4] = (code & (chans - 1)).astype(F32)
    obs_ref[0] = obs_ref[0] + lax.shift_right_logical(cell, 4).astype(F32)
    obs_ref[1] = obs_ref[1] + (cell & (cols - 1)).astype(F32)

    adj_ref[...] = jnp.zeros(adj_ref.shape, F32)
    count = obs_ref.shape[1] // group
    row_ids = iota((rows, 128), 0, F32)
    col_ids = iota((cols, 128), 0, F32)
    level_ids = iota((chans, 128), 0, F32)

    def step(index, carry):
        high, low, masks, marks = [], [], [], []
        for piece in range(group):
            at = index * group + piece
            mark = [obs_ref[field, pl.ds(at, 1), :] for field in range(FIELDS)]
            up = jnp.maximum(0.0, 1.0 - jnp.abs(row_ids - mark[0]))
            along = jnp.maximum(0.0, 1.0 - jnp.abs(col_ids - mark[1]))
            weights = (up[:, None, :] * along[None, :, :]).reshape(cells, 128)
            weights_high = weights.astype(BF16)
            high.append(weights_high)
            low.append((weights - weights_high.astype(F32)).astype(BF16))
            masks.append(level_ids == mark[4])
            marks.append(mark)
        high = jnp.concatenate(high, axis=1)
        low = jnp.concatenate(low, axis=1)
        sampled = dot(grid_both, jnp.concatenate([high, high], axis=0)) + dot(grid_high, low)
        hot_high, hot_low = [], []
        for piece in range(group):
            mine = sampled[:, piece * 128 : (piece + 1) * 128]
            predicted = jnp.sum(jnp.where(masks[piece], mine, 0.0), axis=0, keepdims=True)
            misfit = marks[piece][3] * (predicted - marks[piece][2])
            misfit_high = misfit.astype(BF16).astype(F32)
            hot_high.append(jnp.where(masks[piece], misfit_high, 0.0).astype(BF16))
            hot_low.append(jnp.where(masks[piece], misfit - misfit_high, 0.0).astype(BF16))
        hot_high = jnp.concatenate(hot_high, axis=1)
        hot_low = jnp.concatenate(hot_low, axis=1)
        adj_ref[...] += dot_nt(
            jnp.concatenate([high, high, low], axis=1),
            jnp.concatenate([hot_high, hot_low, hot_high], axis=1),
        )
        return carry

    lax.fori_loop(0, count, step, 0)
    pull_ref[...] = adj_ref[...].astype(BF16)


def forward(slots, tiles, wide, w1, w2, got):
    rows, cols, chans = (wide.shape[0] - 4, wide.shape[1] - 4, wide.shape[2])
    devices = got.shape[0]
    full, rest, _ = slot_layout(slots)
    groups = full * devices + (devices // 2 if rest else 0)
    group = 4
    return pl.pallas_call(
        functools.partial(forward_kernel, slots, tiles, group),
        out_shape=[
            jax.ShapeDtypeStruct((rows * cols, chans), F32),
            jax.ShapeDtypeStruct((rows * cols, chans), BF16),
        ],
        in_specs=[vmem()] * 4,
        out_specs=[vmem()] * 2,
        scratch_shapes=[
            pltpu.VMEM((rows + 4, 40, chans), F32),
            pltpu.VMEM(((rows + 4) * 32, chans), BF16),
            pltpu.VMEM((rows + 2, 32, chans), F32),
            pltpu.VMEM((FIELDS, groups, 128), F32),
        ],
        compiler_params=params(),
        name="forward",
    )(wide, w1, w2, got)


def spread_matrix(steps):
    lons = 16 * steps
    place = iota(((steps + 2) * 16, lons), 0)
    lon = (place & 15) * steps + lax.shift_right_logical(place, 4) - 1
    lon = jnp.where(lon < 0, lon + lons, jnp.where(lon >= lons, lon - lons, lon))
    return jnp.where(iota(((steps + 2) * 16, lons), 1) == lon, 1.0, 0.0).astype(BF16)


def spread(all_ref, pad_ref):
    bands, tiles, rows, group, chans = all_ref.shape
    steps = pad_ref.shape[1] - 2
    matrix = spread_matrix(steps)
    blank = jnp.zeros(pad_ref.shape[1:], BF16)
    pad_ref[0] = blank
    pad_ref[bands * rows + 1] = blank

    def place(band, carry):
        for row in range(rows):
            line = all_ref[band, :, row].reshape(tiles * group, chans)
            pad_ref[1 + band * rows + row] = (
                dot(matrix, line).astype(BF16).reshape(steps + 2, 16, chans)
            )
        return carry

    lax.fori_loop(0, bands, place, 0)


def conv_block(pad_ref, weight_ref, start, rows, flipped):
    steps = pad_ref.shape[1] - 2
    chans = pad_ref.shape[3]
    total = None
    for a in range(3):
        for b in range(3):
            da, db = (2 - a, 2 - b) if flipped else (a, b)
            piece = pad_ref[pl.ds(start + da, rows), db : db + steps]
            term = dot(piece.reshape(rows * steps * 16, chans), weight_ref[3 * a + b])
            total = term if total is None else total + term
    return total


def whole_kernel(block, all_ref, w1_ref, w2_ref, slope_ref, hidden_ref, state_ref, w2t_ref, pad_ref):
    lats = pad_ref.shape[0] - 2
    steps = pad_ref.shape[1] - 2
    chans = pad_ref.shape[3]
    size = block * steps * 16
    spread(all_ref, pad_ref)

    def step(index, carry):
        start = index * block
        first = conv_block(pad_ref, w1_ref, start, block, False)
        sig, hidden = silu_parts(first)
        at = pl.ds(pl.multiple_of(index * size, size), size)
        slope_ref[at, :] = sig * (1.0 + first * (1.0 - sig))
        hidden_ref[:, at] = hidden.astype(BF16).T
        centre = pad_ref[pl.ds(start + 1, block), 1 : 1 + steps].reshape(size, chans)
        state_ref[:, at] = centre.T
        return carry

    lax.fori_loop(0, lats // block, step, 0)
    for tap in range(9):
        w2t_ref[tap] = w2_ref[tap].T


def whole(state_all, w1, w2):
    bands, tiles, rows, group, chans = state_all.shape
    lats, lons = bands * rows, tiles * group
    steps = lons // 16
    block = 512 // lons
    return pl.pallas_call(
        functools.partial(whole_kernel, block),
        out_shape=[
            jax.ShapeDtypeStruct((lats * lons, chans), F32),
            jax.ShapeDtypeStruct((chans, lats * lons), BF16),
            jax.ShapeDtypeStruct((chans, lats * lons), BF16),
            jax.ShapeDtypeStruct((9, chans, chans), BF16),
        ],
        in_specs=[vmem()] * 3,
        out_specs=[vmem()] * 4,
        scratch_shapes=[pltpu.VMEM((lats + 2, steps + 2, 16, chans), BF16)],
        compiler_params=params(),
        name="whole",
    )(state_all, w1, w2)


def tap_sums(turned_ref, pad_ref, out_ref):
    lats = pad_ref.shape[0] - 2
    steps = pad_ref.shape[1] - 2
    chans = pad_ref.shape[3]
    per_row = steps * 16
    part = 4096 // per_row

    def step(tap, carry):
        a, b = tap // 3, tap % 3
        total = None
        for start in range(0, lats, part):
            piece = pad_ref[pl.ds(start + 2 - a, part), pl.ds(2 - b, steps)]
            term = dot(
                turned_ref[:, start * per_row : (start + part) * per_row],
                piece.reshape(part * per_row, chans),
            )
            total = term if total is None else total + term
        out_ref[tap] = total
        return carry

    lax.fori_loop(0, 9, step, 0)


def tail_kernel(block, all_ref, slope_hbm, hidden_hbm, state_hbm, w2t_ref, w1_ref, adj_ref,
                grad_ref, g1_ref, g2_ref, pull_ref, first_ref, near_ref, slope_ref, hidden_ref,
                state_ref, slope_sems, big_sems):
    lats = pull_ref.shape[0] - 2
    steps = pull_ref.shape[1] - 2
    chans = pull_ref.shape[3]
    lons = steps * 16
    size = block * lons
    count = lats // block
    rows = all_ref.shape[2]
    cols = all_ref.shape[3]
    hidden_copy = pltpu.make_async_copy(hidden_hbm, hidden_ref, big_sems.at[0])
    state_copy = pltpu.make_async_copy(state_hbm, state_ref, big_sems.at[1])

    def slope_copy(index, slot):
        at = pl.ds(pl.multiple_of(index * size, size), size)
        return pltpu.make_async_copy(slope_hbm.at[at, :], slope_ref.at[slot], slope_sems.at[slot])

    slope_copy(0, 0).start()
    hidden_copy.start()
    state_copy.start()
    spread(all_ref, pull_ref)
    blank = jnp.zeros(first_ref.shape[1:], BF16)
    first_ref[0] = blank
    first_ref[lats + 1] = blank

    def step(index, carry):
        start = index * block
        slot = index & 1

        @pl.when(index + 1 < count)
        def _():
            slope_copy(index + 1, 1 - slot).start()

        back = conv_block(pull_ref, w2t_ref, start, block, True)
        slope_copy(index, slot).wait()
        pull = (back * slope_ref[slot]).astype(BF16).astype(F32)
        pull = pull.reshape(block, steps, 16, chans)
        last, head = pull[:, steps - 1], pull[:, 0]
        before = jnp.concatenate([last[:, 15:], last[:, :15]], axis=1)
        after = jnp.concatenate([head[:, 1:], head[:, :1]], axis=1)
        to = pl.ds(1 + start, block)
        first_ref[to, 1 : 1 + steps] = pull.astype(BF16)
        first_ref[to, 0] = before.astype(BF16)
        first_ref[to, steps + 1] = after.astype(BF16)
        return carry

    lax.fori_loop(0, count, step, 0)
    hidden_copy.wait()
    tap_sums(hidden_ref, pull_ref, g2_ref)
    state_copy.wait()
    tap_sums(state_ref, first_ref, g1_ref)

    top = lax.axis_index("lat") * rows
    left = lax.axis_index("lon") * cols
    place = iota((3 * cols, lons), 0)
    shift = 1 - lax.shift_right_logical(place, cols.bit_length() - 1)
    lon = left + (place & (cols - 1)) + shift
    lon = jnp.where(lon < 0, lon + lons, jnp.where(lon >= lons, lon - lons, lon))
    column = iota((3 * cols, lons), 1)
    theirs = (column & 15) * steps + lax.shift_right_logical(column, 4)
    select = jnp.where(theirs == lon, 1.0, 0.0).astype(BF16)
    for row in range(rows + 2):
        line = first_ref[top + row, 1 : 1 + steps].reshape(lons, chans)
        near = dot(select, line).astype(BF16)
        for b in range(3):
            near_ref[b, row * cols : (row + 1) * cols, :] = near[b * cols : (b + 1) * cols]
    total = adj_ref[...]
    for a in range(3):
        for b in range(3):
            total = total + dot_nt(
                near_ref[b, (2 - a) * cols : (2 - a + rows) * cols, :], w1_ref[3 * a + b]
            )
    grad_ref[...] = total


def tail(pull_all, slope, hidden, state, w2t, w1, adjoint):
    bands, tiles, rows, group, chans = pull_all.shape
    lats, lons = bands * rows, tiles * group
    steps = lons // 16
    block = 512 // lons
    padded = pltpu.VMEM((lats + 2, steps + 2, 16, chans), BF16)
    return pl.pallas_call(
        functools.partial(tail_kernel, block),
        out_shape=[
            jax.ShapeDtypeStruct((rows * group, chans), F32),
            jax.ShapeDtypeStruct((9, chans, chans), F32),
            jax.ShapeDtypeStruct((9, chans, chans), F32),
        ],
        in_specs=[vmem()] + [pl.BlockSpec(memory_space=pl.ANY)] * 3 + [vmem()] * 3,
        out_specs=[vmem()] * 3,
        scratch_shapes=[
            padded,
            padded,
            pltpu.VMEM((3, (rows + 2) * group, chans), BF16),
            pltpu.VMEM((2, block * lons, chans), F32),
            pltpu.VMEM((chans, lats * lons), BF16),
            pltpu.VMEM((chans, lats * lons), BF16),
            pltpu.SemaphoreType.DMA((2,)),
            pltpu.SemaphoreType.DMA((2,)),
        ],
        compiler_params=params(),
        name="tail",
    )(pull_all, slope, hidden, state, w2t, w1, adjoint)


def with_halo(x, axis, dim, width, wrap):
    count, length = (lax.axis_size(axis), x.shape[dim])
    up = [(i, (i + 1) % count) for i in range(count if wrap else count - 1)]
    down = [(j, i) for i, j in up]
    last = lax.slice_in_dim(x, length - width, length, axis=dim)
    first = lax.slice_in_dim(x, 0, width, axis=dim)
    before = lax.ppermute(last, axis, up)
    after = lax.ppermute(first, axis, down)
    return jnp.concatenate([before, x, after], axis=dim)


def gather_tiles(x):
    bands, tiles = lax.axis_size("lat"), lax.axis_size("lon")
    everything = lax.all_gather(x, ("lat", "lon"), axis=0, tiled=False)
    return everything.reshape((bands, tiles) + x.shape)


def per_device(
    state, weight_first, weight_second, obs_owner, obs_cell, obs_level, obs_count, obs_frac,
    obs_value, obs_weight,
):
    rows, cols, chans = state.shape
    bands = lax.axis_size("lat")
    devices = lax.axis_size(("lat", "lon"))
    slots = max(2, 3 * obs_value.shape[0] // (2 * devices))
    outgoing = route(
        devices, slots, chans, obs_owner, obs_cell, obs_level, obs_count, obs_frac, obs_value,
        obs_weight,
    )
    got = lax.all_to_all(outgoing, ("lat", "lon"), split_axis=0, concat_axis=0, tiled=True)
    wide = with_halo(with_halo(state, "lon", 1, 2, True), "lat", 0, 2, False)
    state_all = gather_tiles(state)
    adjoint, pullback = forward(slots, bands, wide, weight_first, weight_second, got)
    pull_all = gather_tiles(pullback.reshape(rows, cols, chans))
    slope, hidden, turned, w2t = whole(state_all, weight_first, weight_second)
    grad, g1, g2 = tail(pull_all, slope, hidden, turned, w2t, weight_first, adjoint)
    return grad.reshape(rows, cols, chans), g1, g2


def solution(mesh):
    both = P(("lat", "lon"), None)
    placed = (
        P("lat", "lon", None),
        P(),
        P(),
        both,
        both,
        both,
        P(("lat", "lon")),
        P(("lat", "lon"), None, None),
        both,
        both,
    )
    return jax.shard_map(
        per_device,
        mesh=mesh,
        in_specs=placed,
        out_specs=(P("lat", "lon", None), P(), P()),
        check_vma=False,
    )
```

```python
import functools

import jax
import jax.numpy as jnp
from jax import lax
from jax.experimental import pallas as pl
from jax.experimental.pallas import tpu as pltpu
from jax.sharding import PartitionSpec as P

F32 = jnp.float32
BF16 = jnp.bfloat16
FIELDS = 5
VMEM_LIMIT = 60 * 1024 * 1024


def params(limit=VMEM_LIMIT):
    return pltpu.CompilerParams(vmem_limit_bytes=limit)


def vmem():
    return pl.BlockSpec(memory_space=pltpu.VMEM)


def iota(shape, dim, dtype=jnp.int32):
    return lax.broadcasted_iota(jnp.int32, shape, dim).astype(dtype)


def dot(x, y, precision=None):
    return jnp.dot(x, y, precision=precision, preferred_element_type=F32)


def dot_nt(x, y, precision=None):
    return lax.dot_general(
        x, y, (((1,), (1,)), ((), ())), precision=precision, preferred_element_type=F32
    )


def slot_layout(slots):
    full, rest = divmod(slots, 4)
    rows = full * FIELDS + (0 if rest == 0 else -(-FIELDS // 2))
    return full, rest, -(-rows // 8) * 8


def route_kernel(
    devices, slots, chans, owner_ref, count_ref, cell_ref, level_ref, frac_ref, value_ref,
    weight_ref, out_ref
):
    width, blocks = value_ref.shape
    owner = owner_ref[...].astype(F32)
    across = jnp.broadcast_to(owner, (blocks, blocks))
    down = across.T
    earlier = iota((blocks, blocks), 0) < iota((blocks, blocks), 1)
    hits = jnp.where(jnp.logical_and(across == down, earlier), 1.0, 0.0)
    rank = jnp.sum(hits, axis=0, keepdims=True)
    target = rank * float(devices) + owner
    places = iota((slots * devices, blocks), 0, F32) == target
    onehot = jnp.where(places, 1.0, 0.0)
    valid = iota((width, blocks), 0) < count_ref[...]
    fields = jnp.concatenate(
        [
            frac_ref[0],
            frac_ref[1],
            value_ref[...],
            jnp.where(valid, weight_ref[...], 0.0),
            (cell_ref[...] * chans + level_ref[...]).astype(F32),
        ],
        axis=0,
    )
    placed = dot_nt(onehot, fields, lax.Precision.HIGHEST)
    full, rest, rows = slot_layout(slots)
    out_ref[...] = jnp.zeros(out_ref.shape, F32)
    for slot in range(slots):
        for field in range(FIELDS):
            piece = placed[
                slot * devices : (slot + 1) * devices, field * width : (field + 1) * width
            ]
            if slot < 4 * full:
                row, lane = (slot // 4) * FIELDS + field, (slot % 4) * width
            else:
                row = full * FIELDS + field // 2
                lane = (field % 2) * 2 * width + (slot - 4 * full) * width
            out_ref[:, row, lane : lane + width] = piece


def route(devices, slots, chans, obs_owner, obs_cell, obs_level, obs_count, obs_frac, obs_value,
          obs_weight):
    blocks = obs_value.shape[0]
    rows = slot_layout(slots)[2]
    return pl.pallas_call(
        functools.partial(route_kernel, devices, slots, chans),
        out_shape=jax.ShapeDtypeStruct((devices, rows, 128), F32),
        in_specs=[vmem()] * 7,
        out_specs=vmem(),
        compiler_params=params(),
        name="route",
    )(
        obs_owner.reshape(1, blocks),
        obs_count.reshape(1, blocks),
        obs_cell.T,
        obs_level.T,
        jnp.transpose(obs_frac, (1, 2, 0)),
        obs_value.T,
        obs_weight.T,
    )


def silu_parts(first):
    sig = 1.0 / (1.0 + jnp.exp(-first))
    return sig, first * sig


def forward_kernel(slots, tiles, group, wide_ref, w1_ref, w2_ref, got_ref, adj_ref, pull_ref,
                   line_ref, shift_ref, hid_ref, obs_ref, sum_ref):
    rows, cols, chans = (wide_ref.shape[0] - 4, wide_ref.shape[1] - 4, wide_ref.shape[2])
    span = 32
    line_ref[:, 0 : cols + 4, :] = wide_ref[...].astype(F32)
    line_ref[:, cols + 4 :, :] = jnp.zeros(
        (rows + 4, line_ref.shape[1] - cols - 4, chans), F32
    )
    first = jnp.zeros(((rows + 2) * span, chans), F32)
    for b in range(3):
        shift_ref[...] = (
            line_ref[:, b : b + span, :].astype(BF16).reshape((rows + 4) * span, chans)
        )
        for a in range(3):
            first = first + dot(
                shift_ref[a * span : a * span + (rows + 2) * span, :], w1_ref[3 * a + b]
            )
    hidden = silu_parts(first)[1].astype(BF16).astype(F32).reshape(rows + 2, span, chans)
    lat = lax.axis_index("lat") * rows + iota((rows + 2, span, chans), 0) - 1
    hidden = jnp.where(jnp.logical_and(lat >= 0, lat < tiles * rows), hidden, 0.0)
    hid_ref[...] = hidden
    total = line_ref[2 : 2 + rows, 2 : 2 + cols, :].reshape(rows * cols, chans)
    for b in range(3):
        shift_ref[0 : (rows + 2) * cols, :] = (
            hid_ref[:, b : b + cols, :].astype(BF16).reshape((rows + 2) * cols, chans)
        )
        for a in range(3):
            total = total + dot(
                shift_ref[a * cols : a * cols + rows * cols, :], w2_ref[3 * a + b]
            )
    cells = rows * cols
    turned = total.T
    grid_high = turned.astype(BF16)
    grid_low = (turned - grid_high.astype(F32)).astype(BF16)
    grid_both = jnp.concatenate([grid_high, grid_low], axis=1)

    devices = got_ref.shape[0]
    full, rest, _ = slot_layout(slots)
    half = devices // 2
    for field in range(FIELDS):
        for part in range(full):
            obs_ref[field, part * devices : (part + 1) * devices, :] = got_ref[
                :, part * FIELDS + field, :
            ]
        if rest:
            tail = got_ref[:, full * FIELDS + field // 2, :]
            low, high = tail[:half], tail[half:]
            if field % 2 == 0:
                high = pltpu.roll(high, 64, 1)
            else:
                low = pltpu.roll(low, 64, 1)
            obs_ref[field, full * devices : full * devices + half, :] = jnp.where(
                iota((half, 128), 1) < 64, low, high
            )
    code = obs_ref[4].astype(jnp.int32)
    shift = chans.bit_length() - 1
    cell = lax.shift_right_logical(code, shift)
    obs_ref[4] = (code & (chans - 1)).astype(F32)
    obs_ref[0] = obs_ref[0] + lax.shift_right_logical(cell, 4).astype(F32)
    obs_ref[1] = obs_ref[1] + (cell & (cols - 1)).astype(F32)

    sum_ref[...] = jnp.zeros(sum_ref.shape, F32)
    count = obs_ref.shape[1] // group
    row_ids = iota((rows, 128), 0, F32)
    col_ids = iota((cols, 128), 0, F32)
    level_ids = iota((chans, 128), 0, F32)

    def step(index, carry):
        high, low, masks, marks = [], [], [], []
        for piece in range(group):
            at = index * group + piece
            mark = [obs_ref[field, pl.ds(at, 1), :] for field in range(FIELDS)]
            up = jnp.maximum(0.0, 1.0 - jnp.abs(row_ids - mark[0]))
            along = jnp.maximum(0.0, 1.0 - jnp.abs(col_ids - mark[1]))
            weights = (up[:, None, :] * along[None, :, :]).reshape(cells, 128)
            weights_high = weights.astype(BF16)
            high.append(weights_high)
            low.append((weights - weights_high.astype(F32)).astype(BF16))
            masks.append(level_ids == mark[4])
            marks.append(mark)
        high = jnp.concatenate(high, axis=1)
        low = jnp.concatenate(low, axis=1)
        sampled = dot(grid_both, jnp.concatenate([high, high], axis=0)) + dot(grid_high, low)
        hot_high, hot_low = [], []
        for piece in range(group):
            mine = sampled[:, piece * 128 : (piece + 1) * 128]
            predicted = jnp.sum(jnp.where(masks[piece], mine, 0.0), axis=0, keepdims=True)
            misfit = marks[piece][3] * (predicted - marks[piece][2])
            misfit_high = misfit.astype(BF16).astype(F32)
            hot_high.append(jnp.where(masks[piece], misfit_high, 0.0).astype(BF16))
            hot_low.append(jnp.where(masks[piece], misfit - misfit_high, 0.0).astype(BF16))
        hot_high = jnp.concatenate(hot_high, axis=1)
        hot_low = jnp.concatenate(hot_low, axis=1)
        mixed = dot_nt(jnp.concatenate([hot_high, hot_low], axis=0), high)
        sum_ref[...] += mixed[:chans] + (mixed[chans:] + dot_nt(hot_high, low))
        return carry

    lax.fori_loop(0, count, step, 0)
    adjoint = sum_ref[...].T
    adj_ref[...] = adjoint
    pull_ref[...] = adjoint.astype(BF16)


def forward(slots, tiles, wide, w1, w2, got):
    rows, cols, chans = (wide.shape[0] - 4, wide.shape[1] - 4, wide.shape[2])
    devices = got.shape[0]
    full, rest, _ = slot_layout(slots)
    groups = full * devices + (devices // 2 if rest else 0)
    group = 4
    return pl.pallas_call(
        functools.partial(forward_kernel, slots, tiles, group),
        out_shape=[
            jax.ShapeDtypeStruct((rows * cols, chans), F32),
            jax.ShapeDtypeStruct((rows * cols, chans), BF16),
        ],
        in_specs=[vmem()] * 4,
        out_specs=[vmem()] * 2,
        scratch_shapes=[
            pltpu.VMEM((rows + 4, 40, chans), F32),
            pltpu.VMEM(((rows + 4) * 32, chans), BF16),
            pltpu.VMEM((rows + 2, 32, chans), F32),
            pltpu.VMEM((FIELDS, groups, 128), F32),
            pltpu.VMEM((chans, rows * cols), F32),
        ],
        compiler_params=params(),
        name="forward",
    )(wide, w1, w2, got)


def spread_matrix(steps, tiles, split):
    lons = 16 * steps
    place = iota(((steps + 2) * 16, lons), 0)
    lon = (place & 15) * steps + lax.shift_right_logical(place, 4) - 1
    lon = jnp.where(lon < 0, lon + lons, jnp.where(lon >= lons, lon - lons, lon))
    column = iota(((steps + 2) * 16, lons), 1)
    if split:
        half = tiles // 2
        chunk = lax.shift_right_logical(column, 4)
        core = lax.shift_right_logical(chunk, half.bit_length() - 1)
        column = (2 * (chunk & (half - 1)) + core) * 16 + (column & 15)
    return jnp.where(column == lon, 1.0, 0.0).astype(BF16)


def spread(line_of, bands, rows, matrix, pad_ref):
    steps = pad_ref.shape[1] - 2
    blank = jnp.zeros(pad_ref.shape[1:], BF16)
    pad_ref[0] = blank
    pad_ref[bands * rows + 1] = blank

    def place(band, carry):
        for row in range(rows):
            line = line_of(band, row)
            pad_ref[1 + band * rows + row] = (
                dot(matrix, line).astype(BF16).reshape(steps + 2, 16, line.shape[1])
            )
        return carry

    lax.fori_loop(0, bands, place, 0)


def conv_block(pad_ref, weight_ref, start, rows, flipped):
    steps = pad_ref.shape[1] - 2
    chans = pad_ref.shape[3]
    pieces = []
    for a in range(3):
        for b in range(3):
            da, db = (2 - a, 2 - b) if flipped else (a, b)
            piece = pad_ref[pl.ds(start + da, rows), db : db + steps]
            pieces.append(piece.reshape(rows * steps * 16, chans))
    return dot(jnp.concatenate(pieces, axis=1), weight_ref[...].reshape(9 * chans, chans))


def whole_kernel(block, all_ref, w1_ref, w2_ref, slope_ref, hidden_ref, state_ref, w2t_ref, pad_ref):
    lats = pad_ref.shape[0] - 2
    steps = pad_ref.shape[1] - 2
    chans = pad_ref.shape[3]
    size = block * steps * 16
    bands, tiles, rows, group, _ = all_ref.shape
    spread(
        lambda band, row: all_ref[band, :, row].reshape(tiles * group, chans),
        bands, rows, spread_matrix(steps, tiles, False), pad_ref,
    )

    def step(index, carry):
        start = index * block
        first = conv_block(pad_ref, w1_ref, start, block, False)
        sig, hidden = silu_parts(first)
        at = pl.ds(pl.multiple_of(index * size, size), size)
        slope_ref[at, :] = sig * (1.0 + first * (1.0 - sig))
        hidden_ref[:, at] = hidden.astype(BF16).T
        centre = pad_ref[pl.ds(start + 1, block), 1 : 1 + steps].reshape(size, chans)
        state_ref[:, at] = centre.T
        return carry

    lax.fori_loop(0, lats // block, step, 0)
    for tap in range(9):
        w2t_ref[tap] = w2_ref[tap].T


def whole(state_all, w1, w2):
    bands, tiles, rows, group, chans = state_all.shape
    lats, lons = bands * rows, tiles * group
    steps = lons // 16
    block = 512 // lons
    return pl.pallas_call(
        functools.partial(whole_kernel, block),
        out_shape=[
            jax.ShapeDtypeStruct((lats * lons, chans), F32),
            jax.ShapeDtypeStruct((chans, lats * lons), BF16),
            jax.ShapeDtypeStruct((chans, lats * lons), BF16),
            jax.ShapeDtypeStruct((9, chans, chans), BF16),
        ],
        in_specs=[vmem()] * 3,
        out_specs=[vmem()] * 4,
        scratch_shapes=[pltpu.VMEM((lats + 2, steps + 2, 16, chans), BF16)],
        compiler_params=params(),
        name="whole",
    )(state_all, w1, w2)


def tap_sums(turned_ref, pad_ref, sum_ref, out_ref, sem):
    lats = pad_ref.shape[0] - 2
    steps = pad_ref.shape[1] - 2
    chans = pad_ref.shape[3]
    per_row = steps * 16
    part = 4096 // per_row

    def step(tap, carry):
        a, b = tap // 3, tap % 3
        total = None
        for start in range(0, lats, part):
            piece = pad_ref[pl.ds(start + 2 - a, part), pl.ds(2 - b, steps)]
            term = dot(
                turned_ref[:, start * per_row : (start + part) * per_row],
                piece.reshape(part * per_row, chans),
            )
            total = term if total is None else total + term
        sum_ref[tap] = total
        pltpu.make_async_copy(sum_ref.at[tap], out_ref.at[tap], sem.at[tap]).start()
        return carry

    lax.fori_loop(0, 9, step, 0)


def tail_kernel(block, mine_hbm, other_hbm, slope_hbm, hidden_hbm, state_hbm, w2t_ref, w1_ref,
                adj_ref, grad_ref, g1_hbm, g2_hbm, all_ref, pull_ref, first_ref, near_ref,
                slope_ref, hidden_ref, state_ref, g1_ref, g2_ref, slope_sems, big_sems,
                g1_sems, g2_sems):
    lats = pull_ref.shape[0] - 2
    steps = pull_ref.shape[1] - 2
    chans = pull_ref.shape[3]
    lons = steps * 16
    size = block * lons
    count = lats // block
    _, bands, half, rows, cols, _ = all_ref.shape
    core = lax.axis_index("lon") & 1
    mine_copy = pltpu.make_async_copy(mine_hbm, all_ref.at[core], big_sems.at[2])
    other_copy = pltpu.make_async_copy(other_hbm, all_ref.at[1 - core], big_sems.at[3])
    hidden_copy = pltpu.make_async_copy(hidden_hbm, hidden_ref, big_sems.at[0])
    state_copy = pltpu.make_async_copy(state_hbm, state_ref, big_sems.at[1])

    def slope_copy(index, slot):
        at = pl.ds(pl.multiple_of(index * size, size), size)
        return pltpu.make_async_copy(slope_hbm.at[at, :], slope_ref.at[slot], slope_sems.at[slot])

    mine_copy.start()
    other_copy.start()
    slope_copy(0, 0).start()
    hidden_copy.start()
    state_copy.start()
    blank = jnp.zeros(first_ref.shape[1:], BF16)
    first_ref[0] = blank
    first_ref[lats + 1] = blank
    matrix = spread_matrix(steps, 2 * half, True)
    mine_copy.wait()
    other_copy.wait()
    spread(
        lambda band, row: all_ref[:, band, :, row].reshape(lons, chans),
        bands, rows, matrix, pull_ref,
    )

    def step(index, carry):
        start = index * block
        slot = index & 1

        @pl.when(index + 1 < count)
        def _():
            slope_copy(index + 1, 1 - slot).start()

        back = conv_block(pull_ref, w2t_ref, start, block, True)
        slope_copy(index, slot).wait()
        pull = (back * slope_ref[slot]).astype(BF16).astype(F32)
        pull = pull.reshape(block, steps, 16, chans)
        last, head = pull[:, steps - 1], pull[:, 0]
        before = jnp.concatenate([last[:, 15:], last[:, :15]], axis=1)
        after = jnp.concatenate([head[:, 1:], head[:, :1]], axis=1)
        to = pl.ds(1 + start, block)
        first_ref[to, 1 : 1 + steps] = pull.astype(BF16)
        first_ref[to, 0] = before.astype(BF16)
        first_ref[to, steps + 1] = after.astype(BF16)
        return carry

    hidden_copy.wait()
    tap_sums(hidden_ref, pull_ref, g2_ref, g2_hbm, g2_sems)
    lax.fori_loop(0, count, step, 0)
    state_copy.wait()
    tap_sums(state_ref, first_ref, g1_ref, g1_hbm, g1_sems)

    top = lax.axis_index("lat") * rows
    left = lax.axis_index("lon") * cols
    place = iota((3 * cols, lons), 0)
    shift = 1 - lax.shift_right_logical(place, cols.bit_length() - 1)
    lon = left + (place & (cols - 1)) + shift
    lon = jnp.where(lon < 0, lon + lons, jnp.where(lon >= lons, lon - lons, lon))
    column = iota((3 * cols, lons), 1)
    theirs = (column & 15) * steps + lax.shift_right_logical(column, 4)
    select = jnp.where(theirs == lon, 1.0, 0.0).astype(BF16)
    for row in range(rows + 2):
        line = first_ref[top + row, 1 : 1 + steps].reshape(lons, chans)
        near = dot(select, line).astype(BF16)
        for b in range(3):
            near_ref[b, row * cols : (row + 1) * cols, :] = near[b * cols : (b + 1) * cols]
    total = adj_ref[...]
    for a in range(3):
        for b in range(3):
            total = total + dot_nt(
                near_ref[b, (2 - a) * cols : (2 - a + rows) * cols, :], w1_ref[3 * a + b]
            )
    grad_ref[...] = total
    for tap in range(9):
        pltpu.make_async_copy(g2_ref.at[tap], g2_hbm.at[tap], g2_sems.at[tap]).wait()
        pltpu.make_async_copy(g1_ref.at[tap], g1_hbm.at[tap], g1_sems.at[tap]).wait()


def tail(mine, other, slope, hidden, state, w2t, w1, adjoint):
    bands, half, rows, group, chans = mine.shape
    lats, lons = bands * rows, 2 * half * group
    steps = lons // 16
    block = 512 // lons
    padded = pltpu.VMEM((lats + 2, steps + 2, 16, chans), BF16)
    anywhere = pl.BlockSpec(memory_space=pl.ANY)
    return pl.pallas_call(
        functools.partial(tail_kernel, block),
        out_shape=[
            jax.ShapeDtypeStruct((rows * group, chans), F32),
            jax.ShapeDtypeStruct((9, chans, chans), F32),
            jax.ShapeDtypeStruct((9, chans, chans), F32),
        ],
        in_specs=[anywhere] * 5 + [vmem()] * 3,
        out_specs=[vmem(), anywhere, anywhere],
        scratch_shapes=[
            pltpu.VMEM((2,) + mine.shape, BF16),
            padded,
            padded,
            pltpu.VMEM((3, (rows + 2) * group, chans), BF16),
            pltpu.VMEM((2, block * lons, chans), F32),
            pltpu.VMEM((chans, lats * lons), BF16),
            pltpu.VMEM((chans, lats * lons), BF16),
            pltpu.VMEM((9, chans, chans), F32),
            pltpu.VMEM((9, chans, chans), F32),
            pltpu.SemaphoreType.DMA((2,)),
            pltpu.SemaphoreType.DMA((4,)),
            pltpu.SemaphoreType.DMA((9,)),
            pltpu.SemaphoreType.DMA((9,)),
        ],
        compiler_params=params(),
        name="tail",
    )(mine, other, slope, hidden, state, w2t, w1, adjoint)


def with_halo(x, axis, dim, width, wrap):
    count, length = (lax.axis_size(axis), x.shape[dim])
    up = [(i, (i + 1) % count) for i in range(count if wrap else count - 1)]
    down = [(j, i) for i, j in up]
    last = lax.slice_in_dim(x, length - width, length, axis=dim)
    first = lax.slice_in_dim(x, 0, width, axis=dim)
    before = lax.ppermute(last, axis, up)
    after = lax.ppermute(first, axis, down)
    return jnp.concatenate([before, x, after], axis=dim)


def gather_state(x):
    return lax.all_gather(lax.all_gather(x, "lon"), "lat")


def gather_tiles(x):
    bands, tiles = lax.axis_size("lat"), lax.axis_size("lon")
    half = tiles // 2
    same = [[2 * q + core for q in range(half)] for core in range(2)]
    copies = jnp.broadcast_to(x[None], (half,) + x.shape)
    line = lax.all_to_all(copies, "lon", 0, 0, axis_index_groups=same, tiled=True)
    copies = jnp.broadcast_to(line[None], (bands,) + line.shape)
    mine = lax.all_to_all(copies, "lat", 0, 0, tiled=True)
    other = lax.ppermute(mine, "lon", [(i, i ^ 1) for i in range(tiles)])
    return mine, other


def per_device(
    state, weight_first, weight_second, obs_owner, obs_cell, obs_level, obs_count, obs_frac,
    obs_value, obs_weight,
):
    rows, cols, chans = state.shape
    bands = lax.axis_size("lat")
    devices = lax.axis_size(("lat", "lon"))
    slots = max(2, 3 * obs_value.shape[0] // (2 * devices))
    outgoing = route(
        devices, slots, chans, obs_owner, obs_cell, obs_level, obs_count, obs_frac, obs_value,
        obs_weight,
    )
    got = lax.all_to_all(outgoing, ("lat", "lon"), split_axis=0, concat_axis=0, tiled=True)
    wide = with_halo(with_halo(state, "lon", 1, 2, True), "lat", 0, 2, False)
    state_all = gather_state(state)
    adjoint, pullback = forward(slots, bands, wide, weight_first, weight_second, got)
    mine, other = gather_tiles(pullback.reshape(rows, cols, chans))
    slope, hidden, turned, w2t = whole(state_all, weight_first, weight_second)
    grad, g1, g2 = tail(mine, other, slope, hidden, turned, w2t, weight_first, adjoint)
    return grad.reshape(rows, cols, chans), g1, g2


def solution(mesh):
    both = P(("lat", "lon"), None)
    placed = (
        P("lat", "lon", None),
        P(),
        P(),
        both,
        both,
        both,
        P(("lat", "lon")),
        P(("lat", "lon"), None, None),
        both,
        both,
    )
    return jax.shard_map(
        per_device,
        mesh=mesh,
        in_specs=placed,
        out_specs=(P("lat", "lon", None), P(), P()),
        check_vma=False,
    )
```

```python
import functools
import math

import jax
import jax.numpy as jnp
from jax import lax
from jax.experimental import pallas as pl
from jax.experimental.pallas import tpu as pltpu
from jax.sharding import PartitionSpec as P

F32 = jnp.float32
BF16 = jnp.bfloat16
FIELDS = 5
WHOLE_CELLS = 4096
VMEM_LIMIT = 60 * 1024 * 1024


def params(limit=VMEM_LIMIT):
    return pltpu.CompilerParams(vmem_limit_bytes=limit)


def vmem():
    return pl.BlockSpec(memory_space=pltpu.VMEM)


def iota(shape, dim, dtype=jnp.int32):
    return lax.broadcasted_iota(jnp.int32, shape, dim).astype(dtype)


def dot(x, y, precision=None):
    return jnp.dot(x, y, precision=precision, preferred_element_type=F32)


def dot_nt(x, y, precision=None):
    return lax.dot_general(
        x, y, (((1,), (1,)), ((), ())), precision=precision, preferred_element_type=F32
    )


def slot_layout(slots):
    full, rest = divmod(slots, 4)
    rows = full * FIELDS + (0 if rest == 0 else -(-FIELDS // 2))
    return full, rest, -(-rows // 8) * 8


def route_kernel(
    devices, slots, chans, owner_ref, count_ref, cell_ref, level_ref, frac_ref, value_ref,
    weight_ref, out_ref
):
    width, blocks = value_ref.shape
    owner = owner_ref[...].astype(F32)
    across = jnp.broadcast_to(owner, (blocks, blocks))
    down = across.T
    earlier = iota((blocks, blocks), 0) < iota((blocks, blocks), 1)
    hits = jnp.where(jnp.logical_and(across == down, earlier), 1.0, 0.0)
    rank = jnp.sum(hits, axis=0, keepdims=True)
    target = rank * float(devices) + owner
    places = iota((slots * devices, blocks), 0, F32) == target
    onehot = jnp.where(places, 1.0, 0.0)
    valid = iota((width, blocks), 0) < count_ref[...]
    fields = jnp.concatenate(
        [
            frac_ref[0],
            frac_ref[1],
            value_ref[...],
            jnp.where(valid, weight_ref[...], 0.0),
            (cell_ref[...] * chans + level_ref[...]).astype(F32),
        ],
        axis=0,
    )
    placed = dot_nt(onehot, fields, lax.Precision.HIGHEST)
    full, rest, rows = slot_layout(slots)
    out_ref[...] = jnp.zeros(out_ref.shape, F32)
    for slot in range(slots):
        for field in range(FIELDS):
            piece = placed[
                slot * devices : (slot + 1) * devices, field * width : (field + 1) * width
            ]
            if slot < 4 * full:
                row, lane = (slot // 4) * FIELDS + field, (slot % 4) * width
            else:
                row = full * FIELDS + field // 2
                lane = (field % 2) * 2 * width + (slot - 4 * full) * width
            out_ref[:, row, lane : lane + width] = piece


def route(devices, slots, chans, obs_owner, obs_cell, obs_level, obs_count, obs_frac, obs_value,
          obs_weight):
    blocks = obs_value.shape[0]
    rows = slot_layout(slots)[2]
    return pl.pallas_call(
        functools.partial(route_kernel, devices, slots, chans),
        out_shape=jax.ShapeDtypeStruct((devices, rows, 128), F32),
        in_specs=[vmem()] * 7,
        out_specs=vmem(),
        compiler_params=params(),
        name="route",
    )(
        obs_owner.reshape(1, blocks),
        obs_count.reshape(1, blocks),
        obs_cell.T,
        obs_level.T,
        jnp.transpose(obs_frac, (1, 2, 0)),
        obs_value.T,
        obs_weight.T,
    )


def silu_parts(first):
    sig = 1.0 / (1.0 + jnp.exp(-first))
    return sig, first * sig


def forward_kernel(slots, tiles, group, parts, *refs):
    piece_refs, (w1_ref, w2_ref, got_ref, adj_ref, pull_ref) = refs[:9], refs[9:14]
    line_ref, shift_ref, hid_ref, obs_ref, sum_ref = refs[14:]
    rows, cols, chans = piece_refs[4].shape
    span = 32
    heights, widths = (2, rows, 2), (2, cols, 2)
    for place in range(9):
        down, over = place // 3, place % 3
        y, x = (0, 2, 2 + rows)[down], (0, 2, 2 + cols)[over]
        line_ref[y : y + heights[down], x : x + widths[over], :] = piece_refs[place][...].astype(F32)
    line_ref[:, cols + 4 :, :] = jnp.zeros(
        (rows + 4, line_ref.shape[1] - cols - 4, chans), F32
    )
    first = jnp.zeros(((rows + 2) * span, chans), F32)
    for b in range(3):
        shift_ref[...] = (
            line_ref[:, b : b + span, :].astype(BF16).reshape((rows + 4) * span, chans)
        )
        for a in range(3):
            first = first + dot(
                shift_ref[a * span : a * span + (rows + 2) * span, :], w1_ref[3 * a + b]
            )
    hidden = silu_parts(first)[1].astype(BF16).astype(F32).reshape(rows + 2, span, chans)
    lat = lax.axis_index("lat") * rows + iota((rows + 2, span, chans), 0) - 1
    hidden = jnp.where(jnp.logical_and(lat >= 0, lat < tiles * rows), hidden, 0.0)
    hid_ref[...] = hidden
    total = line_ref[2 : 2 + rows, 2 : 2 + cols, :].reshape(rows * cols, chans)
    for b in range(3):
        shift_ref[0 : (rows + 2) * cols, :] = (
            hid_ref[:, b : b + cols, :].astype(BF16).reshape((rows + 2) * cols, chans)
        )
        for a in range(3):
            total = total + dot(
                shift_ref[a * cols : a * cols + rows * cols, :], w2_ref[3 * a + b]
            )
    cells = rows * cols
    turned = total.T
    grid_high = turned.astype(BF16)
    grid_low = (turned - grid_high.astype(F32)).astype(BF16)
    grid_both = jnp.concatenate([grid_high, grid_low], axis=1)

    devices = got_ref.shape[0]
    full, rest, _ = slot_layout(slots)
    half = devices // 2
    for field in range(FIELDS):
        for part in range(full):
            obs_ref[field, part * devices : (part + 1) * devices, :] = got_ref[
                :, part * FIELDS + field, :
            ]
        if rest:
            tail = got_ref[:, full * FIELDS + field // 2, :]
            low, high = tail[:half], tail[half:]
            if field % 2 == 0:
                high = pltpu.roll(high, 64, 1)
            else:
                low = pltpu.roll(low, 64, 1)
            obs_ref[field, full * devices : full * devices + half, :] = jnp.where(
                iota((half, 128), 1) < 64, low, high
            )
    code = obs_ref[4].astype(jnp.int32)
    shift = chans.bit_length() - 1
    cell = lax.shift_right_logical(code, shift)
    obs_ref[4] = (code & (chans - 1)).astype(F32)
    obs_ref[0] = obs_ref[0] + lax.shift_right_logical(cell, 4).astype(F32)
    obs_ref[1] = obs_ref[1] + (cell & (cols - 1)).astype(F32)

    sum_ref[...] = jnp.zeros(sum_ref.shape, F32)
    count = obs_ref.shape[1] // (group * parts)
    row_ids = iota((rows, 128), 0, F32)
    col_ids = iota((cols, 128), 0, F32)
    level_ids = iota((chans, 128), 0, F32)

    def add_group(start):
        high, low, masks, marks = [], [], [], []
        for piece in range(group):
            mark = [obs_ref[field, pl.ds(start + piece, 1), :] for field in range(FIELDS)]
            up = jnp.maximum(0.0, 1.0 - jnp.abs(row_ids - mark[0]))
            along = jnp.maximum(0.0, 1.0 - jnp.abs(col_ids - mark[1]))
            weights = (up[:, None, :] * along[None, :, :]).reshape(cells, 128)
            weights_high = weights.astype(BF16)
            high.append(weights_high)
            low.append((weights - weights_high.astype(F32)).astype(BF16))
            masks.append(level_ids == mark[4])
            marks.append(mark)
        high = jnp.concatenate(high, axis=1)
        low = jnp.concatenate(low, axis=1)
        sampled = dot(grid_both, jnp.concatenate([high, high], axis=0)) + dot(grid_high, low)
        hot_high, hot_low = [], []
        for piece in range(group):
            mine = sampled[:, piece * 128 : (piece + 1) * 128]
            predicted = jnp.sum(jnp.where(masks[piece], mine, 0.0), axis=0, keepdims=True)
            misfit = marks[piece][3] * (predicted - marks[piece][2])
            misfit_high = misfit.astype(BF16).astype(F32)
            hot_high.append(jnp.where(masks[piece], misfit_high, 0.0).astype(BF16))
            hot_low.append(jnp.where(masks[piece], misfit - misfit_high, 0.0).astype(BF16))
        hot_high = jnp.concatenate(hot_high, axis=1)
        hot_low = jnp.concatenate(hot_low, axis=1)
        mixed = dot_nt(jnp.concatenate([hot_high, hot_low], axis=0), high)
        return mixed[:chans] + (mixed[chans:] + dot_nt(hot_high, low))

    def step(index, carry):
        total = sum_ref[...]
        for part in range(parts):
            total = total + add_group((index * parts + part) * group)
        sum_ref[...] = total
        return carry

    lax.fori_loop(0, count, step, 0)
    adjoint = sum_ref[...].T
    adj_ref[...] = adjoint
    pull_ref[...] = adjoint.astype(BF16)


def forward(slots, tiles, pieces, w1, w2, got):
    rows, cols, chans = pieces[4].shape
    devices = got.shape[0]
    full, rest, _ = slot_layout(slots)
    groups = full * devices + (devices // 2 if rest else 0)
    return pl.pallas_call(
        functools.partial(forward_kernel, slots, tiles, 2, 4),
        out_shape=[
            jax.ShapeDtypeStruct((rows * cols, chans), F32),
            jax.ShapeDtypeStruct((rows * cols, chans), BF16),
        ],
        in_specs=[vmem()] * 12,
        out_specs=[vmem()] * 2,
        scratch_shapes=[
            pltpu.VMEM((rows + 4, 40, chans), F32),
            pltpu.VMEM(((rows + 4) * 32, chans), BF16),
            pltpu.VMEM((rows + 2, 32, chans), F32),
            pltpu.VMEM((FIELDS, groups, 128), F32),
            pltpu.VMEM((chans, rows * cols), F32),
        ],
        compiler_params=params(),
        name="forward",
    )(*pieces, w1, w2, got)


def spread_matrix(steps, tiles, split):
    lons = 16 * steps
    place = iota(((steps + 2) * 16, lons), 0)
    lon = (place & 15) * steps + lax.shift_right_logical(place, 4) - 1
    lon = jnp.where(lon < 0, lon + lons, jnp.where(lon >= lons, lon - lons, lon))
    column = iota(((steps + 2) * 16, lons), 1)
    if split:
        half = tiles // 2
        chunk = lax.shift_right_logical(column, 4)
        core = lax.shift_right_logical(chunk, half.bit_length() - 1)
        column = (2 * (chunk & (half - 1)) + core) * 16 + (column & 15)
    return jnp.where(column == lon, 1.0, 0.0).astype(BF16)


def spread(line_of, bands, rows, matrix, pad_ref):
    steps = pad_ref.shape[1] - 2
    blank = jnp.zeros(pad_ref.shape[1:], BF16)
    pad_ref[0] = blank
    pad_ref[bands * rows + 1] = blank

    def place(band, carry):
        for row in range(rows):
            line = line_of(band, row)
            pad_ref[1 + band * rows + row] = (
                dot(matrix, line).astype(BF16).reshape(steps + 2, 16, line.shape[1])
            )
        return carry

    lax.fori_loop(0, bands, place, 0)


def spread_state_kernel(all_ref, pad_ref):
    bands, tiles, rows, group, chans = all_ref.shape
    matrix = spread_matrix(pad_ref.shape[1] - 2, tiles, False)
    spread(
        lambda band, row: all_ref[band, :, row].reshape(tiles * group, chans),
        bands, rows, matrix, pad_ref,
    )


def spread_state(state_all):
    bands, tiles, rows, group, chans = state_all.shape
    return pl.pallas_call(
        spread_state_kernel,
        out_shape=jax.ShapeDtypeStruct((bands * rows + 2, tiles * group // 16 + 2, 16, chans), BF16),
        in_specs=[vmem()],
        out_specs=vmem(),
        compiler_params=params(),
        name="spread_state",
    )(state_all)


def spread_pull_kernel(mine_hbm, other_hbm, pad_ref, plain_ref, all_ref, sems):
    _, bands, half, rows, cols, chans = all_ref.shape
    steps = plain_ref.shape[1]
    core = lax.axis_index("lon") & 1
    copies = [
        pltpu.make_async_copy(mine_hbm, all_ref.at[core], sems.at[0]),
        pltpu.make_async_copy(other_hbm, all_ref.at[1 - core], sems.at[1]),
    ]
    for copy in copies:
        copy.start()
    matrix = spread_matrix(steps, 2 * half, True)
    for copy in copies:
        copy.wait()
    spread(
        lambda band, row: all_ref[:, band, :, row].reshape(steps * 16, chans),
        bands, rows, matrix, pad_ref,
    )
    plain_ref[...] = pad_ref[1 : bands * rows + 1, 1 : steps + 1]


def spread_pull(mine, other):
    bands, half, rows, group, chans = mine.shape
    lats, steps = bands * rows, 2 * half * group // 16
    return pl.pallas_call(
        spread_pull_kernel,
        out_shape=[
            jax.ShapeDtypeStruct((lats + 2, steps + 2, 16, chans), BF16),
            jax.ShapeDtypeStruct((lats, steps, 16, chans), BF16),
        ],
        in_specs=[pl.BlockSpec(memory_space=pl.ANY)] * 2,
        out_specs=[vmem()] * 2,
        scratch_shapes=[pltpu.VMEM((2,) + mine.shape, BF16), pltpu.SemaphoreType.DMA((2,))],
        compiler_params=params(),
        name="spread_pull",
    )(mine, other)


def pad_kernel(plain_ref, pad_ref):
    lats, steps, group, chans = plain_ref.shape
    blank = jnp.zeros(pad_ref.shape[1:], BF16)
    pad_ref[0] = blank
    pad_ref[lats + 1] = blank

    def step(lat, carry):
        pad_ref[lat + 1, 1 : steps + 1] = plain_ref[lat]
        last = plain_ref[lat, steps - 1].astype(F32)
        head = plain_ref[lat, 0].astype(F32)
        pad_ref[lat + 1, 0] = jnp.concatenate([last[15:], last[:15]], axis=0).astype(BF16)
        pad_ref[lat + 1, steps + 1] = jnp.concatenate([head[1:], head[:1]], axis=0).astype(BF16)
        return carry

    lax.fori_loop(0, lats, step, 0, unroll=4)


def pad(plain):
    lats, steps, group, chans = plain.shape
    return pl.pallas_call(
        pad_kernel,
        out_shape=jax.ShapeDtypeStruct((lats + 2, steps + 2, group, chans), BF16),
        in_specs=[vmem()],
        out_specs=vmem(),
        compiler_params=params(),
        name="pad",
    )(plain)


def conv(padded, weight):
    chans = weight.shape[1]
    return lax.conv_general_dilated(
        padded, weight.reshape(3, 3, chans, -1), (1, 1), "VALID",
        dimension_numbers=("HWNC", "HWIO", "HWNC"), preferred_element_type=F32,
    )


def convt(padded, weight):
    chans = weight.shape[1]
    return lax.conv_general_dilated(
        padded, lax.rev(weight.reshape(3, 3, chans, -1), (0, 1)), (1, 1), "VALID",
        dimension_numbers=("HWNC", "HWOI", "HWNC"), preferred_element_type=F32,
    )


def tap_grads(padded, pull):
    chans = pull.shape[3]
    grads = lax.conv_general_dilated(
        padded, pull, (1, 1), "VALID",
        dimension_numbers=("HWCN", "HWIO", "HWNC"), preferred_element_type=F32,
    )
    return grads.reshape(9, -1, chans)


def local_kernel(rows, cols, pull_hbm, w1_ref, adj_ref, grad_ref, pull_ref, near_ref, sem):
    lats, steps, _, chans = pull_hbm.shape
    lons = steps * 16
    top = lax.axis_index("lat") * rows - 1
    begin = jnp.clip(top, 0, lats - rows - 2)
    copy = pltpu.make_async_copy(pull_hbm.at[pl.ds(begin, rows + 2)], pull_ref, sem)
    copy.start()
    left = lax.axis_index("lon") * cols
    place = iota((3 * cols, lons), 0)
    shift = 1 - lax.shift_right_logical(place, cols.bit_length() - 1)
    lon = left + (place & (cols - 1)) + shift
    lon = jnp.where(lon < 0, lon + lons, jnp.where(lon >= lons, lon - lons, lon))
    column = iota((3 * cols, lons), 1)
    theirs = (column & 15) * steps + lax.shift_right_logical(column, 4)
    select = jnp.where(theirs == lon, 1.0, 0.0)
    copy.wait()
    for row in range(rows + 2):
        lat = top + row
        inside = jnp.logical_and(lat >= 0, lat < lats)
        line = pull_ref[jnp.clip(lat - begin, 0, rows + 1)].reshape(lons, chans)
        chosen = jnp.where(inside, select, 0.0).astype(BF16)
        near = dot(chosen, line).astype(BF16)
        for b in range(3):
            near_ref[b, row * cols : (row + 1) * cols, :] = near[b * cols : (b + 1) * cols]
    total = adj_ref[...]
    for a in range(3):
        for b in range(3):
            total = total + dot_nt(
                near_ref[b, (2 - a) * cols : (2 - a + rows) * cols, :], w1_ref[3 * a + b]
            )
    grad_ref[...] = total


def local_grad(rows, cols, pull, w1, adjoint):
    lats, steps, _, chans = pull.shape
    return pl.pallas_call(
        functools.partial(local_kernel, rows, cols),
        out_shape=jax.ShapeDtypeStruct((rows * cols, chans), F32),
        in_specs=[pl.BlockSpec(memory_space=pl.ANY), vmem(), vmem()],
        out_specs=vmem(),
        scratch_shapes=[
            pltpu.VMEM((rows + 2, steps, 16, chans), BF16),
            pltpu.VMEM((3, (rows + 2) * cols, chans), BF16),
            pltpu.SemaphoreType.DMA,
        ],
        compiler_params=params(),
        name="local_grad",
    )(pull, w1, adjoint)


def with_halo(x, sides, width, wrap):
    for axis, dim in sides:
        count, length = (lax.axis_size(axis), x.shape[dim])
        up = [(i, (i + 1) % count) for i in range(count if wrap else count - 1)]
        down = [(j, i) for i, j in up]
        last = lax.slice_in_dim(x, length - width, length, axis=dim)
        first = lax.slice_in_dim(x, 0, width, axis=dim)
        before = lax.ppermute(last, axis, up)
        after = lax.ppermute(first, axis, down)
        x = jnp.concatenate([before, x, after], axis=dim)
    return x


def widen_tile(field):
    across = with_halo(field, (("lon", 1),), 1, True)
    return with_halo(across, (("lat", 0),), 1, False)


def tile_conv(padded, weight, rows, cols, flipped):
    total = jnp.zeros((rows * cols, weight.shape[2]), jnp.float32)
    for first_tap in range(3):
        for second_tap in range(3):
            if flipped:
                piece = padded[
                    2 - first_tap : 2 - first_tap + rows, 2 - second_tap : 2 - second_tap + cols
                ]
                total = total + lax.dot_general(
                    piece.reshape(rows * cols, -1),
                    weight[3 * first_tap + second_tap],
                    (((1,), (1,)), ((), ())),
                    preferred_element_type=jnp.float32,
                )
            else:
                piece = padded[first_tap : first_tap + rows, second_tap : second_tap + cols]
                total = total + jnp.dot(
                    piece.reshape(rows * cols, -1),
                    weight[3 * first_tap + second_tap],
                    preferred_element_type=jnp.float32,
                )
    return total.reshape(rows, cols, -1)


def tile_grads(padded, pullback, rows, cols):
    flat_pull = pullback.reshape(rows * cols, -1)
    result = []
    for first_tap in range(3):
        for second_tap in range(3):
            piece = padded[first_tap : first_tap + rows, second_tap : second_tap + cols].reshape(
                rows * cols, -1
            )
            result.append(
                lax.dot_general(
                    piece, flat_pull, (((0,), (0,)), ((), ())), preferred_element_type=jnp.float32
                )
            )
    return jnp.stack(result)


def route_blocks(obs_owner, obs_cell, obs_level, obs_count, obs_frac, obs_value, obs_weight):
    devices = lax.axis_size(("lat", "lon"))
    blocks, width = obs_value.shape
    slots = max(2, 3 * blocks // (2 * devices))
    owner = obs_owner[:, 0]
    order = lax.broadcasted_iota(jnp.int32, (blocks, blocks), 1) < lax.broadcasted_iota(
        jnp.int32, (blocks, blocks), 0
    )
    earlier = jnp.logical_and(owner[:, None] == owner[None, :], order)
    rank = jnp.sum(earlier.astype(jnp.int32), axis=1)
    target = owner * slots + rank
    valid = (lax.broadcasted_iota(jnp.int32, (blocks, width), 1) < obs_count[:, None]).astype(
        jnp.float32
    )
    packed = jnp.stack(
        [
            obs_frac[:, 0, :],
            obs_frac[:, 1, :],
            obs_value,
            obs_weight,
            obs_cell.astype(jnp.float32),
            obs_level.astype(jnp.float32),
            valid,
        ],
        axis=1,
    )
    outgoing = jnp.zeros((devices * slots, 7, width), jnp.float32).at[target].set(packed)
    return lax.all_to_all(outgoing, ("lat", "lon"), split_axis=0, concat_axis=0, tiled=True)


def observe(corrected, arrived, rows, cols, chans):
    fields = jnp.transpose(arrived, (1, 0, 2)).reshape(7, -1)
    row_total = fields.shape[1]
    span_rows = math.gcd(row_total, 1024)
    fields = jnp.transpose(fields.reshape(7, row_total // span_rows, span_rows), (1, 0, 2))
    grid = corrected.reshape(rows * cols, chans)
    cells = lax.broadcasted_iota(jnp.int32, (1, rows * cols), 1)
    levels = lax.broadcasted_iota(jnp.int32, (1, chans), 1)

    def advance(summed, portion):
        frac_lat = portion[0][:, None]
        frac_lon = portion[1][:, None]
        corner = portion[4].astype(jnp.int32)[:, None]
        level = portion[5].astype(jnp.int32)[:, None]
        weights = (1.0 - frac_lat) * (1.0 - frac_lon) * (cells == corner).astype(jnp.float32)
        weights = weights + (1.0 - frac_lat) * frac_lon * (cells == corner + 1).astype(jnp.float32)
        weights = weights + frac_lat * (1.0 - frac_lon) * (cells == corner + cols).astype(
            jnp.float32
        )
        weights = weights + frac_lat * frac_lon * (cells == corner + cols + 1).astype(jnp.float32)
        onehot = (levels == level).astype(jnp.float32)
        sampled = jnp.dot(
            weights, grid, precision=lax.Precision.HIGHEST, preferred_element_type=jnp.float32
        )
        predicted = jnp.sum(sampled * onehot, axis=1)
        misfit = portion[6] * portion[3] * (predicted - portion[2])
        summed = summed + lax.dot_general(
            weights,
            onehot * misfit[:, None],
            (((0,), (0,)), ((), ())),
            precision=lax.Precision.HIGHEST,
            preferred_element_type=jnp.float32,
        )
        return (summed, None)

    summed, unused = lax.scan(advance, jnp.zeros((rows * cols, chans), jnp.float32), fields)
    return summed.reshape(rows, cols, chans)


def by_tiles(
    state,
    weight_first,
    weight_second,
    obs_owner,
    obs_cell,
    obs_level,
    obs_count,
    obs_frac,
    obs_value,
    obs_weight,
):
    rows, cols, chans = state.shape
    wide_state = widen_tile(state)
    first = tile_conv(wide_state, weight_first, rows, cols, False)
    hidden = jax.nn.silu(first).astype(jnp.bfloat16)
    wide_hidden = widen_tile(hidden)
    corrected = state.astype(jnp.float32) + tile_conv(wide_hidden, weight_second, rows, cols, False)
    arrived = route_blocks(
        obs_owner, obs_cell, obs_level, obs_count, obs_frac, obs_value, obs_weight
    )
    adjoint = observe(corrected, arrived, rows, cols, chans)
    pullback = adjoint.astype(jnp.bfloat16)
    wide_pull = widen_tile(pullback)
    local_second = tile_grads(wide_hidden, pullback, rows, cols)
    back = tile_conv(wide_pull, weight_second, rows, cols, True)
    sig = jax.nn.sigmoid(first)
    pull_first = (back * sig * (1.0 + first * (1.0 - sig))).astype(jnp.bfloat16)
    wide_pull_first = widen_tile(pull_first)
    local_first = tile_grads(wide_state, pull_first, rows, cols)
    state_grad = adjoint + tile_conv(wide_pull_first, weight_first, rows, cols, True)
    grad_first, grad_second = lax.psum((local_first, local_second), ("lat", "lon"))
    return (state_grad, grad_first, grad_second)


def halo_pieces(x):
    bands, tiles = lax.axis_size("lat"), lax.axis_size("lon")
    rows, cols, _ = x.shape
    pieces = []
    for dy in (-1, 0, 1):
        for dx in (-1, 0, 1):
            if dy == 0 and dx == 0:
                pieces.append(x)
                continue
            block = x
            if dy:
                block = block[rows - 2 :] if dy < 0 else block[:2]
            if dx:
                block = block[:, cols - 2 :] if dx < 0 else block[:, :2]
            pairs = []
            for lat in range(bands):
                for lon in range(tiles):
                    from_lat, from_lon = lat + dy, (lon + dx) % tiles
                    if 0 <= from_lat < bands:
                        pairs.append((from_lat * tiles + from_lon, lat * tiles + lon))
            pieces.append(lax.ppermute(block, ("lat", "lon"), pairs))
    return pieces


def gather_state(x):
    bands, tiles = lax.axis_size("lat"), lax.axis_size("lon")
    return lax.all_gather(x, ("lat", "lon")).reshape((bands, tiles) + x.shape)


def gather_tiles(x):
    bands, tiles = lax.axis_size("lat"), lax.axis_size("lon")
    half = tiles // 2
    same = [[2 * q + core for q in range(half)] for core in range(2)]
    copies = jnp.broadcast_to(x[None], (half,) + x.shape)
    line = lax.all_to_all(copies, "lon", 0, 0, axis_index_groups=same, tiled=True)
    copies = jnp.broadcast_to(line[None], (bands,) + line.shape)
    mine = lax.all_to_all(copies, "lat", 0, 0, tiled=True)
    other = lax.ppermute(mine, "lon", [(i, i ^ 1) for i in range(tiles)])
    return mine, other


def per_device(
    state, weight_first, weight_second, obs_owner, obs_cell, obs_level, obs_count, obs_frac,
    obs_value, obs_weight,
):
    rows, cols, chans = state.shape
    bands = lax.axis_size("lat")
    devices = lax.axis_size(("lat", "lon"))
    if devices * rows * cols > WHOLE_CELLS:
        return by_tiles(
            state, weight_first, weight_second, obs_owner, obs_cell, obs_level, obs_count,
            obs_frac, obs_value, obs_weight,
        )
    slots = max(2, 3 * obs_value.shape[0] // (2 * devices))
    state_all = gather_state(state)
    pieces = halo_pieces(state)
    outgoing = route(
        devices, slots, chans, obs_owner, obs_cell, obs_level, obs_count, obs_frac, obs_value,
        obs_weight,
    )
    got = lax.all_to_all(outgoing, ("lat", "lon"), split_axis=0, concat_axis=0, tiled=True)
    adjoint, pullback = forward(slots, bands, pieces, weight_first, weight_second, got)
    mine, other = gather_tiles(pullback.reshape(rows, cols, chans))

    wide_state = spread_state(state_all)
    first = conv(wide_state, weight_first)
    sig = jax.nn.sigmoid(first)
    hidden = (first * sig).astype(BF16)
    slope = sig * (1.0 + first * (1.0 - sig))
    wide_hidden = pad(hidden)

    wide_pull, pull = spread_pull(mine, other)
    g2 = tap_grads(wide_hidden, pull)
    pull_first = (convt(wide_pull, weight_second) * slope).astype(BF16)
    g1 = tap_grads(wide_state, pull_first)
    grad = local_grad(rows, cols, pull_first, weight_first, adjoint)
    return grad.reshape(rows, cols, chans), g1, g2


def solution(mesh):
    both = P(("lat", "lon"), None)
    placed = (
        P("lat", "lon", None),
        P(),
        P(),
        both,
        both,
        both,
        P(("lat", "lon")),
        P(("lat", "lon"), None, None),
        both,
        both,
    )
    return jax.shard_map(
        per_device,
        mesh=mesh,
        in_specs=placed,
        out_specs=(P("lat", "lon", None), P(), P()),
        check_vma=False,
    )
```

```python
import functools
import math

import jax
import jax.numpy as jnp
from jax import lax
from jax.experimental import pallas as pl
from jax.experimental.pallas import tpu as pltpu
from jax.sharding import PartitionSpec as P

F32 = jnp.float32
BF16 = jnp.bfloat16
FIELDS = 5
SPAN = 32
WHOLE_CELLS = 4096
VMEM_LIMIT = 60 * 1024 * 1024


def params(limit=VMEM_LIMIT):
    return pltpu.CompilerParams(vmem_limit_bytes=limit)


def cost(flops, moved):
    return pl.CostEstimate(flops=int(flops), bytes_accessed=int(moved), transcendentals=0)


def vmem():
    return pl.BlockSpec(memory_space=pltpu.VMEM)


def iota(shape, dim, dtype=jnp.int32):
    return lax.broadcasted_iota(jnp.int32, shape, dim).astype(dtype)


def dot(x, y, precision=None):
    return jnp.dot(x, y, precision=precision, preferred_element_type=F32)


def dot_nt(x, y, precision=None):
    return lax.dot_general(
        x, y, (((1,), (1,)), ((), ())), precision=precision, preferred_element_type=F32
    )


def slot_layout(slots):
    full, rest = divmod(slots, 4)
    rows = full * FIELDS + (0 if rest == 0 else -(-FIELDS // 2))
    return full, rest, -(-rows // 8) * 8


def route_kernel(
    devices, slots, chans, owner_ref, count_ref, cell_ref, level_ref, frac_ref, value_ref,
    weight_ref, out_ref
):
    width, blocks = value_ref.shape
    owner = owner_ref[...].astype(F32)
    across = jnp.broadcast_to(owner, (blocks, blocks))
    down = across.T
    earlier = iota((blocks, blocks), 0) < iota((blocks, blocks), 1)
    hits = jnp.where(jnp.logical_and(across == down, earlier), 1.0, 0.0)
    rank = jnp.sum(hits, axis=0, keepdims=True)
    target = rank * float(devices) + owner
    places = iota((slots * devices, blocks), 0, F32) == target
    onehot = jnp.where(places, 1.0, 0.0)
    valid = iota((width, blocks), 0) < count_ref[...]
    fields = jnp.concatenate(
        [
            frac_ref[0],
            frac_ref[1],
            value_ref[...],
            jnp.where(valid, weight_ref[...], 0.0),
            (cell_ref[...] * chans + level_ref[...]).astype(F32),
        ],
        axis=0,
    )
    placed = dot_nt(onehot, fields, lax.Precision.HIGHEST)
    full, rest, rows = slot_layout(slots)
    out_ref[...] = jnp.zeros(out_ref.shape, F32)
    for slot in range(slots):
        for field in range(FIELDS):
            piece = placed[
                slot * devices : (slot + 1) * devices, field * width : (field + 1) * width
            ]
            if slot < 4 * full:
                row, lane = (slot // 4) * FIELDS + field, (slot % 4) * width
            else:
                row = full * FIELDS + field // 2
                lane = (field % 2) * 2 * width + (slot - 4 * full) * width
            out_ref[:, row, lane : lane + width] = piece


def route(devices, slots, chans, obs_owner, obs_cell, obs_level, obs_count, obs_frac, obs_value,
          obs_weight):
    blocks = obs_value.shape[0]
    rows = slot_layout(slots)[2]
    return pl.pallas_call(
        functools.partial(route_kernel, devices, slots, chans),
        out_shape=jax.ShapeDtypeStruct((devices, rows, 128), F32),
        in_specs=[vmem()] * 7,
        out_specs=vmem(),
        compiler_params=params(),
        name="route",
    )(
        obs_owner.reshape(1, blocks),
        obs_count.reshape(1, blocks),
        obs_cell.T,
        obs_level.T,
        jnp.transpose(obs_frac, (1, 2, 0)),
        obs_value.T,
        obs_weight.T,
    )


def silu_parts(first):
    sig = 1.0 / (1.0 + jnp.exp(-first))
    return sig, first * sig


def inside_grid(rows, shape, bands):
    lat = lax.axis_index("lat") * rows + iota(shape, 0) - 1
    return jnp.logical_and(lat >= 0, lat < bands * rows)


def forward_kernel(slots, bands, group, parts, tile_ref, north_ref, south_ref, west_ref, east_ref,
                   w1_ref, w2_ref, got_ref, adj_ref, pull_ref, slope_ref, line_ref, shift_ref,
                   hid_ref, obs_ref, sum_ref):
    rows, cols, chans = tile_ref.shape
    span = hid_ref.shape[1]
    line_ref[0:2, 2 : 2 + cols, :] = north_ref[...].astype(F32)
    line_ref[2 : 2 + rows, 2 : 2 + cols, :] = tile_ref[...].astype(F32)
    line_ref[2 + rows :, 2 : 2 + cols, :] = south_ref[...].astype(F32)
    line_ref[:, 0:2, :] = west_ref[...].astype(F32)
    line_ref[:, 2 + cols : 4 + cols, :] = east_ref[...].astype(F32)
    line_ref[:, cols + 4 :, :] = jnp.zeros(
        (rows + 4, line_ref.shape[1] - cols - 4, chans), F32
    )
    first = jnp.zeros(((rows + 2) * span, chans), F32)
    for b in range(3):
        shift_ref[...] = (
            line_ref[:, b : b + span, :].astype(BF16).reshape((rows + 4) * span, chans)
        )
        for a in range(3):
            first = first + dot(
                shift_ref[a * span : a * span + (rows + 2) * span, :], w1_ref[3 * a + b]
            )
    sig, hidden = silu_parts(first)
    slope_ref[...] = sig * (1.0 + first * (1.0 - sig))
    hidden = hidden.astype(BF16).astype(F32).reshape(rows + 2, span, chans)
    hidden = jnp.where(inside_grid(rows, hidden.shape, bands), hidden, 0.0)
    hid_ref[...] = hidden
    total = line_ref[2 : 2 + rows, 2 : 2 + cols, :].reshape(rows * cols, chans)
    for b in range(3):
        shift_ref[0 : (rows + 2) * cols, :] = (
            hid_ref[:, b : b + cols, :].astype(BF16).reshape((rows + 2) * cols, chans)
        )
        for a in range(3):
            total = total + dot(
                shift_ref[a * cols : a * cols + rows * cols, :], w2_ref[3 * a + b]
            )
    cells = rows * cols
    turned = total.T
    grid_high = turned.astype(BF16)
    grid_low = (turned - grid_high.astype(F32)).astype(BF16)
    grid_both = jnp.concatenate([grid_high, grid_low], axis=1)

    devices = got_ref.shape[0]
    full, rest, _ = slot_layout(slots)
    half = devices // 2
    for field in range(FIELDS):
        for part in range(full):
            obs_ref[field, part * devices : (part + 1) * devices, :] = got_ref[
                :, part * FIELDS + field, :
            ]
        if rest:
            tail = got_ref[:, full * FIELDS + field // 2, :]
            low, high = tail[:half], tail[half:]
            if field % 2 == 0:
                high = pltpu.roll(high, 64, 1)
            else:
                low = pltpu.roll(low, 64, 1)
            obs_ref[field, full * devices : full * devices + half, :] = jnp.where(
                iota((half, 128), 1) < 64, low, high
            )
    code = obs_ref[4].astype(jnp.int32)
    shift = chans.bit_length() - 1
    cell = lax.shift_right_logical(code, shift)
    obs_ref[4] = (code & (chans - 1)).astype(F32)
    obs_ref[0] = obs_ref[0] + lax.shift_right_logical(cell, 4).astype(F32)
    obs_ref[1] = obs_ref[1] + (cell & (cols - 1)).astype(F32)

    sum_ref[...] = jnp.zeros(sum_ref.shape, F32)
    count = obs_ref.shape[1] // (group * parts)
    row_ids = iota((rows, 128), 0, F32)
    col_ids = iota((cols, 128), 0, F32)
    level_ids = iota((chans, 128), 0, F32)

    def add_group(start):
        high, low, masks, marks = [], [], [], []
        for piece in range(group):
            mark = [obs_ref[field, pl.ds(start + piece, 1), :] for field in range(FIELDS)]
            up = jnp.maximum(0.0, 1.0 - jnp.abs(row_ids - mark[0]))
            along = jnp.maximum(0.0, 1.0 - jnp.abs(col_ids - mark[1]))
            weights = (up[:, None, :] * along[None, :, :]).reshape(cells, 128)
            weights_high = weights.astype(BF16)
            high.append(weights_high)
            low.append((weights - weights_high.astype(F32)).astype(BF16))
            masks.append(level_ids == mark[4])
            marks.append(mark)
        high = jnp.concatenate(high, axis=1)
        low = jnp.concatenate(low, axis=1)
        sampled = dot(grid_both, jnp.concatenate([high, high], axis=0)) + dot(grid_high, low)
        hot_high, hot_low = [], []
        for piece in range(group):
            mine = sampled[:, piece * 128 : (piece + 1) * 128]
            predicted = jnp.sum(jnp.where(masks[piece], mine, 0.0), axis=0, keepdims=True)
            misfit = marks[piece][3] * (predicted - marks[piece][2])
            misfit_high = misfit.astype(BF16).astype(F32)
            hot_high.append(jnp.where(masks[piece], misfit_high, 0.0).astype(BF16))
            hot_low.append(jnp.where(masks[piece], misfit - misfit_high, 0.0).astype(BF16))
        hot_high = jnp.concatenate(hot_high, axis=1)
        hot_low = jnp.concatenate(hot_low, axis=1)
        mixed = dot_nt(
            jnp.concatenate([hot_high, hot_low], axis=0), jnp.concatenate([high, low], axis=0)
        )
        return mixed[:chans, :cells] + (mixed[chans:, :cells] + mixed[:chans, cells:])

    def step(index, carry):
        total = sum_ref[...]
        for part in range(parts):
            total = total + add_group((index * parts + part) * group)
        sum_ref[...] = total
        return carry

    lax.fori_loop(0, count, step, 0)
    adjoint = sum_ref[...].T
    adj_ref[...] = adjoint
    pull_ref[...] = adjoint.astype(BF16)


def forward(slots, bands, pieces, w1, w2, got):
    rows, cols, chans = pieces[0].shape
    devices = got.shape[0]
    full, rest, _ = slot_layout(slots)
    groups = full * devices + (devices // 2 if rest else 0)
    return pl.pallas_call(
        functools.partial(forward_kernel, slots, bands, 2, 4),
        out_shape=[
            jax.ShapeDtypeStruct((rows * cols, chans), F32),
            jax.ShapeDtypeStruct((rows * cols, chans), BF16),
            jax.ShapeDtypeStruct(((rows + 2) * SPAN, chans), F32),
        ],
        in_specs=[vmem()] * 8,
        out_specs=[vmem()] * 3,
        scratch_shapes=[
            pltpu.VMEM((rows + 4, SPAN + 8, chans), F32),
            pltpu.VMEM(((rows + 4) * SPAN, chans), BF16),
            pltpu.VMEM((rows + 2, SPAN, chans), F32),
            pltpu.VMEM((FIELDS, groups, 128), F32),
            pltpu.VMEM((chans, rows * cols), F32),
        ],
        compiler_params=params(),
        cost_estimate=cost(4e9, 4e6),
        name="forward",
    )(*pieces, w1, w2, got)


def spread_matrix(steps, tiles, split):
    lons = 16 * steps
    place = iota(((steps + 2) * 16, lons), 0)
    lon = (place & 15) * steps + lax.shift_right_logical(place, 4) - 1
    lon = jnp.where(lon < 0, lon + lons, jnp.where(lon >= lons, lon - lons, lon))
    column = iota(((steps + 2) * 16, lons), 1)
    if split:
        half = tiles // 2
        chunk = lax.shift_right_logical(column, 4)
        core = lax.shift_right_logical(chunk, half.bit_length() - 1)
        column = (2 * (chunk & (half - 1)) + core) * 16 + (column & 15)
    return jnp.where(column == lon, 1.0, 0.0).astype(BF16)


def spread(line_of, start, lats, matrix, pad_ref):
    steps = pad_ref.shape[1] - 2
    for row in range(pad_ref.shape[0]):
        lat = start + row
        inside = jnp.logical_and(lat >= 0, lat < lats)
        line = line_of(jnp.clip(lat, 0, lats - 1))
        chosen = jnp.where(inside, matrix, 0.0).astype(BF16)
        pad_ref[row] = dot(chosen, line).astype(BF16).reshape(steps + 2, 16, line.shape[1])


def conv_block(pad_ref, weight_ref, start, rows, flipped):
    steps = pad_ref.shape[1] - 2
    chans = pad_ref.shape[3]
    pieces = []
    for a in range(3):
        for b in range(3):
            da, db = (2 - a, 2 - b) if flipped else (a, b)
            piece = pad_ref[pl.ds(start + da, rows), db : db + steps]
            pieces.append(piece.reshape(rows * steps * 16, chans))
    return dot(jnp.concatenate(pieces, axis=1), weight_ref[...].reshape(9 * chans, chans))


def whole_kernel(block, all_ref, w1_ref, w2_ref, slope_ref, hidden_ref, state_ref, w2t_ref, pad_ref):
    bands, tiles, rows, group, chans = all_ref.shape
    lats, lons = bands * rows, tiles * group
    steps = lons // 16
    size = block * lons
    mine = pad_ref.shape[0] - 4
    base = (lax.axis_index("lon") & 1) * mine
    spread(
        lambda lat: all_ref[lat // rows, :, lat % rows].reshape(lons, chans),
        base - 2, lats, spread_matrix(steps, tiles, False).astype(F32), pad_ref,
    )

    def step(index, carry):
        start = index * block
        first = conv_block(pad_ref, w1_ref, start, block, False)
        sig, hidden = silu_parts(first)
        at = pl.ds(pl.multiple_of(index * size, size), size)
        slope_ref[at, :] = sig * (1.0 + first * (1.0 - sig))
        lat = base - 1 + start + lax.shift_right_logical(
            iota((size, chans), 0), lons.bit_length() - 1
        )
        hidden = jnp.where(jnp.logical_and(lat >= 0, lat < lats), hidden, 0.0)
        hidden_ref[:, at] = hidden.astype(BF16).T
        centre = pad_ref[pl.ds(start + 1, block), 1 : 1 + steps].reshape(size, chans)
        state_ref[:, at] = centre.T
        return carry

    lax.fori_loop(0, (mine + 2) // block, step, 0)
    for tap in range(9):
        w2t_ref[tap] = w2_ref[tap].T


def whole(state_all, w1, w2):
    bands, tiles, rows, group, chans = state_all.shape
    lats, lons = bands * rows, tiles * group
    mine = lats // 2
    steps = lons // 16
    cells = (mine + 2) * lons
    return pl.pallas_call(
        functools.partial(whole_kernel, 3),
        out_shape=[
            jax.ShapeDtypeStruct((cells, chans), F32),
            jax.ShapeDtypeStruct((chans, cells), BF16),
            jax.ShapeDtypeStruct((chans, cells), BF16),
            jax.ShapeDtypeStruct((9, chans, chans), BF16),
        ],
        in_specs=[vmem()] * 3,
        out_specs=[vmem()] * 4,
        scratch_shapes=[pltpu.VMEM((mine + 4, steps + 2, 16, chans), BF16)],
        compiler_params=params(),
        cost_estimate=cost(6e9, 10e6),
        name="whole",
    )(state_all, w1, w2)


def tap_sums(turned_ref, pad_ref, first_row, rows, sum_ref, out_ref, sem):
    steps = pad_ref.shape[1] - 2
    chans = pad_ref.shape[3]
    lons = steps * 16

    def step(tap, carry):
        a, b = tap // 3, tap % 3
        piece = pad_ref[first_row : first_row + rows, pl.ds(2 - b, steps)]
        at = pl.ds(pl.multiple_of(a * lons, lons), rows * lons)
        sum_ref[tap] = dot(turned_ref[:, at], piece.reshape(rows * lons, chans))
        pltpu.make_async_copy(sum_ref.at[tap], out_ref.at[tap], sem.at[tap]).start()
        return carry

    lax.fori_loop(0, 9, step, 0)


def tail_kernel(block, mine_hbm, other_hbm, slope_hbm, hidden_hbm, state_hbm, w2t_ref, g1_hbm,
                g2_hbm, all_ref, pull_ref, first_ref, slope_ref, hidden_ref, state_ref, g1_ref,
                g2_ref, big_sems, g1_sems, g2_sems):
    steps = pull_ref.shape[1] - 2
    chans = pull_ref.shape[3]
    lons = steps * 16
    size = block * lons
    _, bands, half, rows, cols, _ = all_ref.shape
    lats = bands * rows
    mine = lats // 2
    core = lax.axis_index("lon") & 1
    base = core * mine
    mine_copy = pltpu.make_async_copy(mine_hbm, all_ref.at[core], big_sems.at[0])
    other_copy = pltpu.make_async_copy(other_hbm, all_ref.at[1 - core], big_sems.at[1])
    hidden_copy = pltpu.make_async_copy(hidden_hbm, hidden_ref, big_sems.at[2])
    slope_copy = pltpu.make_async_copy(
        slope_hbm.at[pl.ds(lons, mine * lons), :], slope_ref, big_sems.at[3]
    )
    state_copy = pltpu.make_async_copy(state_hbm, state_ref, big_sems.at[4])
    mine_copy.start()
    other_copy.start()
    hidden_copy.start()
    slope_copy.start()
    state_copy.start()
    matrix = spread_matrix(steps, 2 * half, True).astype(F32)
    mine_copy.wait()
    other_copy.wait()
    spread(
        lambda lat: all_ref[:, lat // rows, :, lat % rows].reshape(lons, chans),
        base - 1, lats, matrix, pull_ref,
    )
    hidden_copy.wait()
    tap_sums(hidden_ref, pull_ref, 1, mine, g2_ref, g2_hbm, g2_sems)
    slope_copy.wait()

    def step(index, carry):
        start = index * block
        back = conv_block(pull_ref, w2t_ref, start, block, True)
        at = pl.ds(pl.multiple_of(index * size, size), size)
        pull = (back * slope_ref[at, :]).astype(BF16).astype(F32)
        pull = pull.reshape(block, steps, 16, chans)
        last, head = pull[:, steps - 1], pull[:, 0]
        before = jnp.concatenate([last[:, 15:], last[:, :15]], axis=1)
        after = jnp.concatenate([head[:, 1:], head[:, :1]], axis=1)
        to = pl.ds(start, block)
        first_ref[to, 1 : 1 + steps] = pull.astype(BF16)
        first_ref[to, 0] = before.astype(BF16)
        first_ref[to, steps + 1] = after.astype(BF16)
        return carry

    lax.fori_loop(0, mine // block, step, 0)
    state_copy.wait()
    tap_sums(state_ref, first_ref, 0, mine, g1_ref, g1_hbm, g1_sems)
    for tap in range(9):
        pltpu.make_async_copy(g2_ref.at[tap], g2_hbm.at[tap], g2_sems.at[tap]).wait()
        pltpu.make_async_copy(g1_ref.at[tap], g1_hbm.at[tap], g1_sems.at[tap]).wait()


def tail(mine, other, slope, hidden, state, w2t):
    bands, half, rows, group, chans = mine.shape
    lats, lons = bands * rows, 2 * half * group
    steps = lons // 16
    ours = lats // 2
    anywhere = pl.BlockSpec(memory_space=pl.ANY)
    return pl.pallas_call(
        functools.partial(tail_kernel, 4),
        out_shape=[jax.ShapeDtypeStruct((9, chans, chans), F32)] * 2,
        in_specs=[anywhere] * 5 + [vmem()],
        out_specs=[anywhere] * 2,
        scratch_shapes=[
            pltpu.VMEM((2,) + mine.shape, BF16),
            pltpu.VMEM((ours + 2, steps + 2, 16, chans), BF16),
            pltpu.VMEM((ours, steps + 2, 16, chans), BF16),
            pltpu.VMEM((ours * lons, chans), F32),
            pltpu.VMEM(hidden.shape, BF16),
            pltpu.VMEM(state.shape, BF16),
            pltpu.VMEM((9, chans, chans), F32),
            pltpu.VMEM((9, chans, chans), F32),
            pltpu.SemaphoreType.DMA((5,)),
            pltpu.SemaphoreType.DMA((9,)),
            pltpu.SemaphoreType.DMA((9,)),
        ],
        compiler_params=params(),
        cost_estimate=cost(10e9, 15e6),
        name="tail",
    )(mine, other, slope, hidden, state, w2t)


def local_kernel(mine_hbm, other_hbm, slope_ref, adj_ref, w1_ref, w2_ref, grad_ref, near_ref,
                 line_ref, shift_ref, pull_ref, sems):
    bands, half, rows, cols, chans = mine_hbm.shape
    span = pull_ref.shape[1]
    lat, lon = lax.axis_index("lat"), lax.axis_index("lon")
    west = lax.shift_right_logical((lon + 2 * half - 1) & (2 * half - 1), 1)
    east = lax.shift_right_logical((lon + 1) & (2 * half - 1), 1)
    here = lax.shift_right_logical(lon, 1)
    copies = []
    for down in range(3):
        band = jnp.clip(lat + down - 1, 0, bands - 1)
        for over, (source, q) in enumerate(((other_hbm, west), (mine_hbm, here), (other_hbm, east))):
            copy = pltpu.make_async_copy(
                source.at[band, q], near_ref.at[down, over], sems.at[down, over]
            )
            copy.start()
            copies.append(copy)
    line_ref[:, cols + 4 :, :] = jnp.zeros(
        (rows + 4, line_ref.shape[1] - cols - 4, chans), F32
    )
    for copy in copies:
        copy.wait()
    for down, (y, height, first) in enumerate(((0, 2, rows - 2), (2, rows, 0), (2 + rows, 2, 0))):
        band = lat + down - 1
        for over, (x, width, left) in enumerate(((0, 2, cols - 2), (2, cols, 0), (2 + cols, 2, 0))):
            part = near_ref[down, over].astype(F32)[
                first : first + height, left : left + width
            ]
            if down != 1:
                part = jnp.where(jnp.logical_and(band >= 0, band < bands), part, 0.0)
            line_ref[y : y + height, x : x + width, :] = part
    back = jnp.zeros(((rows + 2) * span, chans), F32)
    for b in range(3):
        shift_ref[...] = (
            line_ref[:, 2 - b : 2 - b + span, :].astype(BF16).reshape((rows + 4) * span, chans)
        )
        for a in range(3):
            piece = shift_ref[(2 - a) * span : (2 - a) * span + (rows + 2) * span, :]
            back = back + dot_nt(piece, w2_ref[3 * a + b])
    pull = (back * slope_ref[...]).reshape(rows + 2, span, chans)
    pull_ref[...] = jnp.where(inside_grid(rows, pull.shape, bands), pull, 0.0)
    total = adj_ref[...]
    for b in range(3):
        shift_ref[0 : (rows + 2) * cols, :] = (
            pull_ref[:, 2 - b : 2 - b + cols, :].astype(BF16).reshape((rows + 2) * cols, chans)
        )
        for a in range(3):
            piece = shift_ref[(2 - a) * cols : (2 - a) * cols + rows * cols, :]
            total = total + dot_nt(piece, w1_ref[3 * a + b])
    grad_ref[...] = total


def local_grad(mine, other, slope, adjoint, w1, w2):
    bands, half, rows, cols, chans = mine.shape
    return pl.pallas_call(
        local_kernel,
        out_shape=jax.ShapeDtypeStruct((rows * cols, chans), F32),
        in_specs=[pl.BlockSpec(memory_space=pl.ANY)] * 2 + [vmem()] * 4,
        out_specs=vmem(),
        scratch_shapes=[
            pltpu.VMEM((3, 3, rows, cols, chans), BF16),
            pltpu.VMEM((rows + 4, SPAN + 8, chans), F32),
            pltpu.VMEM(((rows + 4) * SPAN, chans), BF16),
            pltpu.VMEM((rows + 2, SPAN, chans), F32),
            pltpu.SemaphoreType.DMA((3, 3)),
        ],
        compiler_params=params(),
        cost_estimate=cost(3e9, 4e6),
        name="local_grad",
    )(mine, other, slope, adjoint, w1, w2)


def with_halo(x, sides, width, wrap):
    for axis, dim in sides:
        count, length = (lax.axis_size(axis), x.shape[dim])
        up = [(i, (i + 1) % count) for i in range(count if wrap else count - 1)]
        down = [(j, i) for i, j in up]
        last = lax.slice_in_dim(x, length - width, length, axis=dim)
        first = lax.slice_in_dim(x, 0, width, axis=dim)
        before = lax.ppermute(last, axis, up)
        after = lax.ppermute(first, axis, down)
        x = jnp.concatenate([before, x, after], axis=dim)
    return x


def widen_tile(field):
    across = with_halo(field, (("lon", 1),), 1, True)
    return with_halo(across, (("lat", 0),), 1, False)


def tile_conv(padded, weight, rows, cols, flipped):
    total = jnp.zeros((rows * cols, weight.shape[2]), jnp.float32)
    for first_tap in range(3):
        for second_tap in range(3):
            if flipped:
                piece = padded[
                    2 - first_tap : 2 - first_tap + rows, 2 - second_tap : 2 - second_tap + cols
                ]
                total = total + lax.dot_general(
                    piece.reshape(rows * cols, -1),
                    weight[3 * first_tap + second_tap],
                    (((1,), (1,)), ((), ())),
                    preferred_element_type=jnp.float32,
                )
            else:
                piece = padded[first_tap : first_tap + rows, second_tap : second_tap + cols]
                total = total + jnp.dot(
                    piece.reshape(rows * cols, -1),
                    weight[3 * first_tap + second_tap],
                    preferred_element_type=jnp.float32,
                )
    return total.reshape(rows, cols, -1)


def tile_grads(padded, pullback, rows, cols):
    flat_pull = pullback.reshape(rows * cols, -1)
    result = []
    for first_tap in range(3):
        for second_tap in range(3):
            piece = padded[first_tap : first_tap + rows, second_tap : second_tap + cols].reshape(
                rows * cols, -1
            )
            result.append(
                lax.dot_general(
                    piece, flat_pull, (((0,), (0,)), ((), ())), preferred_element_type=jnp.float32
                )
            )
    return jnp.stack(result)


def route_blocks(obs_owner, obs_cell, obs_level, obs_count, obs_frac, obs_value, obs_weight):
    devices = lax.axis_size(("lat", "lon"))
    blocks, width = obs_value.shape
    slots = max(2, 3 * blocks // (2 * devices))
    owner = obs_owner[:, 0]
    order = lax.broadcasted_iota(jnp.int32, (blocks, blocks), 1) < lax.broadcasted_iota(
        jnp.int32, (blocks, blocks), 0
    )
    earlier = jnp.logical_and(owner[:, None] == owner[None, :], order)
    rank = jnp.sum(earlier.astype(jnp.int32), axis=1)
    target = owner * slots + rank
    valid = (lax.broadcasted_iota(jnp.int32, (blocks, width), 1) < obs_count[:, None]).astype(
        jnp.float32
    )
    packed = jnp.stack(
        [
            obs_frac[:, 0, :],
            obs_frac[:, 1, :],
            obs_value,
            obs_weight,
            obs_cell.astype(jnp.float32),
            obs_level.astype(jnp.float32),
            valid,
        ],
        axis=1,
    )
    outgoing = jnp.zeros((devices * slots, 7, width), jnp.float32).at[target].set(packed)
    return lax.all_to_all(outgoing, ("lat", "lon"), split_axis=0, concat_axis=0, tiled=True)


def observe(corrected, arrived, rows, cols, chans):
    fields = jnp.transpose(arrived, (1, 0, 2)).reshape(7, -1)
    row_total = fields.shape[1]
    span_rows = math.gcd(row_total, 1024)
    fields = jnp.transpose(fields.reshape(7, row_total // span_rows, span_rows), (1, 0, 2))
    grid = corrected.reshape(rows * cols, chans)
    cells = lax.broadcasted_iota(jnp.int32, (1, rows * cols), 1)
    levels = lax.broadcasted_iota(jnp.int32, (1, chans), 1)

    def advance(summed, portion):
        frac_lat = portion[0][:, None]
        frac_lon = portion[1][:, None]
        corner = portion[4].astype(jnp.int32)[:, None]
        level = portion[5].astype(jnp.int32)[:, None]
        weights = (1.0 - frac_lat) * (1.0 - frac_lon) * (cells == corner).astype(jnp.float32)
        weights = weights + (1.0 - frac_lat) * frac_lon * (cells == corner + 1).astype(jnp.float32)
        weights = weights + frac_lat * (1.0 - frac_lon) * (cells == corner + cols).astype(
            jnp.float32
        )
        weights = weights + frac_lat * frac_lon * (cells == corner + cols + 1).astype(jnp.float32)
        onehot = (levels == level).astype(jnp.float32)
        sampled = jnp.dot(
            weights, grid, precision=lax.Precision.HIGHEST, preferred_element_type=jnp.float32
        )
        predicted = jnp.sum(sampled * onehot, axis=1)
        misfit = portion[6] * portion[3] * (predicted - portion[2])
        summed = summed + lax.dot_general(
            weights,
            onehot * misfit[:, None],
            (((0,), (0,)), ((), ())),
            precision=lax.Precision.HIGHEST,
            preferred_element_type=jnp.float32,
        )
        return (summed, None)

    summed, unused = lax.scan(advance, jnp.zeros((rows * cols, chans), jnp.float32), fields)
    return summed.reshape(rows, cols, chans)


def by_tiles(
    state,
    weight_first,
    weight_second,
    obs_owner,
    obs_cell,
    obs_level,
    obs_count,
    obs_frac,
    obs_value,
    obs_weight,
):
    rows, cols, chans = state.shape
    wide_state = widen_tile(state)
    first = tile_conv(wide_state, weight_first, rows, cols, False)
    hidden = jax.nn.silu(first).astype(jnp.bfloat16)
    wide_hidden = widen_tile(hidden)
    corrected = state.astype(jnp.float32) + tile_conv(wide_hidden, weight_second, rows, cols, False)
    arrived = route_blocks(
        obs_owner, obs_cell, obs_level, obs_count, obs_frac, obs_value, obs_weight
    )
    adjoint = observe(corrected, arrived, rows, cols, chans)
    pullback = adjoint.astype(jnp.bfloat16)
    wide_pull = widen_tile(pullback)
    local_second = tile_grads(wide_hidden, pullback, rows, cols)
    back = tile_conv(wide_pull, weight_second, rows, cols, True)
    sig = jax.nn.sigmoid(first)
    pull_first = (back * sig * (1.0 + first * (1.0 - sig))).astype(jnp.bfloat16)
    wide_pull_first = widen_tile(pull_first)
    local_first = tile_grads(wide_state, pull_first, rows, cols)
    state_grad = adjoint + tile_conv(wide_pull_first, weight_first, rows, cols, True)
    grad_first, grad_second = lax.psum((local_first, local_second), ("lat", "lon"))
    return (state_grad, grad_first, grad_second)


def halo_pieces(x):
    bands, tiles = lax.axis_size("lat"), lax.axis_size("lon")
    rows, cols, _ = x.shape
    north = lax.ppermute(x[rows - 2 :], "lat", [(i, i + 1) for i in range(bands - 1)])
    south = lax.ppermute(x[:2], "lat", [(i + 1, i) for i in range(bands - 1)])
    last = jnp.concatenate([p[:, cols - 2 :] for p in (north, x, south)], axis=0)
    first = jnp.concatenate([p[:, :2] for p in (north, x, south)], axis=0)
    west = lax.ppermute(last, "lon", [(i, (i + 1) % tiles) for i in range(tiles)])
    east = lax.ppermute(first, "lon", [((i + 1) % tiles, i) for i in range(tiles)])
    return x, north, south, west, east


def gather_state(x):
    bands, tiles = lax.axis_size("lat"), lax.axis_size("lon")
    return lax.all_gather(x, ("lat", "lon")).reshape((bands, tiles) + x.shape)


def gather_tiles(x):
    bands, tiles = lax.axis_size("lat"), lax.axis_size("lon")
    half = tiles // 2
    same = [[2 * q + core for q in range(half)] for core in range(2)]
    copies = jnp.broadcast_to(x[None], (half,) + x.shape)
    line = lax.all_to_all(copies, "lon", 0, 0, axis_index_groups=same, tiled=True)
    copies = jnp.broadcast_to(line[None], (bands,) + line.shape)
    mine = lax.all_to_all(copies, "lat", 0, 0, tiled=True)
    other = lax.ppermute(mine, "lon", [(i, i ^ 1) for i in range(tiles)])
    return mine, other


def per_device(
    state, weight_first, weight_second, obs_owner, obs_cell, obs_level, obs_count, obs_frac,
    obs_value, obs_weight,
):
    rows, cols, chans = state.shape
    bands = lax.axis_size("lat")
    devices = lax.axis_size(("lat", "lon"))
    if devices * rows * cols > WHOLE_CELLS:
        return by_tiles(
            state, weight_first, weight_second, obs_owner, obs_cell, obs_level, obs_count,
            obs_frac, obs_value, obs_weight,
        )
    slots = max(2, 3 * obs_value.shape[0] // (2 * devices))
    state_all = gather_state(state)
    pieces = halo_pieces(state)
    outgoing = route(
        devices, slots, chans, obs_owner, obs_cell, obs_level, obs_count, obs_frac, obs_value,
        obs_weight,
    )
    got = lax.all_to_all(outgoing, ("lat", "lon"), split_axis=0, concat_axis=0, tiled=True)
    adjoint, pullback, near_slope = forward(
        slots, bands, pieces, weight_first, weight_second, got
    )
    mine, other = gather_tiles(pullback.reshape(rows, cols, chans))
    slope, hidden, turned, w2t = whole(state_all, weight_first, weight_second)
    sums = tail(mine, other, slope, hidden, turned, w2t)
    swap = [(i, i ^ 1) for i in range(lax.axis_size("lon"))]
    theirs = [lax.ppermute(part, "lon", swap) for part in sums]
    grad = local_grad(mine, other, near_slope, adjoint, weight_first, weight_second)
    g1, g2 = [part + their for part, their in zip(sums, theirs)]
    return grad.reshape(rows, cols, chans), g1, g2


def solution(mesh):
    both = P(("lat", "lon"), None)
    placed = (
        P("lat", "lon", None),
        P(),
        P(),
        both,
        both,
        both,
        P(("lat", "lon")),
        P(("lat", "lon"), None, None),
        both,
        both,
    )
    return jax.shard_map(
        per_device,
        mesh=mesh,
        in_specs=placed,
        out_specs=(P("lat", "lon", None), P(), P()),
        check_vma=False,
    )
```

```python
import functools
import math

import jax
import jax.numpy as jnp
from jax import lax
from jax.experimental import pallas as pl
from jax.experimental.pallas import tpu as pltpu
from jax.sharding import PartitionSpec as P

F32 = jnp.float32
BF16 = jnp.bfloat16
FIELDS = 5
SPAN = 32
WHOLE_CELLS = 4096
VMEM_LIMIT = 60 * 1024 * 1024


def params(limit=VMEM_LIMIT):
    return pltpu.CompilerParams(vmem_limit_bytes=limit)


def cost(flops, moved):
    return pl.CostEstimate(flops=int(flops), bytes_accessed=int(moved), transcendentals=0)


def vmem():
    return pl.BlockSpec(memory_space=pltpu.VMEM)


def iota(shape, dim, dtype=jnp.int32):
    return lax.broadcasted_iota(jnp.int32, shape, dim).astype(dtype)


def dot(x, y, precision=None):
    return jnp.dot(x, y, precision=precision, preferred_element_type=F32)


def dot_nt(x, y, precision=None):
    return lax.dot_general(
        x, y, (((1,), (1,)), ((), ())), precision=precision, preferred_element_type=F32
    )


def slot_layout(slots):
    full, rest = divmod(slots, 4)
    rows = full * FIELDS + (0 if rest == 0 else -(-FIELDS // 2))
    return full, rest, -(-rows // 8) * 8


def route_kernel(
    devices, slots, chans, owner_ref, count_ref, cell_ref, level_ref, frac_ref, value_ref,
    weight_ref, out_ref
):
    width, blocks = value_ref.shape
    owner = owner_ref[...].astype(F32)
    across = jnp.broadcast_to(owner, (blocks, blocks))
    down = across.T
    earlier = iota((blocks, blocks), 0) < iota((blocks, blocks), 1)
    hits = jnp.where(jnp.logical_and(across == down, earlier), 1.0, 0.0)
    rank = jnp.sum(hits, axis=0, keepdims=True)
    target = rank * float(devices) + owner
    places = iota((slots * devices, blocks), 0, F32) == target
    onehot = jnp.where(places, 1.0, 0.0)
    valid = iota((width, blocks), 0) < count_ref[...]
    fields = jnp.concatenate(
        [
            frac_ref[0],
            frac_ref[1],
            value_ref[...],
            jnp.where(valid, weight_ref[...], 0.0),
            (cell_ref[...] * chans + level_ref[...]).astype(F32),
        ],
        axis=0,
    )
    placed = dot_nt(onehot, fields, lax.Precision.HIGHEST)
    full, rest, rows = slot_layout(slots)
    out_ref[...] = jnp.zeros(out_ref.shape, F32)
    for slot in range(slots):
        for field in range(FIELDS):
            piece = placed[
                slot * devices : (slot + 1) * devices, field * width : (field + 1) * width
            ]
            if slot < 4 * full:
                row, lane = (slot // 4) * FIELDS + field, (slot % 4) * width
            else:
                row = full * FIELDS + field // 2
                lane = (field % 2) * 2 * width + (slot - 4 * full) * width
            out_ref[:, row, lane : lane + width] = piece


def route(devices, slots, chans, obs_owner, obs_cell, obs_level, obs_count, obs_frac, obs_value,
          obs_weight):
    blocks = obs_value.shape[0]
    rows = slot_layout(slots)[2]
    return pl.pallas_call(
        functools.partial(route_kernel, devices, slots, chans),
        out_shape=jax.ShapeDtypeStruct((devices, rows, 128), F32),
        in_specs=[vmem()] * 7,
        out_specs=vmem(),
        compiler_params=params(),
        name="route",
    )(
        obs_owner.reshape(1, blocks),
        obs_count.reshape(1, blocks),
        obs_cell.T,
        obs_level.T,
        jnp.transpose(obs_frac, (1, 2, 0)),
        obs_value.T,
        obs_weight.T,
    )


def silu_parts(first):
    sig = 1.0 / (1.0 + jnp.exp(-first))
    return sig, first * sig


def inside_grid(rows, shape, bands):
    lat = lax.axis_index("lat") * rows + iota(shape, 0) - 1
    return jnp.logical_and(lat >= 0, lat < bands * rows)


def forward_kernel(slots, bands, group, parts, tile_ref, north_ref, south_ref, west_ref, east_ref,
                   w1_ref, w2_ref, got_ref, adj_ref, pull_ref, slope_ref, line_ref, shift_ref,
                   hid_ref, obs_ref, sum_ref):
    rows, cols, chans = tile_ref.shape
    span = hid_ref.shape[1]
    line_ref[0:2, 2 : 2 + cols, :] = north_ref[...].astype(F32)
    line_ref[2 : 2 + rows, 2 : 2 + cols, :] = tile_ref[...].astype(F32)
    line_ref[2 + rows :, 2 : 2 + cols, :] = south_ref[...].astype(F32)
    line_ref[:, 0:2, :] = west_ref[...].astype(F32)
    line_ref[:, 2 + cols : 4 + cols, :] = east_ref[...].astype(F32)
    line_ref[:, cols + 4 :, :] = jnp.zeros(
        (rows + 4, line_ref.shape[1] - cols - 4, chans), F32
    )
    first = jnp.zeros(((rows + 2) * span, chans), F32)
    for b in range(3):
        shift_ref[...] = (
            line_ref[:, b : b + span, :].astype(BF16).reshape((rows + 4) * span, chans)
        )
        for a in range(3):
            first = first + dot(
                shift_ref[a * span : a * span + (rows + 2) * span, :], w1_ref[3 * a + b]
            )
    sig, hidden = silu_parts(first)
    slope_ref[...] = sig * (1.0 + first * (1.0 - sig))
    hidden = hidden.astype(BF16).astype(F32).reshape(rows + 2, span, chans)
    hidden = jnp.where(inside_grid(rows, hidden.shape, bands), hidden, 0.0)
    hid_ref[...] = hidden
    total = line_ref[2 : 2 + rows, 2 : 2 + cols, :].reshape(rows * cols, chans)
    for b in range(3):
        shift_ref[0 : (rows + 2) * cols, :] = (
            hid_ref[:, b : b + cols, :].astype(BF16).reshape((rows + 2) * cols, chans)
        )
        for a in range(3):
            total = total + dot(
                shift_ref[a * cols : a * cols + rows * cols, :], w2_ref[3 * a + b]
            )
    cells = rows * cols
    turned = total.T
    grid_high = turned.astype(BF16)
    grid_low = (turned - grid_high.astype(F32)).astype(BF16)
    grid_both = jnp.concatenate([grid_high, grid_low], axis=1)

    devices = got_ref.shape[0]
    full, rest, _ = slot_layout(slots)
    half = devices // 2
    for field in range(FIELDS):
        for part in range(full):
            obs_ref[field, part * devices : (part + 1) * devices, :] = got_ref[
                :, part * FIELDS + field, :
            ]
        if rest:
            tail = got_ref[:, full * FIELDS + field // 2, :]
            low, high = tail[:half], tail[half:]
            if field % 2 == 0:
                high = pltpu.roll(high, 64, 1)
            else:
                low = pltpu.roll(low, 64, 1)
            obs_ref[field, full * devices : full * devices + half, :] = jnp.where(
                iota((half, 128), 1) < 64, low, high
            )
    code = obs_ref[4].astype(jnp.int32)
    shift = chans.bit_length() - 1
    cell = lax.shift_right_logical(code, shift)
    obs_ref[4] = (code & (chans - 1)).astype(F32)
    obs_ref[0] = obs_ref[0] + lax.shift_right_logical(cell, 4).astype(F32)
    obs_ref[1] = obs_ref[1] + (cell & (cols - 1)).astype(F32)

    sum_ref[...] = jnp.zeros(sum_ref.shape, F32)
    count = obs_ref.shape[1] // (group * parts)
    row_ids = iota((rows, 128), 0, F32)
    col_ids = iota((cols, 128), 0, F32)
    level_ids = iota((chans, 128), 0, F32)

    def add_group(start):
        high, low, masks, marks = [], [], [], []
        for piece in range(group):
            mark = [obs_ref[field, pl.ds(start + piece, 1), :] for field in range(FIELDS)]
            up = jnp.maximum(0.0, 1.0 - jnp.abs(row_ids - mark[0]))
            along = jnp.maximum(0.0, 1.0 - jnp.abs(col_ids - mark[1]))
            weights = (up[:, None, :] * along[None, :, :]).reshape(cells, 128)
            weights_high = weights.astype(BF16)
            high.append(weights_high)
            low.append((weights - weights_high.astype(F32)).astype(BF16))
            masks.append(level_ids == mark[4])
            marks.append(mark)
        high = jnp.concatenate(high, axis=1)
        low = jnp.concatenate(low, axis=1)
        sampled = dot(grid_both, jnp.concatenate([high, high], axis=0)) + dot(grid_high, low)
        hot_high, hot_low = [], []
        for piece in range(group):
            mine = sampled[:, piece * 128 : (piece + 1) * 128]
            predicted = jnp.sum(jnp.where(masks[piece], mine, 0.0), axis=0, keepdims=True)
            misfit = marks[piece][3] * (predicted - marks[piece][2])
            misfit_high = misfit.astype(BF16).astype(F32)
            hot_high.append(jnp.where(masks[piece], misfit_high, 0.0).astype(BF16))
            hot_low.append(jnp.where(masks[piece], misfit - misfit_high, 0.0).astype(BF16))
        hot_high = jnp.concatenate(hot_high, axis=1)
        hot_low = jnp.concatenate(hot_low, axis=1)
        mixed = dot_nt(
            jnp.concatenate([hot_high, hot_low], axis=0), jnp.concatenate([high, low], axis=0)
        )
        return mixed[:chans, :cells] + (mixed[chans:, :cells] + mixed[:chans, cells:])

    def step(index, carry):
        total = sum_ref[...]
        for part in range(parts):
            total = total + add_group((index * parts + part) * group)
        sum_ref[...] = total
        return carry

    lax.fori_loop(0, count, step, 0)
    adjoint = sum_ref[...].T
    adj_ref[...] = adjoint
    pull_ref[...] = adjoint.astype(BF16)


def forward(slots, bands, pieces, w1, w2, got):
    rows, cols, chans = pieces[0].shape
    devices = got.shape[0]
    full, rest, _ = slot_layout(slots)
    groups = full * devices + (devices // 2 if rest else 0)
    return pl.pallas_call(
        functools.partial(forward_kernel, slots, bands, 2, 4),
        out_shape=[
            jax.ShapeDtypeStruct((rows * cols, chans), F32),
            jax.ShapeDtypeStruct((rows * cols, chans), BF16),
            jax.ShapeDtypeStruct(((rows + 2) * SPAN, chans), F32),
        ],
        in_specs=[vmem()] * 8,
        out_specs=[vmem()] * 3,
        scratch_shapes=[
            pltpu.VMEM((rows + 4, SPAN + 8, chans), F32),
            pltpu.VMEM(((rows + 4) * SPAN, chans), BF16),
            pltpu.VMEM((rows + 2, SPAN, chans), F32),
            pltpu.VMEM((FIELDS, groups, 128), F32),
            pltpu.VMEM((chans, rows * cols), F32),
        ],
        compiler_params=params(),
        cost_estimate=cost(4e9, 4e6),
        name="forward",
    )(*pieces, w1, w2, got)


def spread_matrix(steps, tiles):
    lons = 16 * steps
    half = tiles // 2
    place = iota(((steps + 2) * 16, lons), 0)
    lon = (place & 15) * steps + lax.shift_right_logical(place, 4) - 1
    lon = jnp.where(lon < 0, lon + lons, jnp.where(lon >= lons, lon - lons, lon))
    column = iota(((steps + 2) * 16, lons), 1)
    chunk = lax.shift_right_logical(column, 4)
    core = lax.shift_right_logical(chunk, half.bit_length() - 1)
    column = (2 * (chunk & (half - 1)) + core) * 16 + (column & 15)
    return jnp.where(column == lon, 1.0, 0.0)


def spread(line_of, start, lats, matrix, pad_ref):
    steps = pad_ref.shape[1] - 2
    for row in range(pad_ref.shape[0]):
        lat = start + row
        inside = jnp.logical_and(lat >= 0, lat < lats)
        line = line_of(jnp.clip(lat, 0, lats - 1))
        chosen = jnp.where(inside, matrix, 0.0).astype(BF16)
        pad_ref[row] = dot(chosen, line).astype(BF16).reshape(steps + 2, 16, line.shape[1])


def conv_block(pad_ref, weight_ref, start, rows, flipped):
    steps = pad_ref.shape[1] - 2
    chans = pad_ref.shape[3]
    pieces = []
    for a in range(3):
        for b in range(3):
            da, db = (2 - a, 2 - b) if flipped else (a, b)
            piece = pad_ref[pl.ds(start + da, rows), db : db + steps]
            pieces.append(piece.reshape(rows * steps * 16, chans))
    return dot(jnp.concatenate(pieces, axis=1), weight_ref[...].reshape(9 * chans, chans))


def whole_kernel(block, mine_hbm, other_hbm, w1_ref, w2_ref, slope_ref, hidden_ref, state_ref,
                 w2t_ref, pad_ref, all_ref, sems):
    _, bands, half, rows, group, chans = all_ref.shape
    lats, lons = bands * rows, 2 * half * group
    steps = lons // 16
    size = block * lons
    mine = pad_ref.shape[0] - 4
    core = lax.axis_index("lon") & 1
    base = core * mine
    mine_copy = pltpu.make_async_copy(mine_hbm, all_ref.at[core], sems.at[0])
    other_copy = pltpu.make_async_copy(other_hbm, all_ref.at[1 - core], sems.at[1])
    mine_copy.start()
    other_copy.start()
    matrix = spread_matrix(steps, 2 * half)
    for tap in range(9):
        w2t_ref[tap] = w2_ref[tap].T
    mine_copy.wait()
    other_copy.wait()
    spread(
        lambda lat: all_ref[:, lat // rows, :, lat % rows].reshape(lons, chans),
        base - 2, lats, matrix, pad_ref,
    )

    def step(index, carry):
        start = index * block
        first = conv_block(pad_ref, w1_ref, start, block, False)
        sig, hidden = silu_parts(first)
        at = pl.ds(pl.multiple_of(index * size, size), size)
        slope_ref[at, :] = sig * (1.0 + first * (1.0 - sig))
        lat = base - 1 + start + lax.shift_right_logical(
            iota((size, chans), 0), lons.bit_length() - 1
        )
        hidden = jnp.where(jnp.logical_and(lat >= 0, lat < lats), hidden, 0.0)
        hidden_ref[:, at] = hidden.astype(BF16).T
        centre = pad_ref[pl.ds(start + 1, block), 1 : 1 + steps].reshape(size, chans)
        state_ref[:, at] = centre.T
        return carry

    lax.fori_loop(0, (mine + 2) // block, step, 0)


def whole(state_mine, state_other, w1, w2):
    bands, half, rows, group, chans = state_mine.shape
    lats, lons = bands * rows, 2 * half * group
    mine = lats // 2
    steps = lons // 16
    cells = (mine + 2) * lons
    return pl.pallas_call(
        functools.partial(whole_kernel, 3),
        out_shape=[
            jax.ShapeDtypeStruct((cells, chans), F32),
            jax.ShapeDtypeStruct((chans, cells), BF16),
            jax.ShapeDtypeStruct((chans, cells), BF16),
            jax.ShapeDtypeStruct((9, chans, chans), BF16),
        ],
        in_specs=[pl.BlockSpec(memory_space=pl.ANY)] * 2 + [vmem()] * 2,
        out_specs=[vmem()] * 4,
        scratch_shapes=[
            pltpu.VMEM((mine + 4, steps + 2, 16, chans), BF16),
            pltpu.VMEM((2,) + state_mine.shape, BF16),
            pltpu.SemaphoreType.DMA((2,)),
        ],
        compiler_params=params(),
        cost_estimate=cost(6e9, 10e6),
        name="whole",
    )(state_mine, state_other, w1, w2)


def tap_sums(turned_ref, pad_ref, first_row, rows, sum_ref, out_ref, sem):
    steps = pad_ref.shape[1] - 2
    chans = pad_ref.shape[3]
    lons = steps * 16

    def step(tap, carry):
        a, b = tap // 3, tap % 3
        piece = pad_ref[first_row : first_row + rows, pl.ds(2 - b, steps)]
        at = pl.ds(pl.multiple_of(a * lons, lons), rows * lons)
        sum_ref[tap] = dot(turned_ref[:, at], piece.reshape(rows * lons, chans))
        pltpu.make_async_copy(sum_ref.at[tap], out_ref.at[tap], sem.at[tap]).start()
        return carry

    lax.fori_loop(0, 9, step, 0)


def tail_kernel(block, mine_hbm, other_hbm, slope_hbm, hidden_hbm, state_hbm, w2t_ref, g1_hbm,
                g2_hbm, all_ref, pull_ref, first_ref, slope_ref, hidden_ref, state_ref, g1_ref,
                g2_ref, big_sems, g1_sems, g2_sems):
    steps = pull_ref.shape[1] - 2
    chans = pull_ref.shape[3]
    lons = steps * 16
    size = block * lons
    _, bands, half, rows, cols, _ = all_ref.shape
    lats = bands * rows
    mine = lats // 2
    core = lax.axis_index("lon") & 1
    base = core * mine
    mine_copy = pltpu.make_async_copy(mine_hbm, all_ref.at[core], big_sems.at[0])
    other_copy = pltpu.make_async_copy(other_hbm, all_ref.at[1 - core], big_sems.at[1])
    hidden_copy = pltpu.make_async_copy(hidden_hbm, hidden_ref, big_sems.at[2])
    slope_copy = pltpu.make_async_copy(
        slope_hbm.at[pl.ds(lons, mine * lons), :], slope_ref, big_sems.at[3]
    )
    state_copy = pltpu.make_async_copy(state_hbm, state_ref, big_sems.at[4])
    mine_copy.start()
    other_copy.start()
    hidden_copy.start()
    slope_copy.start()
    state_copy.start()
    matrix = spread_matrix(steps, 2 * half)
    mine_copy.wait()
    other_copy.wait()
    spread(
        lambda lat: all_ref[:, lat // rows, :, lat % rows].reshape(lons, chans),
        base - 1, lats, matrix, pull_ref,
    )
    hidden_copy.wait()
    tap_sums(hidden_ref, pull_ref, 1, mine, g2_ref, g2_hbm, g2_sems)
    slope_copy.wait()

    def step(index, carry):
        start = index * block
        back = conv_block(pull_ref, w2t_ref, start, block, True)
        at = pl.ds(pl.multiple_of(index * size, size), size)
        pull = (back * slope_ref[at, :]).astype(BF16).astype(F32)
        pull = pull.reshape(block, steps, 16, chans)
        last, head = pull[:, steps - 1], pull[:, 0]
        before = jnp.concatenate([last[:, 15:], last[:, :15]], axis=1)
        after = jnp.concatenate([head[:, 1:], head[:, :1]], axis=1)
        to = pl.ds(start, block)
        first_ref[to, 1 : 1 + steps] = pull.astype(BF16)
        first_ref[to, 0] = before.astype(BF16)
        first_ref[to, steps + 1] = after.astype(BF16)
        return carry

    lax.fori_loop(0, mine // block, step, 0)
    state_copy.wait()
    tap_sums(state_ref, first_ref, 0, mine, g1_ref, g1_hbm, g1_sems)
    for tap in range(9):
        pltpu.make_async_copy(g2_ref.at[tap], g2_hbm.at[tap], g2_sems.at[tap]).wait()
        pltpu.make_async_copy(g1_ref.at[tap], g1_hbm.at[tap], g1_sems.at[tap]).wait()


def tail(mine, other, slope, hidden, state, w2t):
    bands, half, rows, group, chans = mine.shape
    lats, lons = bands * rows, 2 * half * group
    steps = lons // 16
    ours = lats // 2
    anywhere = pl.BlockSpec(memory_space=pl.ANY)
    return pl.pallas_call(
        functools.partial(tail_kernel, 4),
        out_shape=[jax.ShapeDtypeStruct((9, chans, chans), F32)] * 2,
        in_specs=[anywhere] * 5 + [vmem()],
        out_specs=[anywhere] * 2,
        scratch_shapes=[
            pltpu.VMEM((2,) + mine.shape, BF16),
            pltpu.VMEM((ours + 2, steps + 2, 16, chans), BF16),
            pltpu.VMEM((ours, steps + 2, 16, chans), BF16),
            pltpu.VMEM((ours * lons, chans), F32),
            pltpu.VMEM(hidden.shape, BF16),
            pltpu.VMEM(state.shape, BF16),
            pltpu.VMEM((9, chans, chans), F32),
            pltpu.VMEM((9, chans, chans), F32),
            pltpu.SemaphoreType.DMA((5,)),
            pltpu.SemaphoreType.DMA((9,)),
            pltpu.SemaphoreType.DMA((9,)),
        ],
        compiler_params=params(),
        cost_estimate=cost(10e9, 15e6),
        name="tail",
    )(mine, other, slope, hidden, state, w2t)


def local_kernel(mine_hbm, other_hbm, slope_ref, adj_ref, w1_ref, w2_ref, grad_ref, near_ref,
                 line_ref, shift_ref, pull_ref, sems):
    bands, half, rows, cols, chans = mine_hbm.shape
    span = pull_ref.shape[1]
    lat, lon = lax.axis_index("lat"), lax.axis_index("lon")
    west = lax.shift_right_logical((lon + 2 * half - 1) & (2 * half - 1), 1)
    east = lax.shift_right_logical((lon + 1) & (2 * half - 1), 1)
    here = lax.shift_right_logical(lon, 1)
    copies = []
    for down in range(3):
        band = jnp.clip(lat + down - 1, 0, bands - 1)
        for over, (source, q) in enumerate(((other_hbm, west), (mine_hbm, here), (other_hbm, east))):
            copy = pltpu.make_async_copy(
                source.at[band, q], near_ref.at[down, over], sems.at[down, over]
            )
            copy.start()
            copies.append(copy)
    line_ref[:, cols + 4 :, :] = jnp.zeros(
        (rows + 4, line_ref.shape[1] - cols - 4, chans), F32
    )
    for copy in copies:
        copy.wait()
    for down, (y, height, first) in enumerate(((0, 2, rows - 2), (2, rows, 0), (2 + rows, 2, 0))):
        band = lat + down - 1
        for over, (x, width, left) in enumerate(((0, 2, cols - 2), (2, cols, 0), (2 + cols, 2, 0))):
            part = near_ref[down, over].astype(F32)[
                first : first + height, left : left + width
            ]
            if down != 1:
                part = jnp.where(jnp.logical_and(band >= 0, band < bands), part, 0.0)
            line_ref[y : y + height, x : x + width, :] = part
    back = jnp.zeros(((rows + 2) * span, chans), F32)
    for b in range(3):
        shift_ref[...] = (
            line_ref[:, 2 - b : 2 - b + span, :].astype(BF16).reshape((rows + 4) * span, chans)
        )
        for a in range(3):
            piece = shift_ref[(2 - a) * span : (2 - a) * span + (rows + 2) * span, :]
            back = back + dot_nt(piece, w2_ref[3 * a + b])
    pull = (back * slope_ref[...]).reshape(rows + 2, span, chans)
    pull_ref[...] = jnp.where(inside_grid(rows, pull.shape, bands), pull, 0.0)
    total = adj_ref[...]
    for b in range(3):
        shift_ref[0 : (rows + 2) * cols, :] = (
            pull_ref[:, 2 - b : 2 - b + cols, :].astype(BF16).reshape((rows + 2) * cols, chans)
        )
        for a in range(3):
            piece = shift_ref[(2 - a) * cols : (2 - a) * cols + rows * cols, :]
            total = total + dot_nt(piece, w1_ref[3 * a + b])
    grad_ref[...] = total


def local_grad(mine, other, slope, adjoint, w1, w2):
    bands, half, rows, cols, chans = mine.shape
    return pl.pallas_call(
        local_kernel,
        out_shape=jax.ShapeDtypeStruct((rows * cols, chans), F32),
        in_specs=[pl.BlockSpec(memory_space=pl.ANY)] * 2 + [vmem()] * 4,
        out_specs=vmem(),
        scratch_shapes=[
            pltpu.VMEM((3, 3, rows, cols, chans), BF16),
            pltpu.VMEM((rows + 4, SPAN + 8, chans), F32),
            pltpu.VMEM(((rows + 4) * SPAN, chans), BF16),
            pltpu.VMEM((rows + 2, SPAN, chans), F32),
            pltpu.SemaphoreType.DMA((3, 3)),
        ],
        compiler_params=params(),
        cost_estimate=cost(3e9, 4e6),
        name="local_grad",
    )(mine, other, slope, adjoint, w1, w2)


def add_kernel(a1_ref, a2_ref, b1_ref, b2_ref, o1_ref, o2_ref):
    o1_ref[...] = a1_ref[...] + b1_ref[...]
    o2_ref[...] = a2_ref[...] + b2_ref[...]


def add_pairs(ours, theirs):
    shape = ours[0].shape
    block = pl.BlockSpec((1,) + shape[1:], lambda tap: (tap, 0, 0))
    return pl.pallas_call(
        add_kernel,
        grid=(shape[0],),
        out_shape=[jax.ShapeDtypeStruct(shape, F32)] * 2,
        in_specs=[block] * 4,
        out_specs=[block] * 2,
        compiler_params=params(),
        name="add_pairs",
    )(*ours, *theirs)


def with_halo(x, sides, width, wrap):
    for axis, dim in sides:
        count, length = (lax.axis_size(axis), x.shape[dim])
        up = [(i, (i + 1) % count) for i in range(count if wrap else count - 1)]
        down = [(j, i) for i, j in up]
        last = lax.slice_in_dim(x, length - width, length, axis=dim)
        first = lax.slice_in_dim(x, 0, width, axis=dim)
        before = lax.ppermute(last, axis, up)
        after = lax.ppermute(first, axis, down)
        x = jnp.concatenate([before, x, after], axis=dim)
    return x


def widen_tile(field):
    across = with_halo(field, (("lon", 1),), 1, True)
    return with_halo(across, (("lat", 0),), 1, False)


def tile_conv(padded, weight, rows, cols, flipped):
    total = jnp.zeros((rows * cols, weight.shape[2]), jnp.float32)
    for first_tap in range(3):
        for second_tap in range(3):
            if flipped:
                piece = padded[
                    2 - first_tap : 2 - first_tap + rows, 2 - second_tap : 2 - second_tap + cols
                ]
                total = total + lax.dot_general(
                    piece.reshape(rows * cols, -1),
                    weight[3 * first_tap + second_tap],
                    (((1,), (1,)), ((), ())),
                    preferred_element_type=jnp.float32,
                )
            else:
                piece = padded[first_tap : first_tap + rows, second_tap : second_tap + cols]
                total = total + jnp.dot(
                    piece.reshape(rows * cols, -1),
                    weight[3 * first_tap + second_tap],
                    preferred_element_type=jnp.float32,
                )
    return total.reshape(rows, cols, -1)


def tile_grads(padded, pullback, rows, cols):
    flat_pull = pullback.reshape(rows * cols, -1)
    result = []
    for first_tap in range(3):
        for second_tap in range(3):
            piece = padded[first_tap : first_tap + rows, second_tap : second_tap + cols].reshape(
                rows * cols, -1
            )
            result.append(
                lax.dot_general(
                    piece, flat_pull, (((0,), (0,)), ((), ())), preferred_element_type=jnp.float32
                )
            )
    return jnp.stack(result)


def route_blocks(obs_owner, obs_cell, obs_level, obs_count, obs_frac, obs_value, obs_weight):
    devices = lax.axis_size(("lat", "lon"))
    blocks, width = obs_value.shape
    slots = max(2, 3 * blocks // (2 * devices))
    owner = obs_owner[:, 0]
    order = lax.broadcasted_iota(jnp.int32, (blocks, blocks), 1) < lax.broadcasted_iota(
        jnp.int32, (blocks, blocks), 0
    )
    earlier = jnp.logical_and(owner[:, None] == owner[None, :], order)
    rank = jnp.sum(earlier.astype(jnp.int32), axis=1)
    target = owner * slots + rank
    valid = (lax.broadcasted_iota(jnp.int32, (blocks, width), 1) < obs_count[:, None]).astype(
        jnp.float32
    )
    packed = jnp.stack(
        [
            obs_frac[:, 0, :],
            obs_frac[:, 1, :],
            obs_value,
            obs_weight,
            obs_cell.astype(jnp.float32),
            obs_level.astype(jnp.float32),
            valid,
        ],
        axis=1,
    )
    outgoing = jnp.zeros((devices * slots, 7, width), jnp.float32).at[target].set(packed)
    return lax.all_to_all(outgoing, ("lat", "lon"), split_axis=0, concat_axis=0, tiled=True)


def observe(corrected, arrived, rows, cols, chans):
    fields = jnp.transpose(arrived, (1, 0, 2)).reshape(7, -1)
    row_total = fields.shape[1]
    span_rows = math.gcd(row_total, 1024)
    fields = jnp.transpose(fields.reshape(7, row_total // span_rows, span_rows), (1, 0, 2))
    grid = corrected.reshape(rows * cols, chans)
    cells = lax.broadcasted_iota(jnp.int32, (1, rows * cols), 1)
    levels = lax.broadcasted_iota(jnp.int32, (1, chans), 1)

    def advance(summed, portion):
        frac_lat = portion[0][:, None]
        frac_lon = portion[1][:, None]
        corner = portion[4].astype(jnp.int32)[:, None]
        level = portion[5].astype(jnp.int32)[:, None]
        weights = (1.0 - frac_lat) * (1.0 - frac_lon) * (cells == corner).astype(jnp.float32)
        weights = weights + (1.0 - frac_lat) * frac_lon * (cells == corner + 1).astype(jnp.float32)
        weights = weights + frac_lat * (1.0 - frac_lon) * (cells == corner + cols).astype(
            jnp.float32
        )
        weights = weights + frac_lat * frac_lon * (cells == corner + cols + 1).astype(jnp.float32)
        onehot = (levels == level).astype(jnp.float32)
        sampled = jnp.dot(
            weights, grid, precision=lax.Precision.HIGHEST, preferred_element_type=jnp.float32
        )
        predicted = jnp.sum(sampled * onehot, axis=1)
        misfit = portion[6] * portion[3] * (predicted - portion[2])
        summed = summed + lax.dot_general(
            weights,
            onehot * misfit[:, None],
            (((0,), (0,)), ((), ())),
            precision=lax.Precision.HIGHEST,
            preferred_element_type=jnp.float32,
        )
        return (summed, None)

    summed, unused = lax.scan(advance, jnp.zeros((rows * cols, chans), jnp.float32), fields)
    return summed.reshape(rows, cols, chans)


def by_tiles(
    state,
    weight_first,
    weight_second,
    obs_owner,
    obs_cell,
    obs_level,
    obs_count,
    obs_frac,
    obs_value,
    obs_weight,
):
    rows, cols, chans = state.shape
    wide_state = widen_tile(state)
    first = tile_conv(wide_state, weight_first, rows, cols, False)
    hidden = jax.nn.silu(first).astype(jnp.bfloat16)
    wide_hidden = widen_tile(hidden)
    corrected = state.astype(jnp.float32) + tile_conv(wide_hidden, weight_second, rows, cols, False)
    arrived = route_blocks(
        obs_owner, obs_cell, obs_level, obs_count, obs_frac, obs_value, obs_weight
    )
    adjoint = observe(corrected, arrived, rows, cols, chans)
    pullback = adjoint.astype(jnp.bfloat16)
    wide_pull = widen_tile(pullback)
    local_second = tile_grads(wide_hidden, pullback, rows, cols)
    back = tile_conv(wide_pull, weight_second, rows, cols, True)
    sig = jax.nn.sigmoid(first)
    pull_first = (back * sig * (1.0 + first * (1.0 - sig))).astype(jnp.bfloat16)
    wide_pull_first = widen_tile(pull_first)
    local_first = tile_grads(wide_state, pull_first, rows, cols)
    state_grad = adjoint + tile_conv(wide_pull_first, weight_first, rows, cols, True)
    grad_first, grad_second = lax.psum((local_first, local_second), ("lat", "lon"))
    return (state_grad, grad_first, grad_second)


def halo_pieces(x, after):
    bands, tiles = lax.axis_size("lat"), lax.axis_size("lon")
    rows, cols, _ = x.shape
    north = lax.ppermute(x[rows - 2 :], "lat", [(i, i + 1) for i in range(bands - 1)])
    south = lax.ppermute(x[:2], "lat", [(i + 1, i) for i in range(bands - 1)])
    last = jnp.concatenate([p[:, cols - 2 :] for p in (north, x, south)], axis=0)
    first = jnp.concatenate([p[:, :2] for p in (north, x, south)], axis=0)
    last, first, after = lax.optimization_barrier((last, first, after))
    west = lax.ppermute(last, "lon", [(i, (i + 1) % tiles) for i in range(tiles)])
    east = lax.ppermute(first, "lon", [((i + 1) % tiles, i) for i in range(tiles)])
    return (x, north, south, west, east), after


def gather_tiles(x):
    bands, tiles = lax.axis_size("lat"), lax.axis_size("lon")
    same = [[device for device in range(bands * tiles) if device % 2 == core] for core in range(2)]
    mine = lax.all_gather(x, ("lat", "lon"), axis_index_groups=same)
    mine = mine.reshape((bands, tiles // 2) + x.shape)
    other = lax.ppermute(mine, "lon", [(i, i ^ 1) for i in range(tiles)])
    return mine, other


def per_device(
    state, weight_first, weight_second, obs_owner, obs_cell, obs_level, obs_count, obs_frac,
    obs_value, obs_weight,
):
    rows, cols, chans = state.shape
    bands = lax.axis_size("lat")
    devices = lax.axis_size(("lat", "lon"))
    if devices * rows * cols > WHOLE_CELLS:
        return by_tiles(
            state, weight_first, weight_second, obs_owner, obs_cell, obs_level, obs_count,
            obs_frac, obs_value, obs_weight,
        )
    slots = max(2, 3 * obs_value.shape[0] // (2 * devices))
    state_mine, state_other = gather_tiles(state)
    outgoing = route(
        devices, slots, chans, obs_owner, obs_cell, obs_level, obs_count, obs_frac, obs_value,
        obs_weight,
    )
    pieces, outgoing = halo_pieces(state, outgoing)
    got = lax.all_to_all(outgoing, ("lat", "lon"), split_axis=0, concat_axis=0, tiled=True)
    adjoint, pullback, near_slope = forward(
        slots, bands, pieces, weight_first, weight_second, got
    )
    mine, other = gather_tiles(pullback.reshape(rows, cols, chans))
    slope, hidden, turned, w2t = whole(
        state_mine, state_other, weight_first, weight_second
    )
    sums = tail(mine, other, slope, hidden, turned, w2t)
    swap = [(i, i ^ 1) for i in range(lax.axis_size("lon"))]
    theirs = [lax.ppermute(part, "lon", swap) for part in sums]
    grad = local_grad(mine, other, near_slope, adjoint, weight_first, weight_second)
    g1, g2 = add_pairs(sums, theirs)
    return grad.reshape(rows, cols, chans), g1, g2


def solution(mesh):
    both = P(("lat", "lon"), None)
    placed = (
        P("lat", "lon", None),
        P(),
        P(),
        both,
        both,
        both,
        P(("lat", "lon")),
        P(("lat", "lon"), None, None),
        both,
        both,
    )
    return jax.shard_map(
        per_device,
        mesh=mesh,
        in_specs=placed,
        out_specs=(P("lat", "lon", None), P(), P()),
        check_vma=False,
    )
```

```python
import functools
import math

import jax
import jax.numpy as jnp
from jax import lax
from jax.experimental import pallas as pl
from jax.experimental.pallas import tpu as pltpu
from jax.sharding import PartitionSpec as P

F32 = jnp.float32
BF16 = jnp.bfloat16
FIELDS = 5
SPAN = 32
WHOLE_CELLS = 4096


def params(mebibytes):
    return pltpu.CompilerParams(vmem_limit_bytes=mebibytes * 1024 * 1024)


def cost(flops, moved):
    return pl.CostEstimate(flops=int(flops), bytes_accessed=int(moved), transcendentals=0)


def vmem():
    return pl.BlockSpec(memory_space=pltpu.VMEM)


def anywhere():
    return pl.BlockSpec(memory_space=pl.ANY)


def iota(shape, dim, dtype=jnp.int32):
    return lax.broadcasted_iota(jnp.int32, shape, dim).astype(dtype)


def dot(x, y, precision=None):
    return jnp.dot(x, y, precision=precision, preferred_element_type=F32)


def dot_nt(x, y, precision=None):
    return lax.dot_general(
        x, y, (((1,), (1,)), ((), ())), precision=precision, preferred_element_type=F32
    )


def slot_layout(slots):
    full, rest = divmod(slots, 4)
    rows = full * FIELDS + (0 if rest == 0 else -(-FIELDS // 2))
    return full, rest, -(-rows // 8) * 8


def route_kernel(
    devices, slots, chans, owner_ref, count_ref, cell_ref, level_ref, frac_ref, value_ref,
    weight_ref, out_ref
):
    width, blocks = value_ref.shape
    owner = owner_ref[...].astype(F32)
    across = jnp.broadcast_to(owner, (blocks, blocks))
    down = across.T
    earlier = iota((blocks, blocks), 0) < iota((blocks, blocks), 1)
    hits = jnp.where(jnp.logical_and(across == down, earlier), 1.0, 0.0)
    rank = jnp.sum(hits, axis=0, keepdims=True)
    target = rank * float(devices) + owner
    places = iota((slots * devices, blocks), 0, F32) == target
    onehot = jnp.where(places, 1.0, 0.0)
    valid = iota((width, blocks), 0) < count_ref[...]
    fields = jnp.concatenate(
        [
            frac_ref[0],
            frac_ref[1],
            value_ref[...],
            jnp.where(valid, weight_ref[...], 0.0),
            (cell_ref[...] * chans + level_ref[...]).astype(F32),
        ],
        axis=0,
    )
    placed = dot_nt(onehot, fields, lax.Precision.HIGHEST)
    full, rest, rows = slot_layout(slots)
    out_ref[...] = jnp.zeros(out_ref.shape, F32)
    for slot in range(slots):
        for field in range(FIELDS):
            piece = placed[
                slot * devices : (slot + 1) * devices, field * width : (field + 1) * width
            ]
            if slot < 4 * full:
                row, lane = (slot // 4) * FIELDS + field, (slot % 4) * width
            else:
                row = full * FIELDS + field // 2
                lane = (field % 2) * 2 * width + (slot - 4 * full) * width
            out_ref[:, row, lane : lane + width] = piece


def route(devices, slots, chans, obs_owner, obs_cell, obs_level, obs_count, obs_frac, obs_value,
          obs_weight):
    blocks = obs_value.shape[0]
    rows = slot_layout(slots)[2]
    return pl.pallas_call(
        functools.partial(route_kernel, devices, slots, chans),
        out_shape=jax.ShapeDtypeStruct((devices, rows, 128), F32),
        in_specs=[vmem()] * 7,
        out_specs=vmem(),
        compiler_params=params(16),
        name="route",
    )(
        obs_owner.reshape(1, blocks),
        obs_count.reshape(1, blocks),
        obs_cell.T,
        obs_level.T,
        jnp.transpose(obs_frac, (1, 2, 0)),
        obs_value.T,
        obs_weight.T,
    )


def silu_parts(first):
    sig = 1.0 / (1.0 + jnp.exp(-first))
    return sig, first * sig


def inside_grid(rows, shape, bands):
    lat = lax.axis_index("lat") * rows + iota(shape, 0) - 1
    return jnp.logical_and(lat >= 0, lat < bands * rows)


def band_copies(bands, piece_refs, all_ref, sems):
    core = lax.axis_index("lon") & 1
    lat = lax.axis_index("lat")
    copies = []
    for offset in range(bands):
        band = (lat + bands - offset) % bands
        for side in range(2):
            copies.append(
                pltpu.make_async_copy(
                    piece_refs[2 * offset + side],
                    all_ref.at[core if side == 0 else 1 - core, band],
                    sems.at[offset, side],
                )
            )
    return copies


def nearby_copies(bands, piece_refs, near_ref, sems):
    half = piece_refs[0].shape[0]
    lon = lax.axis_index("lon")
    west = lax.shift_right_logical((lon + 2 * half - 1) & (2 * half - 1), 1)
    east = lax.shift_right_logical((lon + 1) & (2 * half - 1), 1)
    here = lax.shift_right_logical(lon, 1)
    copies = []
    for down, offset in enumerate((1, 0, bands - 1)):
        mine, other = piece_refs[2 * offset], piece_refs[2 * offset + 1]
        for over, (source, q) in enumerate(((other, west), (mine, here), (other, east))):
            copies.append(
                pltpu.make_async_copy(source.at[q], near_ref.at[down, over], sems.at[down, over])
            )
    return copies


def fill_line(bands, near_ref, line_ref):
    rows, cols, chans = near_ref.shape[2:]
    lat = lax.axis_index("lat")
    for down, (y, height, first) in enumerate(((0, 2, rows - 2), (2, rows, 0), (2 + rows, 2, 0))):
        band = lat + down - 1
        for over, (x, width, left) in enumerate(((0, 2, cols - 2), (2, cols, 0), (2 + cols, 2, 0))):
            part = near_ref[down, over].astype(F32)[
                first : first + height, left : left + width
            ]
            if down != 1:
                part = jnp.where(jnp.logical_and(band >= 0, band < bands), part, 0.0)
            line_ref[y : y + height, x : x + width, :] = part
    line_ref[:, cols + 4 :, :] = jnp.zeros(
        (rows + 4, line_ref.shape[1] - cols - 4, chans), F32
    )


def forward_kernel(slots, bands, group, parts, *refs):
    piece_refs, refs = refs[: 2 * bands], refs[2 * bands :]
    w1_ref, w2_ref, got_ref, adj_ref, pull_ref, slope_ref = refs[:6]
    line_ref, shift_ref, hid_ref, obs_ref, sum_ref, near_ref, sems = refs[6:]
    rows, cols, chans = near_ref.shape[2:]
    span = hid_ref.shape[1]
    copies = nearby_copies(bands, piece_refs, near_ref, sems)
    for copy in copies:
        copy.start()
    for copy in copies:
        copy.wait()
    fill_line(bands, near_ref, line_ref)
    first = jnp.zeros(((rows + 2) * span, chans), F32)
    for b in range(3):
        shift_ref[...] = (
            line_ref[:, b : b + span, :].astype(BF16).reshape((rows + 4) * span, chans)
        )
        for a in range(3):
            first = first + dot(
                shift_ref[a * span : a * span + (rows + 2) * span, :], w1_ref[3 * a + b]
            )
    sig, hidden = silu_parts(first)
    slope_ref[...] = sig * (1.0 + first * (1.0 - sig))
    hidden = hidden.astype(BF16).astype(F32).reshape(rows + 2, span, chans)
    hidden = jnp.where(inside_grid(rows, hidden.shape, bands), hidden, 0.0)
    hid_ref[...] = hidden
    total = line_ref[2 : 2 + rows, 2 : 2 + cols, :].reshape(rows * cols, chans)
    for b in range(3):
        shift_ref[0 : (rows + 2) * cols, :] = (
            hid_ref[:, b : b + cols, :].astype(BF16).reshape((rows + 2) * cols, chans)
        )
        for a in range(3):
            total = total + dot(
                shift_ref[a * cols : a * cols + rows * cols, :], w2_ref[3 * a + b]
            )
    cells = rows * cols
    turned = total.T
    grid_high = turned.astype(BF16)
    grid_low = (turned - grid_high.astype(F32)).astype(BF16)
    grid_both = jnp.concatenate([grid_high, grid_low], axis=1)

    devices = got_ref.shape[0]
    full, rest, _ = slot_layout(slots)
    half = devices // 2
    for field in range(FIELDS):
        for part in range(full):
            obs_ref[field, part * devices : (part + 1) * devices, :] = got_ref[
                :, part * FIELDS + field, :
            ]
        if rest:
            tail = got_ref[:, full * FIELDS + field // 2, :]
            low, high = tail[:half], tail[half:]
            if field % 2 == 0:
                high = pltpu.roll(high, 64, 1)
            else:
                low = pltpu.roll(low, 64, 1)
            obs_ref[field, full * devices : full * devices + half, :] = jnp.where(
                iota((half, 128), 1) < 64, low, high
            )
    code = obs_ref[4].astype(jnp.int32)
    shift = chans.bit_length() - 1
    cell = lax.shift_right_logical(code, shift)
    obs_ref[4] = (code & (chans - 1)).astype(F32)
    obs_ref[0] = obs_ref[0] + lax.shift_right_logical(cell, 4).astype(F32)
    obs_ref[1] = obs_ref[1] + (cell & (cols - 1)).astype(F32)

    sum_ref[...] = jnp.zeros(sum_ref.shape, F32)
    count = obs_ref.shape[1] // (group * parts)
    row_ids = iota((rows, 128), 0, F32)
    col_ids = iota((cols, 128), 0, F32)
    level_ids = iota((chans, 128), 0, F32)

    def add_group(start):
        high, low, masks, marks = [], [], [], []
        for piece in range(group):
            mark = [obs_ref[field, pl.ds(start + piece, 1), :] for field in range(FIELDS)]
            up = jnp.maximum(0.0, 1.0 - jnp.abs(row_ids - mark[0]))
            along = jnp.maximum(0.0, 1.0 - jnp.abs(col_ids - mark[1]))
            weights = (up[:, None, :] * along[None, :, :]).reshape(cells, 128)
            weights_high = weights.astype(BF16)
            high.append(weights_high)
            low.append((weights - weights_high.astype(F32)).astype(BF16))
            masks.append(level_ids == mark[4])
            marks.append(mark)
        high = jnp.concatenate(high, axis=1)
        low = jnp.concatenate(low, axis=1)
        sampled = dot(grid_both, jnp.concatenate([high, high], axis=0)) + dot(grid_high, low)
        hot_high, hot_low = [], []
        for piece in range(group):
            mine = sampled[:, piece * 128 : (piece + 1) * 128]
            predicted = jnp.sum(jnp.where(masks[piece], mine, 0.0), axis=0, keepdims=True)
            misfit = marks[piece][3] * (predicted - marks[piece][2])
            misfit_high = misfit.astype(BF16).astype(F32)
            hot_high.append(jnp.where(masks[piece], misfit_high, 0.0).astype(BF16))
            hot_low.append(jnp.where(masks[piece], misfit - misfit_high, 0.0).astype(BF16))
        hot_high = jnp.concatenate(hot_high, axis=1)
        hot_low = jnp.concatenate(hot_low, axis=1)
        mixed = dot_nt(
            jnp.concatenate([hot_high, hot_low], axis=0), jnp.concatenate([high, low], axis=0)
        )
        return mixed[:chans, :cells] + (mixed[chans:, :cells] + mixed[:chans, cells:])

    def step(index, carry):
        total = sum_ref[...]
        for part in range(parts):
            total = total + add_group((index * parts + part) * group)
        sum_ref[...] = total
        return carry

    lax.fori_loop(0, count, step, 0)
    adjoint = sum_ref[...].T
    adj_ref[...] = adjoint
    pull_ref[...] = adjoint.astype(BF16)


def forward(slots, bands, pieces, w1, w2, got):
    half, rows, cols, chans = pieces[0].shape
    devices = got.shape[0]
    full, rest, _ = slot_layout(slots)
    groups = full * devices + (devices // 2 if rest else 0)
    return pl.pallas_call(
        functools.partial(forward_kernel, slots, bands, 2, 4),
        out_shape=[
            jax.ShapeDtypeStruct((rows * cols, chans), F32),
            jax.ShapeDtypeStruct((rows * cols, chans), BF16),
            jax.ShapeDtypeStruct(((rows + 2) * SPAN, chans), F32),
        ],
        in_specs=[anywhere()] * len(pieces) + [vmem()] * 3,
        out_specs=[vmem()] * 3,
        scratch_shapes=[
            pltpu.VMEM((rows + 4, SPAN + 8, chans), F32),
            pltpu.VMEM(((rows + 4) * SPAN, chans), BF16),
            pltpu.VMEM((rows + 2, SPAN, chans), F32),
            pltpu.VMEM((FIELDS, groups, 128), F32),
            pltpu.VMEM((chans, rows * cols), F32),
            pltpu.VMEM((3, 3, rows, cols, chans), BF16),
            pltpu.SemaphoreType.DMA((3, 3)),
        ],
        compiler_params=params(24),
        cost_estimate=cost(4e9, 4e6),
        name="forward",
    )(*pieces, w1, w2, got)


def spread_matrix(steps, tiles):
    lons = 16 * steps
    half = tiles // 2
    place = iota(((steps + 2) * 16, lons), 0)
    lon = (place & 15) * steps + lax.shift_right_logical(place, 4) - 1
    lon = jnp.where(lon < 0, lon + lons, jnp.where(lon >= lons, lon - lons, lon))
    column = iota(((steps + 2) * 16, lons), 1)
    chunk = lax.shift_right_logical(column, 4)
    core = lax.shift_right_logical(chunk, half.bit_length() - 1)
    column = (2 * (chunk & (half - 1)) + core) * 16 + (column & 15)
    return jnp.where(column == lon, 1.0, 0.0)


def spread(line_of, start, lats, matrix, pad_ref):
    steps = pad_ref.shape[1] - 2
    for row in range(pad_ref.shape[0]):
        lat = start + row
        inside = jnp.logical_and(lat >= 0, lat < lats)
        line = line_of(jnp.clip(lat, 0, lats - 1))
        chosen = jnp.where(inside, matrix, 0.0).astype(BF16)
        pad_ref[row] = dot(chosen, line).astype(BF16).reshape(steps + 2, 16, line.shape[1])


def conv_block(pad_ref, weight_ref, start, rows, flipped):
    steps = pad_ref.shape[1] - 2
    chans = pad_ref.shape[3]
    pieces = []
    for a in range(3):
        for b in range(3):
            da, db = (2 - a, 2 - b) if flipped else (a, b)
            piece = pad_ref[pl.ds(start + da, rows), db : db + steps]
            pieces.append(piece.reshape(rows * steps * 16, chans))
    return dot(jnp.concatenate(pieces, axis=1), weight_ref[...].reshape(9 * chans, chans))


def whole_kernel(block, *refs):
    bands = refs[-2].shape[1]
    piece_refs, refs = refs[: 2 * bands], refs[2 * bands :]
    w1_ref, w2_ref, slope_ref, hidden_ref, state_ref, w2t_ref, pad_ref, all_ref, sems = refs
    _, _, half, rows, group, chans = all_ref.shape
    lats, lons = bands * rows, 2 * half * group
    steps = lons // 16
    size = block * lons
    mine = pad_ref.shape[0] - 4
    base = (lax.axis_index("lon") & 1) * mine
    copies = band_copies(bands, piece_refs, all_ref, sems)
    for copy in copies:
        copy.start()
    matrix = spread_matrix(steps, 2 * half)
    for tap in range(9):
        w2t_ref[tap] = w2_ref[tap].T
    for copy in copies:
        copy.wait()
    spread(
        lambda lat: all_ref[:, lat // rows, :, lat % rows].reshape(lons, chans),
        base - 2, lats, matrix, pad_ref,
    )

    def step(index, carry):
        start = index * block
        first = conv_block(pad_ref, w1_ref, start, block, False)
        sig, hidden = silu_parts(first)
        at = pl.ds(pl.multiple_of(index * size, size), size)
        slope_ref[at, :] = sig * (1.0 + first * (1.0 - sig))
        lat = base - 1 + start + lax.shift_right_logical(
            iota((size, chans), 0), lons.bit_length() - 1
        )
        hidden = jnp.where(jnp.logical_and(lat >= 0, lat < lats), hidden, 0.0)
        hidden_ref[:, at] = hidden.astype(BF16).T
        centre = pad_ref[pl.ds(start + 1, block), 1 : 1 + steps].reshape(size, chans)
        state_ref[:, at] = centre.T
        return carry

    lax.fori_loop(0, (mine + 2) // block, step, 0)


def whole(bands, pieces, w1, w2):
    half, rows, group, chans = pieces[0].shape
    lats, lons = bands * rows, 2 * half * group
    mine = lats // 2
    steps = lons // 16
    cells = (mine + 2) * lons
    return pl.pallas_call(
        functools.partial(whole_kernel, 3),
        out_shape=[
            jax.ShapeDtypeStruct((cells, chans), F32),
            jax.ShapeDtypeStruct((chans, cells), BF16),
            jax.ShapeDtypeStruct((chans, cells), BF16),
            jax.ShapeDtypeStruct((9, chans, chans), BF16),
        ],
        in_specs=[anywhere()] * len(pieces) + [vmem()] * 2,
        out_specs=[vmem()] * 4,
        scratch_shapes=[
            pltpu.VMEM((mine + 4, steps + 2, 16, chans), BF16),
            pltpu.VMEM((2, bands) + pieces[0].shape, BF16),
            pltpu.SemaphoreType.DMA((bands, 2)),
        ],
        compiler_params=params(28),
        cost_estimate=cost(6e9, 10e6),
        name="whole",
    )(*pieces, w1, w2)


def tap_sums(turned_ref, pad_ref, first_row, rows, sum_ref, out_ref, sem):
    steps = pad_ref.shape[1] - 2
    chans = pad_ref.shape[3]
    lons = steps * 16

    def step(tap, carry):
        a, b = tap // 3, tap % 3
        piece = pad_ref[first_row : first_row + rows, pl.ds(2 - b, steps)]
        at = pl.ds(pl.multiple_of(a * lons, lons), rows * lons)
        sum_ref[tap] = dot(turned_ref[:, at], piece.reshape(rows * lons, chans))
        pltpu.make_async_copy(sum_ref.at[tap], out_ref.at[tap], sem.at[tap]).start()
        return carry

    lax.fori_loop(0, 9, step, 0)


def tail_kernel(block, *refs):
    bands = (len(refs) - 18) // 2
    piece_refs, refs = refs[: 2 * bands], refs[2 * bands :]
    slope_hbm, hidden_hbm, state_hbm, w2t_ref, g1_hbm, g2_hbm = refs[:6]
    all_ref, pull_ref, first_ref, slope_ref, hidden_ref, state_ref, g1_ref, g2_ref = refs[6:14]
    piece_sems, big_sems, g1_sems, g2_sems = refs[14:]
    steps = pull_ref.shape[1] - 2
    chans = pull_ref.shape[3]
    lons = steps * 16
    size = block * lons
    _, bands, half, rows, cols, _ = all_ref.shape
    lats = bands * rows
    mine = lats // 2
    base = (lax.axis_index("lon") & 1) * mine
    copies = band_copies(bands, piece_refs, all_ref, piece_sems)
    hidden_copy = pltpu.make_async_copy(hidden_hbm, hidden_ref, big_sems.at[0])
    slope_copy = pltpu.make_async_copy(
        slope_hbm.at[pl.ds(lons, mine * lons), :], slope_ref, big_sems.at[1]
    )
    state_copy = pltpu.make_async_copy(state_hbm, state_ref, big_sems.at[2])
    for copy in copies:
        copy.start()
    hidden_copy.start()
    slope_copy.start()
    state_copy.start()
    matrix = spread_matrix(steps, 2 * half)
    for copy in copies:
        copy.wait()
    spread(
        lambda lat: all_ref[:, lat // rows, :, lat % rows].reshape(lons, chans),
        base - 1, lats, matrix, pull_ref,
    )
    hidden_copy.wait()
    tap_sums(hidden_ref, pull_ref, 1, mine, g2_ref, g2_hbm, g2_sems)
    slope_copy.wait()

    def step(index, carry):
        start = index * block
        back = conv_block(pull_ref, w2t_ref, start, block, True)
        at = pl.ds(pl.multiple_of(index * size, size), size)
        pull = (back * slope_ref[at, :]).astype(BF16).astype(F32)
        pull = pull.reshape(block, steps, 16, chans)
        last, head = pull[:, steps - 1], pull[:, 0]
        before = jnp.concatenate([last[:, 15:], last[:, :15]], axis=1)
        after = jnp.concatenate([head[:, 1:], head[:, :1]], axis=1)
        to = pl.ds(start, block)
        first_ref[to, 1 : 1 + steps] = pull.astype(BF16)
        first_ref[to, 0] = before.astype(BF16)
        first_ref[to, steps + 1] = after.astype(BF16)
        return carry

    lax.fori_loop(0, mine // block, step, 0)
    state_copy.wait()
    tap_sums(state_ref, first_ref, 0, mine, g1_ref, g1_hbm, g1_sems)
    for tap in range(9):
        pltpu.make_async_copy(g2_ref.at[tap], g2_hbm.at[tap], g2_sems.at[tap]).wait()
        pltpu.make_async_copy(g1_ref.at[tap], g1_hbm.at[tap], g1_sems.at[tap]).wait()


def tail(bands, pieces, slope, hidden, state, w2t):
    half, rows, group, chans = pieces[0].shape
    lats, lons = bands * rows, 2 * half * group
    steps = lons // 16
    ours = lats // 2
    return pl.pallas_call(
        functools.partial(tail_kernel, 4),
        out_shape=[jax.ShapeDtypeStruct((9, chans, chans), F32)] * 2,
        in_specs=[anywhere()] * (len(pieces) + 3) + [vmem()],
        out_specs=[anywhere()] * 2,
        scratch_shapes=[
            pltpu.VMEM((2, bands) + pieces[0].shape, BF16),
            pltpu.VMEM((ours + 2, steps + 2, 16, chans), BF16),
            pltpu.VMEM((ours, steps + 2, 16, chans), BF16),
            pltpu.VMEM((ours * lons, chans), F32),
            pltpu.VMEM(hidden.shape, BF16),
            pltpu.VMEM(state.shape, BF16),
            pltpu.VMEM((9, chans, chans), F32),
            pltpu.VMEM((9, chans, chans), F32),
            pltpu.SemaphoreType.DMA((bands, 2)),
            pltpu.SemaphoreType.DMA((3,)),
            pltpu.SemaphoreType.DMA((9,)),
            pltpu.SemaphoreType.DMA((9,)),
        ],
        compiler_params=params(36),
        cost_estimate=cost(10e9, 15e6),
        name="tail",
    )(*pieces, slope, hidden, state, w2t)


def local_kernel(bands, *refs):
    piece_refs, refs = refs[: 2 * bands], refs[2 * bands :]
    slope_ref, adj_ref, w1_ref, w2_ref, grad_ref = refs[:5]
    near_ref, line_ref, shift_ref, pull_ref, sems = refs[5:]
    rows, cols, chans = near_ref.shape[2:]
    span = pull_ref.shape[1]
    copies = nearby_copies(bands, piece_refs, near_ref, sems)
    for copy in copies:
        copy.start()
    for copy in copies:
        copy.wait()
    fill_line(bands, near_ref, line_ref)
    back = jnp.zeros(((rows + 2) * span, chans), F32)
    for b in range(3):
        shift_ref[...] = (
            line_ref[:, 2 - b : 2 - b + span, :].astype(BF16).reshape((rows + 4) * span, chans)
        )
        for a in range(3):
            piece = shift_ref[(2 - a) * span : (2 - a) * span + (rows + 2) * span, :]
            back = back + dot_nt(piece, w2_ref[3 * a + b])
    pull = (back * slope_ref[...]).reshape(rows + 2, span, chans)
    pull_ref[...] = jnp.where(inside_grid(rows, pull.shape, bands), pull, 0.0)
    total = adj_ref[...]
    for b in range(3):
        shift_ref[0 : (rows + 2) * cols, :] = (
            pull_ref[:, 2 - b : 2 - b + cols, :].astype(BF16).reshape((rows + 2) * cols, chans)
        )
        for a in range(3):
            piece = shift_ref[(2 - a) * cols : (2 - a) * cols + rows * cols, :]
            total = total + dot_nt(piece, w1_ref[3 * a + b])
    grad_ref[...] = total


def local_grad(bands, pieces, slope, adjoint, w1, w2):
    half, rows, cols, chans = pieces[0].shape
    return pl.pallas_call(
        functools.partial(local_kernel, bands),
        out_shape=jax.ShapeDtypeStruct((rows * cols, chans), F32),
        in_specs=[anywhere()] * len(pieces) + [vmem()] * 4,
        out_specs=vmem(),
        scratch_shapes=[
            pltpu.VMEM((3, 3, rows, cols, chans), BF16),
            pltpu.VMEM((rows + 4, SPAN + 8, chans), F32),
            pltpu.VMEM(((rows + 4) * SPAN, chans), BF16),
            pltpu.VMEM((rows + 2, SPAN, chans), F32),
            pltpu.SemaphoreType.DMA((3, 3)),
        ],
        compiler_params=params(16),
        cost_estimate=cost(3e9, 4e6),
        name="local_grad",
    )(*pieces, slope, adjoint, w1, w2)


def with_halo(x, sides, width, wrap):
    for axis, dim in sides:
        count, length = (lax.axis_size(axis), x.shape[dim])
        up = [(i, (i + 1) % count) for i in range(count if wrap else count - 1)]
        down = [(j, i) for i, j in up]
        last = lax.slice_in_dim(x, length - width, length, axis=dim)
        first = lax.slice_in_dim(x, 0, width, axis=dim)
        before = lax.ppermute(last, axis, up)
        after = lax.ppermute(first, axis, down)
        x = jnp.concatenate([before, x, after], axis=dim)
    return x


def widen_tile(field):
    across = with_halo(field, (("lon", 1),), 1, True)
    return with_halo(across, (("lat", 0),), 1, False)


def tile_conv(padded, weight, rows, cols, flipped):
    total = jnp.zeros((rows * cols, weight.shape[2]), jnp.float32)
    for first_tap in range(3):
        for second_tap in range(3):
            if flipped:
                piece = padded[
                    2 - first_tap : 2 - first_tap + rows, 2 - second_tap : 2 - second_tap + cols
                ]
                total = total + lax.dot_general(
                    piece.reshape(rows * cols, -1),
                    weight[3 * first_tap + second_tap],
                    (((1,), (1,)), ((), ())),
                    preferred_element_type=jnp.float32,
                )
            else:
                piece = padded[first_tap : first_tap + rows, second_tap : second_tap + cols]
                total = total + jnp.dot(
                    piece.reshape(rows * cols, -1),
                    weight[3 * first_tap + second_tap],
                    preferred_element_type=jnp.float32,
                )
    return total.reshape(rows, cols, -1)


def tile_grads(padded, pullback, rows, cols):
    flat_pull = pullback.reshape(rows * cols, -1)
    result = []
    for first_tap in range(3):
        for second_tap in range(3):
            piece = padded[first_tap : first_tap + rows, second_tap : second_tap + cols].reshape(
                rows * cols, -1
            )
            result.append(
                lax.dot_general(
                    piece, flat_pull, (((0,), (0,)), ((), ())), preferred_element_type=jnp.float32
                )
            )
    return jnp.stack(result)


def route_blocks(obs_owner, obs_cell, obs_level, obs_count, obs_frac, obs_value, obs_weight):
    devices = lax.axis_size(("lat", "lon"))
    blocks, width = obs_value.shape
    slots = max(2, 3 * blocks // (2 * devices))
    owner = obs_owner[:, 0]
    order = lax.broadcasted_iota(jnp.int32, (blocks, blocks), 1) < lax.broadcasted_iota(
        jnp.int32, (blocks, blocks), 0
    )
    earlier = jnp.logical_and(owner[:, None] == owner[None, :], order)
    rank = jnp.sum(earlier.astype(jnp.int32), axis=1)
    target = owner * slots + rank
    valid = (lax.broadcasted_iota(jnp.int32, (blocks, width), 1) < obs_count[:, None]).astype(
        jnp.float32
    )
    packed = jnp.stack(
        [
            obs_frac[:, 0, :],
            obs_frac[:, 1, :],
            obs_value,
            obs_weight,
            obs_cell.astype(jnp.float32),
            obs_level.astype(jnp.float32),
            valid,
        ],
        axis=1,
    )
    outgoing = jnp.zeros((devices * slots, 7, width), jnp.float32).at[target].set(packed)
    return lax.all_to_all(outgoing, ("lat", "lon"), split_axis=0, concat_axis=0, tiled=True)


def observe(corrected, arrived, rows, cols, chans):
    fields = jnp.transpose(arrived, (1, 0, 2)).reshape(7, -1)
    row_total = fields.shape[1]
    span_rows = math.gcd(row_total, 1024)
    fields = jnp.transpose(fields.reshape(7, row_total // span_rows, span_rows), (1, 0, 2))
    grid = corrected.reshape(rows * cols, chans)
    cells = lax.broadcasted_iota(jnp.int32, (1, rows * cols), 1)
    levels = lax.broadcasted_iota(jnp.int32, (1, chans), 1)

    def advance(summed, portion):
        frac_lat = portion[0][:, None]
        frac_lon = portion[1][:, None]
        corner = portion[4].astype(jnp.int32)[:, None]
        level = portion[5].astype(jnp.int32)[:, None]
        weights = (1.0 - frac_lat) * (1.0 - frac_lon) * (cells == corner).astype(jnp.float32)
        weights = weights + (1.0 - frac_lat) * frac_lon * (cells == corner + 1).astype(jnp.float32)
        weights = weights + frac_lat * (1.0 - frac_lon) * (cells == corner + cols).astype(
            jnp.float32
        )
        weights = weights + frac_lat * frac_lon * (cells == corner + cols + 1).astype(jnp.float32)
        onehot = (levels == level).astype(jnp.float32)
        sampled = jnp.dot(
            weights, grid, precision=lax.Precision.HIGHEST, preferred_element_type=jnp.float32
        )
        predicted = jnp.sum(sampled * onehot, axis=1)
        misfit = portion[6] * portion[3] * (predicted - portion[2])
        summed = summed + lax.dot_general(
            weights,
            onehot * misfit[:, None],
            (((0,), (0,)), ((), ())),
            precision=lax.Precision.HIGHEST,
            preferred_element_type=jnp.float32,
        )
        return (summed, None)

    summed, unused = lax.scan(advance, jnp.zeros((rows * cols, chans), jnp.float32), fields)
    return summed.reshape(rows, cols, chans)


def by_tiles(
    state,
    weight_first,
    weight_second,
    obs_owner,
    obs_cell,
    obs_level,
    obs_count,
    obs_frac,
    obs_value,
    obs_weight,
):
    rows, cols, chans = state.shape
    wide_state = widen_tile(state)
    first = tile_conv(wide_state, weight_first, rows, cols, False)
    hidden = jax.nn.silu(first).astype(jnp.bfloat16)
    wide_hidden = widen_tile(hidden)
    corrected = state.astype(jnp.float32) + tile_conv(wide_hidden, weight_second, rows, cols, False)
    arrived = route_blocks(
        obs_owner, obs_cell, obs_level, obs_count, obs_frac, obs_value, obs_weight
    )
    adjoint = observe(corrected, arrived, rows, cols, chans)
    pullback = adjoint.astype(jnp.bfloat16)
    wide_pull = widen_tile(pullback)
    local_second = tile_grads(wide_hidden, pullback, rows, cols)
    back = tile_conv(wide_pull, weight_second, rows, cols, True)
    sig = jax.nn.sigmoid(first)
    pull_first = (back * sig * (1.0 + first * (1.0 - sig))).astype(jnp.bfloat16)
    wide_pull_first = widen_tile(pull_first)
    local_first = tile_grads(wide_state, pull_first, rows, cols)
    state_grad = adjoint + tile_conv(wide_pull_first, weight_first, rows, cols, True)
    grad_first, grad_second = lax.psum((local_first, local_second), ("lat", "lon"))
    return (state_grad, grad_first, grad_second)


def gather_tiles(x):
    bands, tiles = lax.axis_size("lat"), lax.axis_size("lon")
    half = tiles // 2
    same = [[2 * q + core for q in range(half)] for core in range(2)]
    swap = [(i, i ^ 1) for i in range(tiles)]
    copies = jnp.broadcast_to(x[None], (half,) + x.shape)
    line = lax.all_to_all(copies, "lon", 0, 0, axis_index_groups=same, tiled=True)
    mine = [line]
    for step in range(1, bands):
        mine.append(lax.ppermute(line, "lat", [(i, (i + step) % bands) for i in range(bands)]))
    pieces = []
    for part in mine:
        pieces += [part, lax.ppermute(part, "lon", swap)]
    return pieces


def per_device(
    state, weight_first, weight_second, obs_owner, obs_cell, obs_level, obs_count, obs_frac,
    obs_value, obs_weight,
):
    rows, cols, chans = state.shape
    bands = lax.axis_size("lat")
    devices = lax.axis_size(("lat", "lon"))
    if devices * rows * cols > WHOLE_CELLS:
        return by_tiles(
            state, weight_first, weight_second, obs_owner, obs_cell, obs_level, obs_count,
            obs_frac, obs_value, obs_weight,
        )
    slots = max(2, 3 * obs_value.shape[0] // (2 * devices))
    state_pieces = gather_tiles(state)
    outgoing = route(
        devices, slots, chans, obs_owner, obs_cell, obs_level, obs_count, obs_frac, obs_value,
        obs_weight,
    )
    got = lax.all_to_all(outgoing, ("lat", "lon"), split_axis=0, concat_axis=0, tiled=True)
    adjoint, pullback, near_slope = forward(
        slots, bands, state_pieces, weight_first, weight_second, got
    )
    pull_pieces = gather_tiles(pullback.reshape(rows, cols, chans))
    slope, hidden, turned, w2t = whole(bands, state_pieces, weight_first, weight_second)
    sums = tail(bands, pull_pieces, slope, hidden, turned, w2t)
    swap = [(i, i ^ 1) for i in range(lax.axis_size("lon"))]
    theirs = [lax.ppermute(part, "lon", swap) for part in sums]
    grad = local_grad(bands, pull_pieces, near_slope, adjoint, weight_first, weight_second)
    g1, g2 = [part + their for part, their in zip(sums, theirs)]
    return grad.reshape(rows, cols, chans), g1, g2


def solution(mesh):
    both = P(("lat", "lon"), None)
    placed = (
        P("lat", "lon", None),
        P(),
        P(),
        both,
        both,
        both,
        P(("lat", "lon")),
        P(("lat", "lon"), None, None),
        both,
        both,
    )
    return jax.shard_map(
        per_device,
        mesh=mesh,
        in_specs=placed,
        out_specs=(P("lat", "lon", None), P(), P()),
        check_vma=False,
    )
```

```python
import functools
import math

import jax
import jax.numpy as jnp
from jax import lax
from jax.experimental import pallas as pl
from jax.experimental.pallas import tpu as pltpu
from jax.sharding import PartitionSpec as P

F32 = jnp.float32
BF16 = jnp.bfloat16
FIELDS = 5
SPAN = 32
WHOLE_CELLS = 4096


def params(mebibytes):
    return pltpu.CompilerParams(vmem_limit_bytes=mebibytes * 1024 * 1024)


def cost(flops, moved):
    return pl.CostEstimate(flops=int(flops), bytes_accessed=int(moved), transcendentals=0)


def vmem():
    return pl.BlockSpec(memory_space=pltpu.VMEM)


def anywhere():
    return pl.BlockSpec(memory_space=pl.ANY)


def iota(shape, dim, dtype=jnp.int32):
    return lax.broadcasted_iota(jnp.int32, shape, dim).astype(dtype)


def dot(x, y, precision=None):
    return jnp.dot(x, y, precision=precision, preferred_element_type=F32)


def dot_nt(x, y, precision=None):
    return lax.dot_general(
        x, y, (((1,), (1,)), ((), ())), precision=precision, preferred_element_type=F32
    )


def slot_layout(slots):
    full, rest = divmod(slots, 4)
    rows = full * FIELDS + (0 if rest == 0 else -(-FIELDS // 2))
    return full, rest, -(-rows // 8) * 8


def route_kernel(
    devices, slots, chans, owner_ref, count_ref, cell_ref, level_ref, frac_ref, value_ref,
    weight_ref, out_ref
):
    width, blocks = value_ref.shape
    owner = owner_ref[...].astype(F32)
    across = jnp.broadcast_to(owner, (blocks, blocks))
    down = across.T
    earlier = iota((blocks, blocks), 0) < iota((blocks, blocks), 1)
    hits = jnp.where(jnp.logical_and(across == down, earlier), 1.0, 0.0)
    rank = jnp.sum(hits, axis=0, keepdims=True)
    target = rank * float(devices) + owner
    places = iota((slots * devices, blocks), 0, F32) == target
    onehot = jnp.where(places, 1.0, 0.0)
    valid = iota((width, blocks), 0) < count_ref[...]
    fields = jnp.concatenate(
        [
            frac_ref[0],
            frac_ref[1],
            value_ref[...],
            jnp.where(valid, weight_ref[...], 0.0),
            (cell_ref[...] * chans + level_ref[...]).astype(F32),
        ],
        axis=0,
    )
    placed = dot_nt(onehot, fields, lax.Precision.HIGHEST)
    full, rest, rows = slot_layout(slots)
    out_ref[...] = jnp.zeros(out_ref.shape, F32)
    for slot in range(slots):
        for field in range(FIELDS):
            piece = placed[
                slot * devices : (slot + 1) * devices, field * width : (field + 1) * width
            ]
            if slot < 4 * full:
                row, lane = (slot // 4) * FIELDS + field, (slot % 4) * width
            else:
                row = full * FIELDS + field // 2
                lane = (field % 2) * 2 * width + (slot - 4 * full) * width
            out_ref[:, row, lane : lane + width] = piece


def route(devices, slots, chans, obs_owner, obs_cell, obs_level, obs_count, obs_frac, obs_value,
          obs_weight):
    blocks = obs_value.shape[0]
    rows = slot_layout(slots)[2]
    return pl.pallas_call(
        functools.partial(route_kernel, devices, slots, chans),
        out_shape=jax.ShapeDtypeStruct((devices, rows, 128), F32),
        in_specs=[vmem()] * 7,
        out_specs=vmem(),
        compiler_params=params(16),
        name="route",
    )(
        obs_owner.reshape(1, blocks),
        obs_count.reshape(1, blocks),
        obs_cell.T,
        obs_level.T,
        jnp.transpose(obs_frac, (1, 2, 0)),
        obs_value.T,
        obs_weight.T,
    )


def silu_parts(first):
    sig = 1.0 / (1.0 + jnp.exp(-first))
    return sig, first * sig


def inside_grid(rows, shape, bands):
    lat = lax.axis_index("lat") * rows + iota(shape, 0) - 1
    return jnp.logical_and(lat >= 0, lat < bands * rows)


def band_copies(bands, piece_refs, all_ref, sems):
    core = lax.axis_index("lon") & 1
    lat = lax.axis_index("lat")
    copies = []
    for offset in range(bands):
        band = (lat + bands - offset) % bands
        for side in range(2):
            copies.append(
                pltpu.make_async_copy(
                    piece_refs[2 * offset + side],
                    all_ref.at[core if side == 0 else 1 - core, band],
                    sems.at[offset, side],
                )
            )
    return copies


def nearby_copies(bands, piece_refs, near_ref, sems):
    half = piece_refs[0].shape[0]
    lon = lax.axis_index("lon")
    west = lax.shift_right_logical((lon + 2 * half - 1) & (2 * half - 1), 1)
    east = lax.shift_right_logical((lon + 1) & (2 * half - 1), 1)
    here = lax.shift_right_logical(lon, 1)
    copies = []
    for down, offset in enumerate((1, 0, bands - 1)):
        mine, other = piece_refs[2 * offset], piece_refs[2 * offset + 1]
        for over, (source, q) in enumerate(((other, west), (mine, here), (other, east))):
            copies.append(
                pltpu.make_async_copy(source.at[q], near_ref.at[down, over], sems.at[down, over])
            )
    return copies


def fill_line(bands, near_ref, line_ref):
    rows, cols, chans = near_ref.shape[2:]
    lat = lax.axis_index("lat")
    for down, (y, height, first) in enumerate(((0, 2, rows - 2), (2, rows, 0), (2 + rows, 2, 0))):
        band = lat + down - 1
        for over, (x, width, left) in enumerate(((0, 2, cols - 2), (2, cols, 0), (2 + cols, 2, 0))):
            part = near_ref[down, over].astype(F32)[
                first : first + height, left : left + width
            ]
            if down != 1:
                part = jnp.where(jnp.logical_and(band >= 0, band < bands), part, 0.0)
            line_ref[y : y + height, x : x + width, :] = part
    line_ref[:, cols + 4 :, :] = jnp.zeros(
        (rows + 4, line_ref.shape[1] - cols - 4, chans), F32
    )


def forward_kernel(slots, bands, group, parts, tile_ref, north_ref, south_ref, west_ref, east_ref,
                   w1_ref, w2_ref, got_ref, adj_ref, pull_ref, slope_ref, line_ref, shift_ref,
                   hid_ref, obs_ref, sum_ref):
    rows, cols, chans = tile_ref.shape
    span = hid_ref.shape[1]
    line_ref[0:2, 2 : 2 + cols, :] = north_ref[...].astype(F32)
    line_ref[2 : 2 + rows, 2 : 2 + cols, :] = tile_ref[...].astype(F32)
    line_ref[2 + rows :, 2 : 2 + cols, :] = south_ref[...].astype(F32)
    line_ref[:, 0:2, :] = west_ref[...].astype(F32)
    line_ref[:, 2 + cols : 4 + cols, :] = east_ref[...].astype(F32)
    line_ref[:, cols + 4 :, :] = jnp.zeros(
        (rows + 4, line_ref.shape[1] - cols - 4, chans), F32
    )
    first = jnp.zeros(((rows + 2) * span, chans), F32)
    for b in range(3):
        shift_ref[...] = (
            line_ref[:, b : b + span, :].astype(BF16).reshape((rows + 4) * span, chans)
        )
        for a in range(3):
            first = first + dot(
                shift_ref[a * span : a * span + (rows + 2) * span, :], w1_ref[3 * a + b]
            )
    sig, hidden = silu_parts(first)
    slope_ref[...] = sig * (1.0 + first * (1.0 - sig))
    hidden = hidden.astype(BF16).astype(F32).reshape(rows + 2, span, chans)
    hidden = jnp.where(inside_grid(rows, hidden.shape, bands), hidden, 0.0)
    hid_ref[...] = hidden
    total = line_ref[2 : 2 + rows, 2 : 2 + cols, :].reshape(rows * cols, chans)
    for b in range(3):
        shift_ref[0 : (rows + 2) * cols, :] = (
            hid_ref[:, b : b + cols, :].astype(BF16).reshape((rows + 2) * cols, chans)
        )
        for a in range(3):
            total = total + dot(
                shift_ref[a * cols : a * cols + rows * cols, :], w2_ref[3 * a + b]
            )
    cells = rows * cols
    turned = total.T
    grid_high = turned.astype(BF16)
    grid_low = (turned - grid_high.astype(F32)).astype(BF16)
    grid_both = jnp.concatenate([grid_high, grid_low], axis=1)

    devices = got_ref.shape[0]
    full, rest, _ = slot_layout(slots)
    half = devices // 2
    for field in range(FIELDS):
        for part in range(full):
            obs_ref[field, part * devices : (part + 1) * devices, :] = got_ref[
                :, part * FIELDS + field, :
            ]
        if rest:
            tail = got_ref[:, full * FIELDS + field // 2, :]
            low, high = tail[:half], tail[half:]
            if field % 2 == 0:
                high = pltpu.roll(high, 64, 1)
            else:
                low = pltpu.roll(low, 64, 1)
            obs_ref[field, full * devices : full * devices + half, :] = jnp.where(
                iota((half, 128), 1) < 64, low, high
            )
    code = obs_ref[4].astype(jnp.int32)
    shift = chans.bit_length() - 1
    cell = lax.shift_right_logical(code, shift)
    obs_ref[4] = (code & (chans - 1)).astype(F32)
    obs_ref[0] = obs_ref[0] + lax.shift_right_logical(cell, 4).astype(F32)
    obs_ref[1] = obs_ref[1] + (cell & (cols - 1)).astype(F32)

    sum_ref[...] = jnp.zeros(sum_ref.shape, F32)
    count = obs_ref.shape[1] // (group * parts)
    row_ids = iota((rows, 128), 0, F32)
    col_ids = iota((cols, 128), 0, F32)
    level_ids = iota((chans, 128), 0, F32)

    def add_group(start):
        high, low, masks, marks = [], [], [], []
        for piece in range(group):
            mark = [obs_ref[field, pl.ds(start + piece, 1), :] for field in range(FIELDS)]
            up = jnp.maximum(0.0, 1.0 - jnp.abs(row_ids - mark[0]))
            along = jnp.maximum(0.0, 1.0 - jnp.abs(col_ids - mark[1]))
            weights = (up[:, None, :] * along[None, :, :]).reshape(cells, 128)
            weights_high = weights.astype(BF16)
            high.append(weights_high)
            low.append((weights - weights_high.astype(F32)).astype(BF16))
            masks.append(level_ids == mark[4])
            marks.append(mark)
        high = jnp.concatenate(high, axis=1)
        low = jnp.concatenate(low, axis=1)
        sampled = dot(grid_both, jnp.concatenate([high, high], axis=0)) + dot(grid_high, low)
        hot_high, hot_low = [], []
        for piece in range(group):
            mine = sampled[:, piece * 128 : (piece + 1) * 128]
            predicted = jnp.sum(jnp.where(masks[piece], mine, 0.0), axis=0, keepdims=True)
            misfit = marks[piece][3] * (predicted - marks[piece][2])
            misfit_high = misfit.astype(BF16).astype(F32)
            hot_high.append(jnp.where(masks[piece], misfit_high, 0.0).astype(BF16))
            hot_low.append(jnp.where(masks[piece], misfit - misfit_high, 0.0).astype(BF16))
        hot_high = jnp.concatenate(hot_high, axis=1)
        hot_low = jnp.concatenate(hot_low, axis=1)
        mixed = dot_nt(
            jnp.concatenate([hot_high, hot_low], axis=0), jnp.concatenate([high, low], axis=0)
        )
        return mixed[:chans, :cells] + (mixed[chans:, :cells] + mixed[:chans, cells:])

    def step(index, carry):
        total = sum_ref[...]
        for part in range(parts):
            total = total + add_group((index * parts + part) * group)
        sum_ref[...] = total
        return carry

    lax.fori_loop(0, count, step, 0)
    adjoint = sum_ref[...].T
    adj_ref[...] = adjoint
    pull_ref[...] = adjoint.astype(BF16)


def forward(slots, bands, pieces, w1, w2, got):
    rows, cols, chans = pieces[0].shape
    devices = got.shape[0]
    full, rest, _ = slot_layout(slots)
    groups = full * devices + (devices // 2 if rest else 0)
    return pl.pallas_call(
        functools.partial(forward_kernel, slots, bands, 2, 4),
        out_shape=[
            jax.ShapeDtypeStruct((rows * cols, chans), F32),
            jax.ShapeDtypeStruct((rows * cols, chans), BF16),
            jax.ShapeDtypeStruct(((rows + 2) * SPAN, chans), F32),
        ],
        in_specs=[vmem()] * 8,
        out_specs=[vmem()] * 3,
        scratch_shapes=[
            pltpu.VMEM((rows + 4, SPAN + 8, chans), F32),
            pltpu.VMEM(((rows + 4) * SPAN, chans), BF16),
            pltpu.VMEM((rows + 2, SPAN, chans), F32),
            pltpu.VMEM((FIELDS, groups, 128), F32),
            pltpu.VMEM((chans, rows * cols), F32),
        ],
        compiler_params=params(24),
        cost_estimate=cost(4e9, 4e6),
        name="forward",
    )(*pieces, w1, w2, got)


def spread_matrix(steps, tiles):
    lons = 16 * steps
    half = tiles // 2
    place = iota(((steps + 2) * 16, lons), 0)
    lon = (place & 15) * steps + lax.shift_right_logical(place, 4) - 1
    lon = jnp.where(lon < 0, lon + lons, jnp.where(lon >= lons, lon - lons, lon))
    column = iota(((steps + 2) * 16, lons), 1)
    chunk = lax.shift_right_logical(column, 4)
    core = lax.shift_right_logical(chunk, half.bit_length() - 1)
    column = (2 * (chunk & (half - 1)) + core) * 16 + (column & 15)
    return jnp.where(column == lon, 1.0, 0.0)


def spread(line_of, start, lats, matrix, pad_ref):
    steps = pad_ref.shape[1] - 2
    for row in range(pad_ref.shape[0]):
        lat = start + row
        inside = jnp.logical_and(lat >= 0, lat < lats)
        line = line_of(jnp.clip(lat, 0, lats - 1))
        chosen = jnp.where(inside, matrix, 0.0).astype(BF16)
        pad_ref[row] = dot(chosen, line).astype(BF16).reshape(steps + 2, 16, line.shape[1])


def conv_block(pad_ref, weight_ref, start, rows, flipped):
    steps = pad_ref.shape[1] - 2
    chans = pad_ref.shape[3]
    pieces = []
    for a in range(3):
        for b in range(3):
            da, db = (2 - a, 2 - b) if flipped else (a, b)
            piece = pad_ref[pl.ds(start + da, rows), db : db + steps]
            pieces.append(piece.reshape(rows * steps * 16, chans))
    return dot(jnp.concatenate(pieces, axis=1), weight_ref[...].reshape(9 * chans, chans))


def whole_kernel(block, *refs):
    bands = refs[-2].shape[1]
    piece_refs, refs = refs[: 2 * bands], refs[2 * bands :]
    w1_ref, w2_ref, slope_ref, hidden_ref, state_ref, w2t_ref, pad_ref, all_ref, sems = refs
    _, _, half, rows, group, chans = all_ref.shape
    lats, lons = bands * rows, 2 * half * group
    steps = lons // 16
    size = block * lons
    mine = pad_ref.shape[0] - 4
    base = (lax.axis_index("lon") & 1) * mine
    copies = band_copies(bands, piece_refs, all_ref, sems)
    for copy in copies:
        copy.start()
    matrix = spread_matrix(steps, 2 * half)
    for tap in range(9):
        w2t_ref[tap] = w2_ref[tap].T
    for copy in copies:
        copy.wait()
    spread(
        lambda lat: all_ref[:, lat // rows, :, lat % rows].reshape(lons, chans),
        base - 2, lats, matrix, pad_ref,
    )

    def step(index, carry):
        start = index * block
        first = conv_block(pad_ref, w1_ref, start, block, False)
        sig, hidden = silu_parts(first)
        at = pl.ds(pl.multiple_of(index * size, size), size)
        slope_ref[at, :] = sig * (1.0 + first * (1.0 - sig))
        lat = base - 1 + start + lax.shift_right_logical(
            iota((size, chans), 0), lons.bit_length() - 1
        )
        hidden = jnp.where(jnp.logical_and(lat >= 0, lat < lats), hidden, 0.0)
        hidden_ref[:, at] = hidden.astype(BF16).T
        centre = pad_ref[pl.ds(start + 1, block), 1 : 1 + steps].reshape(size, chans)
        state_ref[:, at] = centre.T
        return carry

    lax.fori_loop(0, (mine + 2) // block, step, 0)


def whole(bands, pieces, w1, w2):
    half, rows, group, chans = pieces[0].shape
    lats, lons = bands * rows, 2 * half * group
    mine = lats // 2
    steps = lons // 16
    cells = (mine + 2) * lons
    return pl.pallas_call(
        functools.partial(whole_kernel, 3),
        out_shape=[
            jax.ShapeDtypeStruct((cells, chans), F32),
            jax.ShapeDtypeStruct((chans, cells), BF16),
            jax.ShapeDtypeStruct((chans, cells), BF16),
            jax.ShapeDtypeStruct((9, chans, chans), BF16),
        ],
        in_specs=[anywhere()] * len(pieces) + [vmem()] * 2,
        out_specs=[vmem()] * 4,
        scratch_shapes=[
            pltpu.VMEM((mine + 4, steps + 2, 16, chans), BF16),
            pltpu.VMEM((2, bands) + pieces[0].shape, BF16),
            pltpu.SemaphoreType.DMA((bands, 2)),
        ],
        compiler_params=params(28),
        cost_estimate=cost(6e9, 10e6),
        name="whole",
    )(*pieces, w1, w2)


def tap_sums(turned_ref, pad_ref, first_row, rows, sum_ref, out_ref, sem):
    steps = pad_ref.shape[1] - 2
    chans = pad_ref.shape[3]
    lons = steps * 16

    def step(tap, carry):
        a, b = tap // 3, tap % 3
        piece = pad_ref[first_row : first_row + rows, pl.ds(2 - b, steps)]
        at = pl.ds(pl.multiple_of(a * lons, lons), rows * lons)
        sum_ref[tap] = dot(turned_ref[:, at], piece.reshape(rows * lons, chans))
        pltpu.make_async_copy(sum_ref.at[tap], out_ref.at[tap], sem.at[tap]).start()
        return carry

    lax.fori_loop(0, 9, step, 0)


def tail_kernel(block, *refs):
    bands = (len(refs) - 18) // 2
    piece_refs, refs = refs[: 2 * bands], refs[2 * bands :]
    slope_hbm, hidden_hbm, state_hbm, w2t_ref, g1_hbm, g2_hbm = refs[:6]
    all_ref, pull_ref, first_ref, slope_ref, hidden_ref, state_ref, g1_ref, g2_ref = refs[6:14]
    piece_sems, big_sems, g1_sems, g2_sems = refs[14:]
    steps = pull_ref.shape[1] - 2
    chans = pull_ref.shape[3]
    lons = steps * 16
    size = block * lons
    _, bands, half, rows, cols, _ = all_ref.shape
    lats = bands * rows
    mine = lats // 2
    base = (lax.axis_index("lon") & 1) * mine
    copies = band_copies(bands, piece_refs, all_ref, piece_sems)
    hidden_copy = pltpu.make_async_copy(hidden_hbm, hidden_ref, big_sems.at[0])
    slope_copy = pltpu.make_async_copy(
        slope_hbm.at[pl.ds(lons, mine * lons), :], slope_ref, big_sems.at[1]
    )
    state_copy = pltpu.make_async_copy(state_hbm, state_ref, big_sems.at[2])
    for copy in copies:
        copy.start()
    hidden_copy.start()
    slope_copy.start()
    state_copy.start()
    matrix = spread_matrix(steps, 2 * half)
    for copy in copies:
        copy.wait()
    spread(
        lambda lat: all_ref[:, lat // rows, :, lat % rows].reshape(lons, chans),
        base - 1, lats, matrix, pull_ref,
    )
    hidden_copy.wait()
    tap_sums(hidden_ref, pull_ref, 1, mine, g2_ref, g2_hbm, g2_sems)
    slope_copy.wait()

    def step(index, carry):
        start = index * block
        back = conv_block(pull_ref, w2t_ref, start, block, True)
        at = pl.ds(pl.multiple_of(index * size, size), size)
        pull = (back * slope_ref[at, :]).astype(BF16).astype(F32)
        pull = pull.reshape(block, steps, 16, chans)
        last, head = pull[:, steps - 1], pull[:, 0]
        before = jnp.concatenate([last[:, 15:], last[:, :15]], axis=1)
        after = jnp.concatenate([head[:, 1:], head[:, :1]], axis=1)
        to = pl.ds(start, block)
        first_ref[to, 1 : 1 + steps] = pull.astype(BF16)
        first_ref[to, 0] = before.astype(BF16)
        first_ref[to, steps + 1] = after.astype(BF16)
        return carry

    lax.fori_loop(0, mine // block, step, 0)
    state_copy.wait()
    tap_sums(state_ref, first_ref, 0, mine, g1_ref, g1_hbm, g1_sems)
    for tap in range(9):
        pltpu.make_async_copy(g2_ref.at[tap], g2_hbm.at[tap], g2_sems.at[tap]).wait()
        pltpu.make_async_copy(g1_ref.at[tap], g1_hbm.at[tap], g1_sems.at[tap]).wait()


def tail(bands, pieces, slope, hidden, state, w2t):
    half, rows, group, chans = pieces[0].shape
    lats, lons = bands * rows, 2 * half * group
    steps = lons // 16
    ours = lats // 2
    return pl.pallas_call(
        functools.partial(tail_kernel, 4),
        out_shape=[jax.ShapeDtypeStruct((9, chans, chans), F32)] * 2,
        in_specs=[anywhere()] * (len(pieces) + 3) + [vmem()],
        out_specs=[anywhere()] * 2,
        scratch_shapes=[
            pltpu.VMEM((2, bands) + pieces[0].shape, BF16),
            pltpu.VMEM((ours + 2, steps + 2, 16, chans), BF16),
            pltpu.VMEM((ours, steps + 2, 16, chans), BF16),
            pltpu.VMEM((ours * lons, chans), F32),
            pltpu.VMEM(hidden.shape, BF16),
            pltpu.VMEM(state.shape, BF16),
            pltpu.VMEM((9, chans, chans), F32),
            pltpu.VMEM((9, chans, chans), F32),
            pltpu.SemaphoreType.DMA((bands, 2)),
            pltpu.SemaphoreType.DMA((3,)),
            pltpu.SemaphoreType.DMA((9,)),
            pltpu.SemaphoreType.DMA((9,)),
        ],
        compiler_params=params(36),
        cost_estimate=cost(10e9, 15e6),
        name="tail",
    )(*pieces, slope, hidden, state, w2t)


def local_kernel(bands, *refs):
    piece_refs, refs = refs[: 2 * bands], refs[2 * bands :]
    slope_ref, adj_ref, w1_ref, w2_ref, grad_ref = refs[:5]
    near_ref, line_ref, shift_ref, pull_ref, sems = refs[5:]
    rows, cols, chans = near_ref.shape[2:]
    span = pull_ref.shape[1]
    copies = nearby_copies(bands, piece_refs, near_ref, sems)
    for copy in copies:
        copy.start()
    for copy in copies:
        copy.wait()
    fill_line(bands, near_ref, line_ref)
    back = jnp.zeros(((rows + 2) * span, chans), F32)
    for b in range(3):
        shift_ref[...] = (
            line_ref[:, 2 - b : 2 - b + span, :].astype(BF16).reshape((rows + 4) * span, chans)
        )
        for a in range(3):
            piece = shift_ref[(2 - a) * span : (2 - a) * span + (rows + 2) * span, :]
            back = back + dot_nt(piece, w2_ref[3 * a + b])
    pull = (back * slope_ref[...]).reshape(rows + 2, span, chans)
    pull_ref[...] = jnp.where(inside_grid(rows, pull.shape, bands), pull, 0.0)
    total = adj_ref[...]
    for b in range(3):
        shift_ref[0 : (rows + 2) * cols, :] = (
            pull_ref[:, 2 - b : 2 - b + cols, :].astype(BF16).reshape((rows + 2) * cols, chans)
        )
        for a in range(3):
            piece = shift_ref[(2 - a) * cols : (2 - a) * cols + rows * cols, :]
            total = total + dot_nt(piece, w1_ref[3 * a + b])
    grad_ref[...] = total


def local_grad(bands, pieces, slope, adjoint, w1, w2):
    half, rows, cols, chans = pieces[0].shape
    return pl.pallas_call(
        functools.partial(local_kernel, bands),
        out_shape=jax.ShapeDtypeStruct((rows * cols, chans), F32),
        in_specs=[anywhere()] * len(pieces) + [vmem()] * 4,
        out_specs=vmem(),
        scratch_shapes=[
            pltpu.VMEM((3, 3, rows, cols, chans), BF16),
            pltpu.VMEM((rows + 4, SPAN + 8, chans), F32),
            pltpu.VMEM(((rows + 4) * SPAN, chans), BF16),
            pltpu.VMEM((rows + 2, SPAN, chans), F32),
            pltpu.SemaphoreType.DMA((3, 3)),
        ],
        compiler_params=params(16),
        cost_estimate=cost(3e9, 4e6),
        name="local_grad",
    )(*pieces, slope, adjoint, w1, w2)


def with_halo(x, sides, width, wrap):
    for axis, dim in sides:
        count, length = (lax.axis_size(axis), x.shape[dim])
        up = [(i, (i + 1) % count) for i in range(count if wrap else count - 1)]
        down = [(j, i) for i, j in up]
        last = lax.slice_in_dim(x, length - width, length, axis=dim)
        first = lax.slice_in_dim(x, 0, width, axis=dim)
        before = lax.ppermute(last, axis, up)
        after = lax.ppermute(first, axis, down)
        x = jnp.concatenate([before, x, after], axis=dim)
    return x


def widen_tile(field):
    across = with_halo(field, (("lon", 1),), 1, True)
    return with_halo(across, (("lat", 0),), 1, False)


def tile_conv(padded, weight, rows, cols, flipped):
    total = jnp.zeros((rows * cols, weight.shape[2]), jnp.float32)
    for first_tap in range(3):
        for second_tap in range(3):
            if flipped:
                piece = padded[
                    2 - first_tap : 2 - first_tap + rows, 2 - second_tap : 2 - second_tap + cols
                ]
                total = total + lax.dot_general(
                    piece.reshape(rows * cols, -1),
                    weight[3 * first_tap + second_tap],
                    (((1,), (1,)), ((), ())),
                    preferred_element_type=jnp.float32,
                )
            else:
                piece = padded[first_tap : first_tap + rows, second_tap : second_tap + cols]
                total = total + jnp.dot(
                    piece.reshape(rows * cols, -1),
                    weight[3 * first_tap + second_tap],
                    preferred_element_type=jnp.float32,
                )
    return total.reshape(rows, cols, -1)


def tile_grads(padded, pullback, rows, cols):
    flat_pull = pullback.reshape(rows * cols, -1)
    result = []
    for first_tap in range(3):
        for second_tap in range(3):
            piece = padded[first_tap : first_tap + rows, second_tap : second_tap + cols].reshape(
                rows * cols, -1
            )
            result.append(
                lax.dot_general(
                    piece, flat_pull, (((0,), (0,)), ((), ())), preferred_element_type=jnp.float32
                )
            )
    return jnp.stack(result)


def route_blocks(obs_owner, obs_cell, obs_level, obs_count, obs_frac, obs_value, obs_weight):
    devices = lax.axis_size(("lat", "lon"))
    blocks, width = obs_value.shape
    slots = max(2, 3 * blocks // (2 * devices))
    owner = obs_owner[:, 0]
    order = lax.broadcasted_iota(jnp.int32, (blocks, blocks), 1) < lax.broadcasted_iota(
        jnp.int32, (blocks, blocks), 0
    )
    earlier = jnp.logical_and(owner[:, None] == owner[None, :], order)
    rank = jnp.sum(earlier.astype(jnp.int32), axis=1)
    target = owner * slots + rank
    valid = (lax.broadcasted_iota(jnp.int32, (blocks, width), 1) < obs_count[:, None]).astype(
        jnp.float32
    )
    packed = jnp.stack(
        [
            obs_frac[:, 0, :],
            obs_frac[:, 1, :],
            obs_value,
            obs_weight,
            obs_cell.astype(jnp.float32),
            obs_level.astype(jnp.float32),
            valid,
        ],
        axis=1,
    )
    outgoing = jnp.zeros((devices * slots, 7, width), jnp.float32).at[target].set(packed)
    return lax.all_to_all(outgoing, ("lat", "lon"), split_axis=0, concat_axis=0, tiled=True)


def observe(corrected, arrived, rows, cols, chans):
    fields = jnp.transpose(arrived, (1, 0, 2)).reshape(7, -1)
    row_total = fields.shape[1]
    span_rows = math.gcd(row_total, 1024)
    fields = jnp.transpose(fields.reshape(7, row_total // span_rows, span_rows), (1, 0, 2))
    grid = corrected.reshape(rows * cols, chans)
    cells = lax.broadcasted_iota(jnp.int32, (1, rows * cols), 1)
    levels = lax.broadcasted_iota(jnp.int32, (1, chans), 1)

    def advance(summed, portion):
        frac_lat = portion[0][:, None]
        frac_lon = portion[1][:, None]
        corner = portion[4].astype(jnp.int32)[:, None]
        level = portion[5].astype(jnp.int32)[:, None]
        weights = (1.0 - frac_lat) * (1.0 - frac_lon) * (cells == corner).astype(jnp.float32)
        weights = weights + (1.0 - frac_lat) * frac_lon * (cells == corner + 1).astype(jnp.float32)
        weights = weights + frac_lat * (1.0 - frac_lon) * (cells == corner + cols).astype(
            jnp.float32
        )
        weights = weights + frac_lat * frac_lon * (cells == corner + cols + 1).astype(jnp.float32)
        onehot = (levels == level).astype(jnp.float32)
        sampled = jnp.dot(
            weights, grid, precision=lax.Precision.HIGHEST, preferred_element_type=jnp.float32
        )
        predicted = jnp.sum(sampled * onehot, axis=1)
        misfit = portion[6] * portion[3] * (predicted - portion[2])
        summed = summed + lax.dot_general(
            weights,
            onehot * misfit[:, None],
            (((0,), (0,)), ((), ())),
            precision=lax.Precision.HIGHEST,
            preferred_element_type=jnp.float32,
        )
        return (summed, None)

    summed, unused = lax.scan(advance, jnp.zeros((rows * cols, chans), jnp.float32), fields)
    return summed.reshape(rows, cols, chans)


def by_tiles(
    state,
    weight_first,
    weight_second,
    obs_owner,
    obs_cell,
    obs_level,
    obs_count,
    obs_frac,
    obs_value,
    obs_weight,
):
    rows, cols, chans = state.shape
    wide_state = widen_tile(state)
    first = tile_conv(wide_state, weight_first, rows, cols, False)
    hidden = jax.nn.silu(first).astype(jnp.bfloat16)
    wide_hidden = widen_tile(hidden)
    corrected = state.astype(jnp.float32) + tile_conv(wide_hidden, weight_second, rows, cols, False)
    arrived = route_blocks(
        obs_owner, obs_cell, obs_level, obs_count, obs_frac, obs_value, obs_weight
    )
    adjoint = observe(corrected, arrived, rows, cols, chans)
    pullback = adjoint.astype(jnp.bfloat16)
    wide_pull = widen_tile(pullback)
    local_second = tile_grads(wide_hidden, pullback, rows, cols)
    back = tile_conv(wide_pull, weight_second, rows, cols, True)
    sig = jax.nn.sigmoid(first)
    pull_first = (back * sig * (1.0 + first * (1.0 - sig))).astype(jnp.bfloat16)
    wide_pull_first = widen_tile(pull_first)
    local_first = tile_grads(wide_state, pull_first, rows, cols)
    state_grad = adjoint + tile_conv(wide_pull_first, weight_first, rows, cols, True)
    grad_first, grad_second = lax.psum((local_first, local_second), ("lat", "lon"))
    return (state_grad, grad_first, grad_second)


def halo_pieces(x):
    bands, tiles = lax.axis_size("lat"), lax.axis_size("lon")
    rows, cols, _ = x.shape
    north = lax.ppermute(x[rows - 2 :], "lat", [(i, i + 1) for i in range(bands - 1)])
    south = lax.ppermute(x[:2], "lat", [(i + 1, i) for i in range(bands - 1)])
    last = jnp.concatenate([p[:, cols - 2 :] for p in (north, x, south)], axis=0)
    first = jnp.concatenate([p[:, :2] for p in (north, x, south)], axis=0)
    west = lax.ppermute(last, "lon", [(i, (i + 1) % tiles) for i in range(tiles)])
    east = lax.ppermute(first, "lon", [((i + 1) % tiles, i) for i in range(tiles)])
    return x, north, south, west, east


def gather_line(x):
    tiles = lax.axis_size("lon")
    half = tiles // 2
    same = [[2 * q + core for q in range(half)] for core in range(2)]
    copies = jnp.broadcast_to(x[None], (half,) + x.shape)
    return lax.all_to_all(copies, "lon", 0, 0, axis_index_groups=same, tiled=True)


def gather_bands(line):
    bands = lax.axis_size("lat")
    return [line] + [
        lax.ppermute(line, "lat", [(i, (i + step) % bands) for i in range(bands)])
        for step in range(1, bands)
    ]


def with_other_core(lines):
    swap = [(i, i ^ 1) for i in range(lax.axis_size("lon"))]
    pieces = []
    for line in lines:
        pieces += [line, lax.ppermute(line, "lon", swap)]
    return pieces


def per_device(
    state, weight_first, weight_second, obs_owner, obs_cell, obs_level, obs_count, obs_frac,
    obs_value, obs_weight,
):
    rows, cols, chans = state.shape
    bands = lax.axis_size("lat")
    devices = lax.axis_size(("lat", "lon"))
    if devices * rows * cols > WHOLE_CELLS:
        return by_tiles(
            state, weight_first, weight_second, obs_owner, obs_cell, obs_level, obs_count,
            obs_frac, obs_value, obs_weight,
        )
    slots = max(2, 3 * obs_value.shape[0] // (2 * devices))
    outgoing = route(
        devices, slots, chans, obs_owner, obs_cell, obs_level, obs_count, obs_frac, obs_value,
        obs_weight,
    )
    pieces = halo_pieces(state)
    got = lax.all_to_all(outgoing, ("lat", "lon"), split_axis=0, concat_axis=0, tiled=True)
    pieces, got, sent = lax.optimization_barrier((pieces, got, state))
    line = gather_line(sent)
    line, pieces, got = lax.optimization_barrier((line, pieces, got))
    state_lines = gather_bands(line)
    adjoint, pullback, near_slope = forward(
        slots, bands, pieces, weight_first, weight_second, got
    )
    state_lines, pullback = lax.optimization_barrier((state_lines, pullback))
    state_pieces = with_other_core(state_lines)
    pull_lines = gather_bands(gather_line(pullback.reshape(rows, cols, chans)))
    firsts = whole(bands, state_pieces, weight_first, weight_second)
    pull_lines, firsts = lax.optimization_barrier((pull_lines, firsts))
    slope, hidden, turned, w2t = firsts
    pull_pieces = with_other_core(pull_lines)
    sums = tail(bands, pull_pieces, slope, hidden, turned, w2t)
    swap = [(i, i ^ 1) for i in range(lax.axis_size("lon"))]
    theirs = [lax.ppermute(part, "lon", swap) for part in sums]
    grad = local_grad(bands, pull_pieces, near_slope, adjoint, weight_first, weight_second)
    g1, g2 = [part + their for part, their in zip(sums, theirs)]
    return grad.reshape(rows, cols, chans), g1, g2


def solution(mesh):
    both = P(("lat", "lon"), None)
    placed = (
        P("lat", "lon", None),
        P(),
        P(),
        both,
        both,
        both,
        P(("lat", "lon")),
        P(("lat", "lon"), None, None),
        both,
        both,
    )
    return jax.shard_map(
        per_device,
        mesh=mesh,
        in_specs=placed,
        out_specs=(P("lat", "lon", None), P(), P()),
        check_vma=False,
    )
```

```python
import functools
import math

import jax
import jax.numpy as jnp
from jax import lax
from jax.experimental import pallas as pl
from jax.experimental.pallas import tpu as pltpu
from jax.sharding import PartitionSpec as P

F32 = jnp.float32
BF16 = jnp.bfloat16
FIELDS = 5
SPAN = 32
WHOLE_CELLS = 4096


def params(mebibytes):
    return pltpu.CompilerParams(vmem_limit_bytes=mebibytes * 1024 * 1024)


def cost(flops, moved):
    return pl.CostEstimate(flops=int(flops), bytes_accessed=int(moved), transcendentals=0)


def vmem():
    return pl.BlockSpec(memory_space=pltpu.VMEM)


def anywhere():
    return pl.BlockSpec(memory_space=pl.ANY)


def iota(shape, dim, dtype=jnp.int32):
    return lax.broadcasted_iota(jnp.int32, shape, dim).astype(dtype)


def dot(x, y, precision=None):
    return jnp.dot(x, y, precision=precision, preferred_element_type=F32)


def dot_nt(x, y, precision=None):
    return lax.dot_general(
        x, y, (((1,), (1,)), ((), ())), precision=precision, preferred_element_type=F32
    )


def slot_layout(slots):
    full, rest = divmod(slots, 4)
    rows = full * FIELDS + (0 if rest == 0 else -(-FIELDS // 2))
    return full, rest, -(-rows // 8) * 8


def route_kernel(
    devices, slots, chans, owner_ref, count_ref, cell_ref, level_ref, frac_ref, value_ref,
    weight_ref, out_ref
):
    width, blocks = value_ref.shape
    owner = owner_ref[...].astype(F32)
    across = jnp.broadcast_to(owner, (blocks, blocks))
    down = across.T
    earlier = iota((blocks, blocks), 0) < iota((blocks, blocks), 1)
    hits = jnp.where(jnp.logical_and(across == down, earlier), 1.0, 0.0)
    rank = jnp.sum(hits, axis=0, keepdims=True)
    target = rank * float(devices) + owner
    places = iota((slots * devices, blocks), 0, F32) == target
    onehot = jnp.where(places, 1.0, 0.0)
    valid = iota((width, blocks), 0) < count_ref[...]
    fields = jnp.concatenate(
        [
            frac_ref[0],
            frac_ref[1],
            value_ref[...],
            jnp.where(valid, weight_ref[...], 0.0),
            (cell_ref[...] * chans + level_ref[...]).astype(F32),
        ],
        axis=0,
    )
    placed = dot_nt(onehot, fields, lax.Precision.HIGHEST)
    full, rest, rows = slot_layout(slots)
    out_ref[...] = jnp.zeros(out_ref.shape, F32)
    for slot in range(slots):
        for field in range(FIELDS):
            piece = placed[
                slot * devices : (slot + 1) * devices, field * width : (field + 1) * width
            ]
            if slot < 4 * full:
                row, lane = (slot // 4) * FIELDS + field, (slot % 4) * width
            else:
                row = full * FIELDS + field // 2
                lane = (field % 2) * 2 * width + (slot - 4 * full) * width
            out_ref[:, row, lane : lane + width] = piece


def route(devices, slots, chans, obs_owner, obs_cell, obs_level, obs_count, obs_frac, obs_value,
          obs_weight):
    blocks = obs_value.shape[0]
    rows = slot_layout(slots)[2]
    return pl.pallas_call(
        functools.partial(route_kernel, devices, slots, chans),
        out_shape=jax.ShapeDtypeStruct((devices, rows, 128), F32),
        in_specs=[vmem()] * 7,
        out_specs=vmem(),
        compiler_params=params(60),
        name="route",
    )(
        obs_owner.reshape(1, blocks),
        obs_count.reshape(1, blocks),
        obs_cell.T,
        obs_level.T,
        jnp.transpose(obs_frac, (1, 2, 0)),
        obs_value.T,
        obs_weight.T,
    )


def silu_parts(first):
    sig = 1.0 / (1.0 + jnp.exp(-first))
    return sig, first * sig


def inside_grid(rows, shape, bands):
    lat = lax.axis_index("lat") * rows + iota(shape, 0) - 1
    return jnp.logical_and(lat >= 0, lat < bands * rows)


def band_copies(bands, piece_refs, all_ref, sems):
    core = lax.axis_index("lon") & 1
    lat = lax.axis_index("lat")
    copies = []
    for offset in range(bands):
        band = (lat + bands - offset) % bands
        for side in range(2):
            copies.append(
                pltpu.make_async_copy(
                    piece_refs[2 * offset + side],
                    all_ref.at[core if side == 0 else 1 - core, band],
                    sems.at[offset, side],
                )
            )
    return copies


def nearby_copies(bands, piece_refs, near_ref, sems):
    half = piece_refs[0].shape[0]
    lon = lax.axis_index("lon")
    west = lax.shift_right_logical((lon + 2 * half - 1) & (2 * half - 1), 1)
    east = lax.shift_right_logical((lon + 1) & (2 * half - 1), 1)
    here = lax.shift_right_logical(lon, 1)
    copies = []
    for down, offset in enumerate((1, 0, bands - 1)):
        mine, other = piece_refs[2 * offset], piece_refs[2 * offset + 1]
        for over, (source, q) in enumerate(((other, west), (mine, here), (other, east))):
            copies.append(
                pltpu.make_async_copy(source.at[q], near_ref.at[down, over], sems.at[down, over])
            )
    return copies


def fill_line(bands, near_ref, line_ref):
    rows, cols, chans = near_ref.shape[2:]
    lat = lax.axis_index("lat")
    for down, (y, height, first) in enumerate(((0, 2, rows - 2), (2, rows, 0), (2 + rows, 2, 0))):
        band = lat + down - 1
        for over, (x, width, left) in enumerate(((0, 2, cols - 2), (2, cols, 0), (2 + cols, 2, 0))):
            part = near_ref[down, over].astype(F32)[
                first : first + height, left : left + width
            ]
            if down != 1:
                part = jnp.where(jnp.logical_and(band >= 0, band < bands), part, 0.0)
            line_ref[y : y + height, x : x + width, :] = part
    line_ref[:, cols + 4 :, :] = jnp.zeros(
        (rows + 4, line_ref.shape[1] - cols - 4, chans), F32
    )


def forward_kernel(slots, bands, group, parts, tile_ref, north_ref, south_ref, west_ref, east_ref,
                   w1_hbm, w2_hbm, got_ref, adj_ref, pull_ref, slope_ref, line_ref, shift_ref,
                   hid_ref, obs_ref, sum_ref, w1_ref, w2_ref, sems):
    w1_copy = pltpu.make_async_copy(w1_hbm, w1_ref, sems.at[0])
    w2_copy = pltpu.make_async_copy(w2_hbm, w2_ref, sems.at[1])
    w1_copy.start()
    w2_copy.start()
    rows, cols, chans = tile_ref.shape
    span = hid_ref.shape[1]
    line_ref[0:2, 2 : 2 + cols, :] = north_ref[...].astype(F32)
    line_ref[2 : 2 + rows, 2 : 2 + cols, :] = tile_ref[...].astype(F32)
    line_ref[2 + rows :, 2 : 2 + cols, :] = south_ref[...].astype(F32)
    line_ref[:, 0:2, :] = west_ref[...].astype(F32)
    line_ref[:, 2 + cols : 4 + cols, :] = east_ref[...].astype(F32)
    line_ref[:, cols + 4 :, :] = jnp.zeros(
        (rows + 4, line_ref.shape[1] - cols - 4, chans), F32
    )
    w1_copy.wait()
    first = jnp.zeros(((rows + 2) * span, chans), F32)
    for b in range(3):
        shift_ref[...] = (
            line_ref[:, b : b + span, :].astype(BF16).reshape((rows + 4) * span, chans)
        )
        for a in range(3):
            first = first + dot(
                shift_ref[a * span : a * span + (rows + 2) * span, :], w1_ref[3 * a + b]
            )
    sig, hidden = silu_parts(first)
    slope_ref[...] = sig * (1.0 + first * (1.0 - sig))
    hidden = hidden.astype(BF16).astype(F32).reshape(rows + 2, span, chans)
    hidden = jnp.where(inside_grid(rows, hidden.shape, bands), hidden, 0.0)
    hid_ref[...] = hidden
    w2_copy.wait()
    total = line_ref[2 : 2 + rows, 2 : 2 + cols, :].reshape(rows * cols, chans)
    for b in range(3):
        shift_ref[0 : (rows + 2) * cols, :] = (
            hid_ref[:, b : b + cols, :].astype(BF16).reshape((rows + 2) * cols, chans)
        )
        for a in range(3):
            total = total + dot(
                shift_ref[a * cols : a * cols + rows * cols, :], w2_ref[3 * a + b]
            )
    cells = rows * cols
    turned = total.T
    grid_high = turned.astype(BF16)
    grid_low = (turned - grid_high.astype(F32)).astype(BF16)
    grid_both = jnp.concatenate([grid_high, grid_low], axis=1)

    devices = got_ref.shape[0]
    full, rest, _ = slot_layout(slots)
    half = devices // 2
    for field in range(FIELDS):
        for part in range(full):
            obs_ref[field, part * devices : (part + 1) * devices, :] = got_ref[
                :, part * FIELDS + field, :
            ]
        if rest:
            tail = got_ref[:, full * FIELDS + field // 2, :]
            low, high = tail[:half], tail[half:]
            if field % 2 == 0:
                high = pltpu.roll(high, 64, 1)
            else:
                low = pltpu.roll(low, 64, 1)
            obs_ref[field, full * devices : full * devices + half, :] = jnp.where(
                iota((half, 128), 1) < 64, low, high
            )
    code = obs_ref[4].astype(jnp.int32)
    shift = chans.bit_length() - 1
    cell = lax.shift_right_logical(code, shift)
    obs_ref[4] = (code & (chans - 1)).astype(F32)
    obs_ref[0] = obs_ref[0] + lax.shift_right_logical(cell, 4).astype(F32)
    obs_ref[1] = obs_ref[1] + (cell & (cols - 1)).astype(F32)

    sum_ref[...] = jnp.zeros(sum_ref.shape, F32)
    count = obs_ref.shape[1] // (group * parts)
    row_ids = iota((rows, 128), 0, F32)
    col_ids = iota((cols, 128), 0, F32)
    level_ids = iota((chans, 128), 0, F32)

    def add_group(start):
        high, low, masks, marks = [], [], [], []
        for piece in range(group):
            mark = [obs_ref[field, pl.ds(start + piece, 1), :] for field in range(FIELDS)]
            up = jnp.maximum(0.0, 1.0 - jnp.abs(row_ids - mark[0]))
            along = jnp.maximum(0.0, 1.0 - jnp.abs(col_ids - mark[1]))
            weights = (up[:, None, :] * along[None, :, :]).reshape(cells, 128)
            weights_high = weights.astype(BF16)
            high.append(weights_high)
            low.append((weights - weights_high.astype(F32)).astype(BF16))
            masks.append(level_ids == mark[4])
            marks.append(mark)
        high = jnp.concatenate(high, axis=1)
        low = jnp.concatenate(low, axis=1)
        sampled = dot(grid_both, jnp.concatenate([high, high], axis=0)) + dot(grid_high, low)
        hot_high, hot_low = [], []
        for piece in range(group):
            mine = sampled[:, piece * 128 : (piece + 1) * 128]
            predicted = jnp.sum(jnp.where(masks[piece], mine, 0.0), axis=0, keepdims=True)
            misfit = marks[piece][3] * (predicted - marks[piece][2])
            misfit_high = misfit.astype(BF16).astype(F32)
            hot_high.append(jnp.where(masks[piece], misfit_high, 0.0).astype(BF16))
            hot_low.append(jnp.where(masks[piece], misfit - misfit_high, 0.0).astype(BF16))
        hot_high = jnp.concatenate(hot_high, axis=1)
        hot_low = jnp.concatenate(hot_low, axis=1)
        mixed = dot_nt(
            jnp.concatenate([hot_high, hot_low], axis=0), jnp.concatenate([high, low], axis=0)
        )
        return mixed[:chans, :cells] + (mixed[chans:, :cells] + mixed[:chans, cells:])

    def step(index, carry):
        total = sum_ref[...]
        for part in range(parts):
            total = total + add_group((index * parts + part) * group)
        sum_ref[...] = total
        return carry

    lax.fori_loop(0, count, step, 0)
    adjoint = sum_ref[...].T
    adj_ref[...] = adjoint
    pull_ref[...] = adjoint.astype(BF16)


def forward(slots, bands, pieces, w1, w2, got):
    rows, cols, chans = pieces[0].shape
    devices = got.shape[0]
    full, rest, _ = slot_layout(slots)
    groups = full * devices + (devices // 2 if rest else 0)
    return pl.pallas_call(
        functools.partial(forward_kernel, slots, bands, 2, 4),
        out_shape=[
            jax.ShapeDtypeStruct((rows * cols, chans), F32),
            jax.ShapeDtypeStruct((rows * cols, chans), BF16),
            jax.ShapeDtypeStruct(((rows + 2) * SPAN, chans), F32),
        ],
        in_specs=[vmem()] * 5 + [anywhere()] * 2 + [vmem()],
        out_specs=[vmem()] * 3,
        scratch_shapes=[
            pltpu.VMEM((rows + 4, SPAN + 8, chans), F32),
            pltpu.VMEM(((rows + 4) * SPAN, chans), BF16),
            pltpu.VMEM((rows + 2, SPAN, chans), F32),
            pltpu.VMEM((FIELDS, groups, 128), F32),
            pltpu.VMEM((chans, rows * cols), F32),
            pltpu.VMEM(w1.shape, BF16),
            pltpu.VMEM(w2.shape, BF16),
            pltpu.SemaphoreType.DMA((2,)),
        ],
        compiler_params=params(58),
        cost_estimate=cost(4e9, 4e6),
        name="forward",
    )(*pieces, w1, w2, got)


def spread_matrix(steps, tiles, backwards):
    lons = 16 * steps
    half = tiles // 2
    place = iota(((steps + 2) * 16, lons), 0)
    lon = (place & 15) * steps + lax.shift_right_logical(place, 4) - 1
    lon = jnp.where(lon < 0, lon + lons, jnp.where(lon >= lons, lon - lons, lon))
    column = iota(((steps + 2) * 16, lons), 1)
    chunk = lax.shift_right_logical(column, 4)
    core = lax.shift_right_logical(chunk, half.bit_length() - 1)
    here = lax.shift_right_logical(lax.axis_index("lon"), 1)
    q = chunk & (half - 1)
    if backwards:
        q = (here - q) & (half - 1)
    column = (2 * q + core) * 16 + (column & 15)
    return jnp.where(column == lon, 1.0, 0.0)


def spread(line_of, start, lats, matrix, pad_ref):
    steps = pad_ref.shape[1] - 2
    for row in range(pad_ref.shape[0]):
        lat = start + row
        inside = jnp.logical_and(lat >= 0, lat < lats)
        line = line_of(jnp.clip(lat, 0, lats - 1))
        chosen = jnp.where(inside, matrix, 0.0).astype(BF16)
        pad_ref[row] = dot(chosen, line).astype(BF16).reshape(steps + 2, 16, line.shape[1])


def conv_block(pad_ref, weight_ref, start, rows, flipped):
    steps = pad_ref.shape[1] - 2
    chans = pad_ref.shape[3]
    pieces = []
    for a in range(3):
        for b in range(3):
            da, db = (2 - a, 2 - b) if flipped else (a, b)
            piece = pad_ref[pl.ds(start + da, rows), db : db + steps]
            pieces.append(piece.reshape(rows * steps * 16, chans))
    return dot(jnp.concatenate(pieces, axis=1), weight_ref[...].reshape(9 * chans, chans))


def whole_kernel(block, *refs):
    bands = refs[-2].shape[1]
    piece_refs, refs = refs[: 2 * bands], refs[2 * bands :]
    w1_ref, w2_ref, slope_ref, hidden_ref, state_ref, w2t_ref, pad_ref, all_ref, sems = refs
    _, _, half, rows, group, chans = all_ref.shape
    lats, lons = bands * rows, 2 * half * group
    steps = lons // 16
    size = block * lons
    mine = pad_ref.shape[0] - 4
    base = (lax.axis_index("lon") & 1) * mine
    copies = band_copies(bands, piece_refs, all_ref, sems)
    for copy in copies:
        copy.start()
    matrix = spread_matrix(steps, 2 * half, True)
    for tap in range(9):
        w2t_ref[tap] = w2_ref[tap].T
    for copy in copies:
        copy.wait()
    spread(
        lambda lat: all_ref[:, lat // rows, :, lat % rows].reshape(lons, chans),
        base - 2, lats, matrix, pad_ref,
    )

    def step(index, carry):
        start = index * block
        first = conv_block(pad_ref, w1_ref, start, block, False)
        sig, hidden = silu_parts(first)
        at = pl.ds(pl.multiple_of(index * size, size), size)
        slope_ref[at, :] = sig * (1.0 + first * (1.0 - sig))
        lat = base - 1 + start + lax.shift_right_logical(
            iota((size, chans), 0), lons.bit_length() - 1
        )
        hidden = jnp.where(jnp.logical_and(lat >= 0, lat < lats), hidden, 0.0)
        hidden_ref[:, at] = hidden.astype(BF16).T
        centre = pad_ref[pl.ds(start + 1, block), 1 : 1 + steps].reshape(size, chans)
        state_ref[:, at] = centre.T
        return carry

    lax.fori_loop(0, (mine + 2) // block, step, 0)


def whole(bands, pieces, w1, w2):
    half, rows, group, chans = pieces[0].shape
    lats, lons = bands * rows, 2 * half * group
    mine = lats // 2
    steps = lons // 16
    cells = (mine + 2) * lons
    return pl.pallas_call(
        functools.partial(whole_kernel, 3),
        out_shape=[
            jax.ShapeDtypeStruct((cells, chans), F32),
            jax.ShapeDtypeStruct((chans, cells), BF16),
            jax.ShapeDtypeStruct((chans, cells), BF16),
            jax.ShapeDtypeStruct((9, chans, chans), BF16),
        ],
        in_specs=[anywhere()] * len(pieces) + [vmem()] * 2,
        out_specs=[vmem()] * 4,
        scratch_shapes=[
            pltpu.VMEM((mine + 4, steps + 2, 16, chans), BF16),
            pltpu.VMEM((2, bands) + pieces[0].shape, BF16),
            pltpu.SemaphoreType.DMA((bands, 2)),
        ],
        compiler_params=params(28),
        cost_estimate=cost(6e9, 10e6),
        name="whole",
    )(*pieces, w1, w2)


def tap_sums(turned_ref, pad_ref, first_row, rows, sum_ref, out_ref, sem):
    steps = pad_ref.shape[1] - 2
    chans = pad_ref.shape[3]
    lons = steps * 16

    def step(tap, carry):
        a, b = tap // 3, tap % 3
        piece = pad_ref[first_row : first_row + rows, pl.ds(2 - b, steps)]
        at = pl.ds(pl.multiple_of(a * lons, lons), rows * lons)
        sum_ref[tap] = dot(turned_ref[:, at], piece.reshape(rows * lons, chans))
        pltpu.make_async_copy(sum_ref.at[tap], out_ref.at[tap], sem.at[tap]).start()
        return carry

    lax.fori_loop(0, 9, step, 0)


def tail_kernel(block, *refs):
    bands = (len(refs) - 18) // 2
    piece_refs, refs = refs[: 2 * bands], refs[2 * bands :]
    slope_hbm, hidden_hbm, state_hbm, w2t_ref, g1_hbm, g2_hbm = refs[:6]
    all_ref, pull_ref, first_ref, slope_ref, hidden_ref, state_ref, g1_ref, g2_ref = refs[6:14]
    piece_sems, big_sems, g1_sems, g2_sems = refs[14:]
    steps = pull_ref.shape[1] - 2
    chans = pull_ref.shape[3]
    lons = steps * 16
    size = block * lons
    _, bands, half, rows, cols, _ = all_ref.shape
    lats = bands * rows
    mine = lats // 2
    base = (lax.axis_index("lon") & 1) * mine
    copies = band_copies(bands, piece_refs, all_ref, piece_sems)
    hidden_copy = pltpu.make_async_copy(hidden_hbm, hidden_ref, big_sems.at[0])
    slope_copy = pltpu.make_async_copy(
        slope_hbm.at[pl.ds(lons, mine * lons), :], slope_ref, big_sems.at[1]
    )
    state_copy = pltpu.make_async_copy(state_hbm, state_ref, big_sems.at[2])
    for copy in copies:
        copy.start()
    hidden_copy.start()
    slope_copy.start()
    state_copy.start()
    matrix = spread_matrix(steps, 2 * half, False)
    for copy in copies:
        copy.wait()
    spread(
        lambda lat: all_ref[:, lat // rows, :, lat % rows].reshape(lons, chans),
        base - 1, lats, matrix, pull_ref,
    )
    hidden_copy.wait()
    tap_sums(hidden_ref, pull_ref, 1, mine, g2_ref, g2_hbm, g2_sems)
    slope_copy.wait()

    def step(index, carry):
        start = index * block
        back = conv_block(pull_ref, w2t_ref, start, block, True)
        at = pl.ds(pl.multiple_of(index * size, size), size)
        pull = (back * slope_ref[at, :]).astype(BF16).astype(F32)
        pull = pull.reshape(block, steps, 16, chans)
        last, head = pull[:, steps - 1], pull[:, 0]
        before = jnp.concatenate([last[:, 15:], last[:, :15]], axis=1)
        after = jnp.concatenate([head[:, 1:], head[:, :1]], axis=1)
        to = pl.ds(start, block)
        first_ref[to, 1 : 1 + steps] = pull.astype(BF16)
        first_ref[to, 0] = before.astype(BF16)
        first_ref[to, steps + 1] = after.astype(BF16)
        return carry

    lax.fori_loop(0, mine // block, step, 0)
    state_copy.wait()
    tap_sums(state_ref, first_ref, 0, mine, g1_ref, g1_hbm, g1_sems)
    for tap in range(9):
        pltpu.make_async_copy(g2_ref.at[tap], g2_hbm.at[tap], g2_sems.at[tap]).wait()
        pltpu.make_async_copy(g1_ref.at[tap], g1_hbm.at[tap], g1_sems.at[tap]).wait()


def tail(bands, pieces, slope, hidden, state, w2t):
    half, rows, group, chans = pieces[0].shape
    lats, lons = bands * rows, 2 * half * group
    steps = lons // 16
    ours = lats // 2
    return pl.pallas_call(
        functools.partial(tail_kernel, 4),
        out_shape=[jax.ShapeDtypeStruct((9, chans, chans), F32)] * 2,
        in_specs=[anywhere()] * (len(pieces) + 3) + [vmem()],
        out_specs=[anywhere()] * 2,
        scratch_shapes=[
            pltpu.VMEM((2, bands) + pieces[0].shape, BF16),
            pltpu.VMEM((ours + 2, steps + 2, 16, chans), BF16),
            pltpu.VMEM((ours, steps + 2, 16, chans), BF16),
            pltpu.VMEM((ours * lons, chans), F32),
            pltpu.VMEM(hidden.shape, BF16),
            pltpu.VMEM(state.shape, BF16),
            pltpu.VMEM((9, chans, chans), F32),
            pltpu.VMEM((9, chans, chans), F32),
            pltpu.SemaphoreType.DMA((bands, 2)),
            pltpu.SemaphoreType.DMA((3,)),
            pltpu.SemaphoreType.DMA((9,)),
            pltpu.SemaphoreType.DMA((9,)),
        ],
        compiler_params=params(36),
        cost_estimate=cost(10e9, 15e6),
        name="tail",
    )(*pieces, slope, hidden, state, w2t)


def local_kernel(bands, *refs):
    piece_refs, refs = refs[: 2 * bands], refs[2 * bands :]
    slope_ref, adj_ref, w1_ref, w2_ref, grad_ref = refs[:5]
    near_ref, line_ref, shift_ref, pull_ref, sems = refs[5:]
    rows, cols, chans = near_ref.shape[2:]
    span = pull_ref.shape[1]
    copies = nearby_copies(bands, piece_refs, near_ref, sems)
    for copy in copies:
        copy.start()
    for copy in copies:
        copy.wait()
    fill_line(bands, near_ref, line_ref)
    back = jnp.zeros(((rows + 2) * span, chans), F32)
    for b in range(3):
        shift_ref[...] = (
            line_ref[:, 2 - b : 2 - b + span, :].astype(BF16).reshape((rows + 4) * span, chans)
        )
        for a in range(3):
            piece = shift_ref[(2 - a) * span : (2 - a) * span + (rows + 2) * span, :]
            back = back + dot_nt(piece, w2_ref[3 * a + b])
    pull = (back * slope_ref[...]).reshape(rows + 2, span, chans)
    pull_ref[...] = jnp.where(inside_grid(rows, pull.shape, bands), pull, 0.0)
    total = adj_ref[...]
    for b in range(3):
        shift_ref[0 : (rows + 2) * cols, :] = (
            pull_ref[:, 2 - b : 2 - b + cols, :].astype(BF16).reshape((rows + 2) * cols, chans)
        )
        for a in range(3):
            piece = shift_ref[(2 - a) * cols : (2 - a) * cols + rows * cols, :]
            total = total + dot_nt(piece, w1_ref[3 * a + b])
    grad_ref[...] = total


def local_grad(bands, pieces, slope, adjoint, w1, w2):
    half, rows, cols, chans = pieces[0].shape
    return pl.pallas_call(
        functools.partial(local_kernel, bands),
        out_shape=jax.ShapeDtypeStruct((rows * cols, chans), F32),
        in_specs=[anywhere()] * len(pieces) + [vmem()] * 4,
        out_specs=vmem(),
        scratch_shapes=[
            pltpu.VMEM((3, 3, rows, cols, chans), BF16),
            pltpu.VMEM((rows + 4, SPAN + 8, chans), F32),
            pltpu.VMEM(((rows + 4) * SPAN, chans), BF16),
            pltpu.VMEM((rows + 2, SPAN, chans), F32),
            pltpu.SemaphoreType.DMA((3, 3)),
        ],
        compiler_params=params(16),
        cost_estimate=cost(3e9, 4e6),
        name="local_grad",
    )(*pieces, slope, adjoint, w1, w2)


def with_halo(x, sides, width, wrap):
    for axis, dim in sides:
        count, length = (lax.axis_size(axis), x.shape[dim])
        up = [(i, (i + 1) % count) for i in range(count if wrap else count - 1)]
        down = [(j, i) for i, j in up]
        last = lax.slice_in_dim(x, length - width, length, axis=dim)
        first = lax.slice_in_dim(x, 0, width, axis=dim)
        before = lax.ppermute(last, axis, up)
        after = lax.ppermute(first, axis, down)
        x = jnp.concatenate([before, x, after], axis=dim)
    return x


def widen_tile(field):
    across = with_halo(field, (("lon", 1),), 1, True)
    return with_halo(across, (("lat", 0),), 1, False)


def tile_conv(padded, weight, rows, cols, flipped):
    total = jnp.zeros((rows * cols, weight.shape[2]), jnp.float32)
    for first_tap in range(3):
        for second_tap in range(3):
            if flipped:
                piece = padded[
                    2 - first_tap : 2 - first_tap + rows, 2 - second_tap : 2 - second_tap + cols
                ]
                total = total + lax.dot_general(
                    piece.reshape(rows * cols, -1),
                    weight[3 * first_tap + second_tap],
                    (((1,), (1,)), ((), ())),
                    preferred_element_type=jnp.float32,
                )
            else:
                piece = padded[first_tap : first_tap + rows, second_tap : second_tap + cols]
                total = total + jnp.dot(
                    piece.reshape(rows * cols, -1),
                    weight[3 * first_tap + second_tap],
                    preferred_element_type=jnp.float32,
                )
    return total.reshape(rows, cols, -1)


def tile_grads(padded, pullback, rows, cols):
    flat_pull = pullback.reshape(rows * cols, -1)
    result = []
    for first_tap in range(3):
        for second_tap in range(3):
            piece = padded[first_tap : first_tap + rows, second_tap : second_tap + cols].reshape(
                rows * cols, -1
            )
            result.append(
                lax.dot_general(
                    piece, flat_pull, (((0,), (0,)), ((), ())), preferred_element_type=jnp.float32
                )
            )
    return jnp.stack(result)


def route_blocks(obs_owner, obs_cell, obs_level, obs_count, obs_frac, obs_value, obs_weight):
    devices = lax.axis_size(("lat", "lon"))
    blocks, width = obs_value.shape
    slots = max(2, 3 * blocks // (2 * devices))
    owner = obs_owner[:, 0]
    order = lax.broadcasted_iota(jnp.int32, (blocks, blocks), 1) < lax.broadcasted_iota(
        jnp.int32, (blocks, blocks), 0
    )
    earlier = jnp.logical_and(owner[:, None] == owner[None, :], order)
    rank = jnp.sum(earlier.astype(jnp.int32), axis=1)
    target = owner * slots + rank
    valid = (lax.broadcasted_iota(jnp.int32, (blocks, width), 1) < obs_count[:, None]).astype(
        jnp.float32
    )
    packed = jnp.stack(
        [
            obs_frac[:, 0, :],
            obs_frac[:, 1, :],
            obs_value,
            obs_weight,
            obs_cell.astype(jnp.float32),
            obs_level.astype(jnp.float32),
            valid,
        ],
        axis=1,
    )
    outgoing = jnp.zeros((devices * slots, 7, width), jnp.float32).at[target].set(packed)
    return lax.all_to_all(outgoing, ("lat", "lon"), split_axis=0, concat_axis=0, tiled=True)


def observe(corrected, arrived, rows, cols, chans):
    fields = jnp.transpose(arrived, (1, 0, 2)).reshape(7, -1)
    row_total = fields.shape[1]
    span_rows = math.gcd(row_total, 1024)
    fields = jnp.transpose(fields.reshape(7, row_total // span_rows, span_rows), (1, 0, 2))
    grid = corrected.reshape(rows * cols, chans)
    cells = lax.broadcasted_iota(jnp.int32, (1, rows * cols), 1)
    levels = lax.broadcasted_iota(jnp.int32, (1, chans), 1)

    def advance(summed, portion):
        frac_lat = portion[0][:, None]
        frac_lon = portion[1][:, None]
        corner = portion[4].astype(jnp.int32)[:, None]
        level = portion[5].astype(jnp.int32)[:, None]
        weights = (1.0 - frac_lat) * (1.0 - frac_lon) * (cells == corner).astype(jnp.float32)
        weights = weights + (1.0 - frac_lat) * frac_lon * (cells == corner + 1).astype(jnp.float32)
        weights = weights + frac_lat * (1.0 - frac_lon) * (cells == corner + cols).astype(
            jnp.float32
        )
        weights = weights + frac_lat * frac_lon * (cells == corner + cols + 1).astype(jnp.float32)
        onehot = (levels == level).astype(jnp.float32)
        sampled = jnp.dot(
            weights, grid, precision=lax.Precision.HIGHEST, preferred_element_type=jnp.float32
        )
        predicted = jnp.sum(sampled * onehot, axis=1)
        misfit = portion[6] * portion[3] * (predicted - portion[2])
        summed = summed + lax.dot_general(
            weights,
            onehot * misfit[:, None],
            (((0,), (0,)), ((), ())),
            precision=lax.Precision.HIGHEST,
            preferred_element_type=jnp.float32,
        )
        return (summed, None)

    summed, unused = lax.scan(advance, jnp.zeros((rows * cols, chans), jnp.float32), fields)
    return summed.reshape(rows, cols, chans)


def by_tiles(
    state,
    weight_first,
    weight_second,
    obs_owner,
    obs_cell,
    obs_level,
    obs_count,
    obs_frac,
    obs_value,
    obs_weight,
):
    rows, cols, chans = state.shape
    wide_state = widen_tile(state)
    first = tile_conv(wide_state, weight_first, rows, cols, False)
    hidden = jax.nn.silu(first).astype(jnp.bfloat16)
    wide_hidden = widen_tile(hidden)
    corrected = state.astype(jnp.float32) + tile_conv(wide_hidden, weight_second, rows, cols, False)
    arrived = route_blocks(
        obs_owner, obs_cell, obs_level, obs_count, obs_frac, obs_value, obs_weight
    )
    adjoint = observe(corrected, arrived, rows, cols, chans)
    pullback = adjoint.astype(jnp.bfloat16)
    wide_pull = widen_tile(pullback)
    local_second = tile_grads(wide_hidden, pullback, rows, cols)
    back = tile_conv(wide_pull, weight_second, rows, cols, True)
    sig = jax.nn.sigmoid(first)
    pull_first = (back * sig * (1.0 + first * (1.0 - sig))).astype(jnp.bfloat16)
    wide_pull_first = widen_tile(pull_first)
    local_first = tile_grads(wide_state, pull_first, rows, cols)
    state_grad = adjoint + tile_conv(wide_pull_first, weight_first, rows, cols, True)
    grad_first, grad_second = lax.psum((local_first, local_second), ("lat", "lon"))
    return (state_grad, grad_first, grad_second)


def halo_pieces(x):
    bands, tiles = lax.axis_size("lat"), lax.axis_size("lon")
    rows, cols, _ = x.shape
    north = lax.ppermute(x[rows - 2 :], "lat", [(i, i + 1) for i in range(bands - 1)])
    south = lax.ppermute(x[:2], "lat", [(i + 1, i) for i in range(bands - 1)])
    last = jnp.concatenate([p[:, cols - 2 :] for p in (north, x, south)], axis=0)
    first = jnp.concatenate([p[:, :2] for p in (north, x, south)], axis=0)
    west = lax.ppermute(last, "lon", [(i, (i + 1) % tiles) for i in range(tiles)])
    east = lax.ppermute(first, "lon", [((i + 1) % tiles, i) for i in range(tiles)])
    return x, north, south, west, east


def gather_line(x):
    tiles = lax.axis_size("lon")
    half = tiles // 2
    same = [[2 * q + core for q in range(half)] for core in range(2)]
    copies = jnp.broadcast_to(x[None], (half,) + x.shape)
    return lax.all_to_all(copies, "lon", 0, 0, axis_index_groups=same, tiled=True)


def gather_line_backwards(x):
    tiles = lax.axis_size("lon")
    return jnp.stack(
        [x]
        + [
            lax.ppermute(x, "lon", [(i, (i + step) % tiles) for i in range(tiles)])
            for step in range(2, tiles, 2)
        ]
    )


def gather_bands(line):
    bands = lax.axis_size("lat")
    return [line] + [
        lax.ppermute(line, "lat", [(i, (i + step) % bands) for i in range(bands)])
        for step in range(1, bands)
    ]


def with_other_core(lines):
    swap = [(i, i ^ 1) for i in range(lax.axis_size("lon"))]
    pieces = []
    for line in lines:
        pieces += [line, lax.ppermute(line, "lon", swap)]
    return pieces


def per_device(
    state, weight_first, weight_second, obs_owner, obs_cell, obs_level, obs_count, obs_frac,
    obs_value, obs_weight,
):
    rows, cols, chans = state.shape
    bands = lax.axis_size("lat")
    devices = lax.axis_size(("lat", "lon"))
    if devices * rows * cols > WHOLE_CELLS:
        return by_tiles(
            state, weight_first, weight_second, obs_owner, obs_cell, obs_level, obs_count,
            obs_frac, obs_value, obs_weight,
        )
    slots = max(2, 3 * obs_value.shape[0] // (2 * devices))
    outgoing = route(
        devices, slots, chans, obs_owner, obs_cell, obs_level, obs_count, obs_frac, obs_value,
        obs_weight,
    )
    outgoing, sent = lax.optimization_barrier((outgoing, state))
    pieces = halo_pieces(state)
    got = lax.all_to_all(outgoing, ("lat", "lon"), split_axis=0, concat_axis=0, tiled=True)
    line = gather_line_backwards(sent)
    line, pieces, got = lax.optimization_barrier((line, pieces, got))
    state_lines = gather_bands(line)
    adjoint, pullback, near_slope = forward(
        slots, bands, pieces, weight_first, weight_second, got
    )
    state_lines, pullback = lax.optimization_barrier((state_lines, pullback))
    state_pieces = with_other_core(state_lines)
    pull_lines = gather_bands(gather_line(pullback.reshape(rows, cols, chans)))
    firsts = whole(bands, state_pieces, weight_first, weight_second)
    pull_lines, firsts = lax.optimization_barrier((pull_lines, firsts))
    slope, hidden, turned, w2t = firsts
    pull_pieces = with_other_core(pull_lines)
    sums = tail(bands, pull_pieces, slope, hidden, turned, w2t)
    swap = [(i, i ^ 1) for i in range(lax.axis_size("lon"))]
    theirs = [lax.ppermute(part, "lon", swap) for part in sums]
    grad = local_grad(bands, pull_pieces, near_slope, adjoint, weight_first, weight_second)
    g1, g2 = [part + their for part, their in zip(sums, theirs)]
    return grad.reshape(rows, cols, chans), g1, g2


def solution(mesh):
    both = P(("lat", "lon"), None)
    placed = (
        P("lat", "lon", None),
        P(),
        P(),
        both,
        both,
        both,
        P(("lat", "lon")),
        P(("lat", "lon"), None, None),
        both,
        both,
    )
    return jax.shard_map(
        per_device,
        mesh=mesh,
        in_specs=placed,
        out_specs=(P("lat", "lon", None), P(), P()),
        check_vma=False,
    )
```

```python
import functools
import math

import jax
import jax.numpy as jnp
from jax import lax
from jax.experimental import pallas as pl
from jax.experimental.pallas import tpu as pltpu
from jax.sharding import PartitionSpec as P

F32 = jnp.float32
BF16 = jnp.bfloat16
FIELDS = 5
SPAN = 32
WHOLE_CELLS = 4096


def params(mebibytes):
    return pltpu.CompilerParams(vmem_limit_bytes=mebibytes * 1024 * 1024)


def cost(flops, moved):
    return pl.CostEstimate(flops=int(flops), bytes_accessed=int(moved), transcendentals=0)


def vmem():
    return pl.BlockSpec(memory_space=pltpu.VMEM)


def anywhere():
    return pl.BlockSpec(memory_space=pl.ANY)


def iota(shape, dim, dtype=jnp.int32):
    return lax.broadcasted_iota(jnp.int32, shape, dim).astype(dtype)


def dot(x, y, precision=None):
    return jnp.dot(x, y, precision=precision, preferred_element_type=F32)


def dot_nt(x, y, precision=None):
    return lax.dot_general(
        x, y, (((1,), (1,)), ((), ())), precision=precision, preferred_element_type=F32
    )


def slot_layout(slots):
    full, rest = divmod(slots, 4)
    rows = full * FIELDS + (0 if rest == 0 else -(-FIELDS // 2))
    return full, rest, -(-rows // 8) * 8


def route_kernel(
    devices, slots, chans, owner_ref, count_ref, cell_ref, level_ref, frac_ref, value_ref,
    weight_ref, out_ref
):
    width, blocks = value_ref.shape
    owner = owner_ref[...].astype(F32)
    across = jnp.broadcast_to(owner, (blocks, blocks))
    down = across.T
    earlier = iota((blocks, blocks), 0) < iota((blocks, blocks), 1)
    hits = jnp.where(jnp.logical_and(across == down, earlier), 1.0, 0.0)
    rank = jnp.sum(hits, axis=0, keepdims=True)
    target = rank * float(devices) + owner
    places = iota((slots * devices, blocks), 0, F32) == target
    onehot = jnp.where(places, 1.0, 0.0)
    valid = iota((width, blocks), 0) < count_ref[...]
    fields = jnp.concatenate(
        [
            frac_ref[0],
            frac_ref[1],
            value_ref[...],
            jnp.where(valid, weight_ref[...], 0.0),
            (cell_ref[...] * chans + level_ref[...]).astype(F32),
        ],
        axis=0,
    )
    placed = dot_nt(onehot, fields, lax.Precision.HIGHEST)
    full, rest, rows = slot_layout(slots)
    out_ref[...] = jnp.zeros(out_ref.shape, F32)
    for slot in range(slots):
        for field in range(FIELDS):
            piece = placed[
                slot * devices : (slot + 1) * devices, field * width : (field + 1) * width
            ]
            if slot < 4 * full:
                row, lane = (slot // 4) * FIELDS + field, (slot % 4) * width
            else:
                row = full * FIELDS + field // 2
                lane = (field % 2) * 2 * width + (slot - 4 * full) * width
            out_ref[:, row, lane : lane + width] = piece


def route(devices, slots, chans, obs_owner, obs_cell, obs_level, obs_count, obs_frac, obs_value,
          obs_weight):
    blocks = obs_value.shape[0]
    rows = slot_layout(slots)[2]
    return pl.pallas_call(
        functools.partial(route_kernel, devices, slots, chans),
        out_shape=jax.ShapeDtypeStruct((devices, rows, 128), F32),
        in_specs=[vmem()] * 7,
        out_specs=vmem(),
        compiler_params=params(60),
        name="route",
    )(
        obs_owner.reshape(1, blocks),
        obs_count.reshape(1, blocks),
        obs_cell.T,
        obs_level.T,
        jnp.transpose(obs_frac, (1, 2, 0)),
        obs_value.T,
        obs_weight.T,
    )


def silu_parts(first):
    sig = 1.0 / (1.0 + jnp.exp(-first))
    return sig, first * sig


def inside_grid(rows, shape, bands):
    lat = lax.axis_index("lat") * rows + iota(shape, 0) - 1
    return jnp.logical_and(lat >= 0, lat < bands * rows)


def band_copies(bands, piece_refs, all_ref, sems):
    core = lax.axis_index("lon") & 1
    lat = lax.axis_index("lat")
    copies = []
    for offset in range(bands):
        band = (lat + bands - offset) % bands
        for side in range(2):
            copies.append(
                pltpu.make_async_copy(
                    piece_refs[2 * offset + side],
                    all_ref.at[core if side == 0 else 1 - core, band],
                    sems.at[offset, side],
                )
            )
    return copies


def nearby_copies(bands, piece_refs, near_ref, sems):
    half = piece_refs[0].shape[0]
    lon = lax.axis_index("lon")
    west = lax.shift_right_logical((lon + 2 * half - 1) & (2 * half - 1), 1)
    east = lax.shift_right_logical((lon + 1) & (2 * half - 1), 1)
    here = lax.shift_right_logical(lon, 1)
    copies = []
    for down, offset in enumerate((1, 0, bands - 1)):
        mine, other = piece_refs[2 * offset], piece_refs[2 * offset + 1]
        for over, (source, q) in enumerate(((other, west), (mine, here), (other, east))):
            copies.append(
                pltpu.make_async_copy(source.at[q], near_ref.at[down, over], sems.at[down, over])
            )
    return copies


def fill_line(bands, near_ref, line_ref):
    rows, cols, chans = near_ref.shape[2:]
    lat = lax.axis_index("lat")
    for down, (y, height, first) in enumerate(((0, 2, rows - 2), (2, rows, 0), (2 + rows, 2, 0))):
        band = lat + down - 1
        for over, (x, width, left) in enumerate(((0, 2, cols - 2), (2, cols, 0), (2 + cols, 2, 0))):
            part = near_ref[down, over].astype(F32)[
                first : first + height, left : left + width
            ]
            if down != 1:
                part = jnp.where(jnp.logical_and(band >= 0, band < bands), part, 0.0)
            line_ref[y : y + height, x : x + width, :] = part
    line_ref[:, cols + 4 :, :] = jnp.zeros(
        (rows + 4, line_ref.shape[1] - cols - 4, chans), F32
    )


def forward_kernel(slots, bands, group, parts, tile_ref, north_ref, south_ref, west_ref, east_ref,
                   w1_hbm, w2_hbm, got_ref, adj_ref, pull_ref, slope_ref, line_ref, shift_ref,
                   hid_ref, obs_ref, sum_ref, w1_ref, w2_ref, sems):
    w1_copy = pltpu.make_async_copy(w1_hbm, w1_ref, sems.at[0])
    w2_copy = pltpu.make_async_copy(w2_hbm, w2_ref, sems.at[1])
    w1_copy.start()
    w2_copy.start()
    rows, cols, chans = tile_ref.shape
    span = hid_ref.shape[1]
    line_ref[0:2, 2 : 2 + cols, :] = north_ref[...].astype(F32)
    line_ref[2 : 2 + rows, 2 : 2 + cols, :] = tile_ref[...].astype(F32)
    line_ref[2 + rows :, 2 : 2 + cols, :] = south_ref[...].astype(F32)
    line_ref[:, 0:2, :] = west_ref[...].astype(F32)
    line_ref[:, 2 + cols : 4 + cols, :] = east_ref[...].astype(F32)
    line_ref[:, cols + 4 :, :] = jnp.zeros(
        (rows + 4, line_ref.shape[1] - cols - 4, chans), F32
    )
    w1_copy.wait()
    first = jnp.zeros(((rows + 2) * span, chans), F32)
    for b in range(3):
        shift_ref[...] = (
            line_ref[:, b : b + span, :].astype(BF16).reshape((rows + 4) * span, chans)
        )
        for a in range(3):
            first = first + dot(
                shift_ref[a * span : a * span + (rows + 2) * span, :], w1_ref[3 * a + b]
            )
    sig, hidden = silu_parts(first)
    slope_ref[...] = sig * (1.0 + first * (1.0 - sig))
    hidden = hidden.astype(BF16).astype(F32).reshape(rows + 2, span, chans)
    hidden = jnp.where(inside_grid(rows, hidden.shape, bands), hidden, 0.0)
    hid_ref[...] = hidden
    w2_copy.wait()
    total = line_ref[2 : 2 + rows, 2 : 2 + cols, :].reshape(rows * cols, chans)
    for b in range(3):
        shift_ref[0 : (rows + 2) * cols, :] = (
            hid_ref[:, b : b + cols, :].astype(BF16).reshape((rows + 2) * cols, chans)
        )
        for a in range(3):
            total = total + dot(
                shift_ref[a * cols : a * cols + rows * cols, :], w2_ref[3 * a + b]
            )
    cells = rows * cols
    turned = total.T
    grid_high = turned.astype(BF16)
    grid_low = (turned - grid_high.astype(F32)).astype(BF16)
    grid_both = jnp.concatenate([grid_high, grid_low], axis=1)

    devices = got_ref.shape[0]
    full, rest, _ = slot_layout(slots)
    half = devices // 2
    for field in range(FIELDS):
        for part in range(full):
            obs_ref[field, part * devices : (part + 1) * devices, :] = got_ref[
                :, part * FIELDS + field, :
            ]
        if rest:
            tail = got_ref[:, full * FIELDS + field // 2, :]
            low, high = tail[:half], tail[half:]
            if field % 2 == 0:
                high = pltpu.roll(high, 64, 1)
            else:
                low = pltpu.roll(low, 64, 1)
            obs_ref[field, full * devices : full * devices + half, :] = jnp.where(
                iota((half, 128), 1) < 64, low, high
            )
    code = obs_ref[4].astype(jnp.int32)
    shift = chans.bit_length() - 1
    cell = lax.shift_right_logical(code, shift)
    obs_ref[4] = (code & (chans - 1)).astype(F32)
    obs_ref[0] = obs_ref[0] + lax.shift_right_logical(cell, 4).astype(F32)
    obs_ref[1] = obs_ref[1] + (cell & (cols - 1)).astype(F32)

    sum_ref[...] = jnp.zeros(sum_ref.shape, F32)
    count = obs_ref.shape[1] // (group * parts)
    row_ids = iota((rows, 128), 0, F32)
    col_ids = iota((cols, 128), 0, F32)
    level_ids = iota((chans, 128), 0, F32)

    def add_group(start):
        high, low, masks, marks = [], [], [], []
        for piece in range(group):
            mark = [obs_ref[field, pl.ds(start + piece, 1), :] for field in range(FIELDS)]
            up = jnp.maximum(0.0, 1.0 - jnp.abs(row_ids - mark[0]))
            along = jnp.maximum(0.0, 1.0 - jnp.abs(col_ids - mark[1]))
            weights = (up[:, None, :] * along[None, :, :]).reshape(cells, 128)
            weights_high = weights.astype(BF16)
            high.append(weights_high)
            low.append((weights - weights_high.astype(F32)).astype(BF16))
            masks.append(level_ids == mark[4])
            marks.append(mark)
        high = jnp.concatenate(high, axis=1)
        low = jnp.concatenate(low, axis=1)
        sampled = dot(grid_both, jnp.concatenate([high, high], axis=0)) + dot(grid_high, low)
        hot_high, hot_low = [], []
        for piece in range(group):
            mine = sampled[:, piece * 128 : (piece + 1) * 128]
            predicted = jnp.sum(jnp.where(masks[piece], mine, 0.0), axis=0, keepdims=True)
            misfit = marks[piece][3] * (predicted - marks[piece][2])
            misfit_high = misfit.astype(BF16).astype(F32)
            hot_high.append(jnp.where(masks[piece], misfit_high, 0.0).astype(BF16))
            hot_low.append(jnp.where(masks[piece], misfit - misfit_high, 0.0).astype(BF16))
        hot_high = jnp.concatenate(hot_high, axis=1)
        hot_low = jnp.concatenate(hot_low, axis=1)
        mixed = dot_nt(
            jnp.concatenate([hot_high, hot_low], axis=0), jnp.concatenate([high, low], axis=0)
        )
        return mixed[:chans, :cells] + (mixed[chans:, :cells] + mixed[:chans, cells:])

    def step(index, carry):
        total = sum_ref[...]
        for part in range(parts):
            total = total + add_group((index * parts + part) * group)
        sum_ref[...] = total
        return carry

    lax.fori_loop(0, count, step, 0)
    adjoint = sum_ref[...].T
    adj_ref[...] = adjoint
    for copy in range(pull_ref.shape[0]):
        pull_ref[copy] = adjoint.astype(BF16)


def forward(slots, bands, copies, pieces, w1, w2, got):
    rows, cols, chans = pieces[0].shape
    devices = got.shape[0]
    full, rest, _ = slot_layout(slots)
    groups = full * devices + (devices // 2 if rest else 0)
    return pl.pallas_call(
        functools.partial(forward_kernel, slots, bands, 2, 4),
        out_shape=[
            jax.ShapeDtypeStruct((rows * cols, chans), F32),
            jax.ShapeDtypeStruct((copies, rows * cols, chans), BF16),
            jax.ShapeDtypeStruct(((rows + 2) * SPAN, chans), F32),
        ],
        in_specs=[vmem()] * 5 + [anywhere()] * 2 + [vmem()],
        out_specs=[vmem()] * 3,
        scratch_shapes=[
            pltpu.VMEM((rows + 4, SPAN + 8, chans), F32),
            pltpu.VMEM(((rows + 4) * SPAN, chans), BF16),
            pltpu.VMEM((rows + 2, SPAN, chans), F32),
            pltpu.VMEM((FIELDS, groups, 128), F32),
            pltpu.VMEM((chans, rows * cols), F32),
            pltpu.VMEM(w1.shape, BF16),
            pltpu.VMEM(w2.shape, BF16),
            pltpu.SemaphoreType.DMA((2,)),
        ],
        compiler_params=params(58),
        cost_estimate=cost(4e9, 4e6),
        name="forward",
    )(*pieces, w1, w2, got)


def spread_matrix(steps, tiles, backwards):
    lons = 16 * steps
    half = tiles // 2
    place = iota(((steps + 2) * 16, lons), 0)
    lon = (place & 15) * steps + lax.shift_right_logical(place, 4) - 1
    lon = jnp.where(lon < 0, lon + lons, jnp.where(lon >= lons, lon - lons, lon))
    column = iota(((steps + 2) * 16, lons), 1)
    chunk = lax.shift_right_logical(column, 4)
    core = lax.shift_right_logical(chunk, half.bit_length() - 1)
    here = lax.shift_right_logical(lax.axis_index("lon"), 1)
    q = chunk & (half - 1)
    if backwards:
        q = (here - q) & (half - 1)
    column = (2 * q + core) * 16 + (column & 15)
    return jnp.where(column == lon, 1.0, 0.0)


def spread(line_of, start, lats, matrix, pad_ref):
    steps = pad_ref.shape[1] - 2
    for row in range(pad_ref.shape[0]):
        lat = start + row
        inside = jnp.logical_and(lat >= 0, lat < lats)
        line = line_of(jnp.clip(lat, 0, lats - 1))
        chosen = jnp.where(inside, matrix, 0.0).astype(BF16)
        pad_ref[row] = dot(chosen, line).astype(BF16).reshape(steps + 2, 16, line.shape[1])


def conv_block(pad_ref, weight_ref, start, rows, flipped):
    steps = pad_ref.shape[1] - 2
    chans = pad_ref.shape[3]
    pieces = []
    for a in range(3):
        for b in range(3):
            da, db = (2 - a, 2 - b) if flipped else (a, b)
            piece = pad_ref[pl.ds(start + da, rows), db : db + steps]
            pieces.append(piece.reshape(rows * steps * 16, chans))
    return dot(jnp.concatenate(pieces, axis=1), weight_ref[...].reshape(9 * chans, chans))


def whole_kernel(block, *refs):
    bands = refs[-2].shape[1]
    piece_refs, refs = refs[: 2 * bands], refs[2 * bands :]
    w1_ref, w2_ref, slope_ref, hidden_ref, state_ref, w2t_ref, pad_ref, all_ref, sems = refs
    _, _, half, rows, group, chans = all_ref.shape
    lats, lons = bands * rows, 2 * half * group
    steps = lons // 16
    size = block * lons
    mine = pad_ref.shape[0] - 4
    base = (lax.axis_index("lon") & 1) * mine
    copies = band_copies(bands, piece_refs, all_ref, sems)
    for copy in copies:
        copy.start()
    matrix = spread_matrix(steps, 2 * half, True)
    for tap in range(9):
        w2t_ref[tap] = w2_ref[tap].T
    for copy in copies:
        copy.wait()
    spread(
        lambda lat: all_ref[:, lat // rows, :, lat % rows].reshape(lons, chans),
        base - 2, lats, matrix, pad_ref,
    )

    def step(index, carry):
        start = index * block
        first = conv_block(pad_ref, w1_ref, start, block, False)
        sig, hidden = silu_parts(first)
        at = pl.ds(pl.multiple_of(index * size, size), size)
        slope_ref[at, :] = sig * (1.0 + first * (1.0 - sig))
        lat = base - 1 + start + lax.shift_right_logical(
            iota((size, chans), 0), lons.bit_length() - 1
        )
        hidden = jnp.where(jnp.logical_and(lat >= 0, lat < lats), hidden, 0.0)
        hidden_ref[:, at] = hidden.astype(BF16).T
        centre = pad_ref[pl.ds(start + 1, block), 1 : 1 + steps].reshape(size, chans)
        state_ref[:, at] = centre.T
        return carry

    lax.fori_loop(0, (mine + 2) // block, step, 0)


def whole(bands, pieces, w1, w2):
    half, rows, group, chans = pieces[0].shape
    lats, lons = bands * rows, 2 * half * group
    mine = lats // 2
    steps = lons // 16
    cells = (mine + 2) * lons
    return pl.pallas_call(
        functools.partial(whole_kernel, 3),
        out_shape=[
            jax.ShapeDtypeStruct((cells, chans), F32),
            jax.ShapeDtypeStruct((chans, cells), BF16),
            jax.ShapeDtypeStruct((chans, cells), BF16),
            jax.ShapeDtypeStruct((9, chans, chans), BF16),
        ],
        in_specs=[anywhere()] * len(pieces) + [vmem()] * 2,
        out_specs=[vmem()] * 4,
        scratch_shapes=[
            pltpu.VMEM((mine + 4, steps + 2, 16, chans), BF16),
            pltpu.VMEM((2, bands) + pieces[0].shape, BF16),
            pltpu.SemaphoreType.DMA((bands, 2)),
        ],
        compiler_params=params(22),
        cost_estimate=cost(6e9, 10e6),
        name="whole",
    )(*pieces, w1, w2)


def tap_sums(turned_ref, pad_ref, first_row, rows, sum_ref, out_ref, sem):
    steps = pad_ref.shape[1] - 2
    chans = pad_ref.shape[3]
    lons = steps * 16

    def step(tap, carry):
        a, b = tap // 3, tap % 3
        piece = pad_ref[first_row : first_row + rows, pl.ds(2 - b, steps)]
        at = pl.ds(pl.multiple_of(a * lons, lons), rows * lons)
        sum_ref[tap] = dot(turned_ref[:, at], piece.reshape(rows * lons, chans))
        pltpu.make_async_copy(sum_ref.at[tap], out_ref.at[tap], sem.at[tap]).start()
        return carry

    lax.fori_loop(0, 9, step, 0)


def second_kernel(bands, *refs):
    piece_refs, refs = refs[: 2 * bands], refs[2 * bands :]
    hidden_hbm, g2_hbm, pull_ref, all_ref, hidden_ref, g2_ref, piece_sems, sem, g2_sems = refs
    steps = pull_ref.shape[1] - 2
    chans = pull_ref.shape[3]
    lons = steps * 16
    _, _, half, rows, _, _ = all_ref.shape
    lats = bands * rows
    mine = lats // 2
    base = (lax.axis_index("lon") & 1) * mine
    copies = band_copies(bands, piece_refs, all_ref, piece_sems)
    hidden_copy = pltpu.make_async_copy(hidden_hbm, hidden_ref, sem)
    for copy in copies:
        copy.start()
    hidden_copy.start()
    matrix = spread_matrix(steps, 2 * half, False)
    for copy in copies:
        copy.wait()
    spread(
        lambda lat: all_ref[:, lat // rows, :, lat % rows].reshape(lons, chans),
        base - 1, lats, matrix, pull_ref,
    )
    hidden_copy.wait()
    tap_sums(hidden_ref, pull_ref, 1, mine, g2_ref, g2_hbm, g2_sems)
    for tap in range(9):
        pltpu.make_async_copy(g2_ref.at[tap], g2_hbm.at[tap], g2_sems.at[tap]).wait()


def second_sums(bands, pieces, hidden):
    half, rows, group, chans = pieces[0].shape
    lats, lons = bands * rows, 2 * half * group
    ours = lats // 2
    return pl.pallas_call(
        functools.partial(second_kernel, bands),
        out_shape=[
            jax.ShapeDtypeStruct((9, chans, chans), F32),
            jax.ShapeDtypeStruct((ours + 2, lons // 16 + 2, 16, chans), BF16),
        ],
        in_specs=[anywhere()] * (len(pieces) + 1),
        out_specs=[anywhere(), vmem()],
        scratch_shapes=[
            pltpu.VMEM((2, bands) + pieces[0].shape, BF16),
            pltpu.VMEM(hidden.shape, BF16),
            pltpu.VMEM((9, chans, chans), F32),
            pltpu.SemaphoreType.DMA((bands, 2)),
            pltpu.SemaphoreType.DMA,
            pltpu.SemaphoreType.DMA((9,)),
        ],
        compiler_params=params(20),
        cost_estimate=cost(5e9, 8e6),
        name="second_sums",
    )(*pieces, hidden)


def first_kernel(block, slope_hbm, state_hbm, pull_ref, w2t_ref, g1_hbm, first_ref, slope_ref,
                 state_ref, g1_ref, sems, g1_sems):
    steps = pull_ref.shape[1] - 2
    chans = pull_ref.shape[3]
    mine = first_ref.shape[0]
    lons = steps * 16
    size = block * lons
    slope_copy = pltpu.make_async_copy(
        slope_hbm.at[pl.ds(lons, mine * lons), :], slope_ref, sems.at[0]
    )
    state_copy = pltpu.make_async_copy(state_hbm, state_ref, sems.at[1])
    slope_copy.start()
    state_copy.start()
    slope_copy.wait()

    def step(index, carry):
        start = index * block
        back = conv_block(pull_ref, w2t_ref, start, block, True)
        at = pl.ds(pl.multiple_of(index * size, size), size)
        pull = (back * slope_ref[at, :]).astype(BF16).astype(F32)
        pull = pull.reshape(block, steps, 16, chans)
        last, head = pull[:, steps - 1], pull[:, 0]
        before = jnp.concatenate([last[:, 15:], last[:, :15]], axis=1)
        after = jnp.concatenate([head[:, 1:], head[:, :1]], axis=1)
        to = pl.ds(start, block)
        first_ref[to, 1 : 1 + steps] = pull.astype(BF16)
        first_ref[to, 0] = before.astype(BF16)
        first_ref[to, steps + 1] = after.astype(BF16)
        return carry

    lax.fori_loop(0, mine // block, step, 0)
    state_copy.wait()
    tap_sums(state_ref, first_ref, 0, mine, g1_ref, g1_hbm, g1_sems)
    for tap in range(9):
        pltpu.make_async_copy(g1_ref.at[tap], g1_hbm.at[tap], g1_sems.at[tap]).wait()


def first_sums(slope, state, pull, w2t):
    ours, wide, group, chans = pull.shape[0] - 2, *pull.shape[1:]
    lons = (wide - 2) * group
    return pl.pallas_call(
        functools.partial(first_kernel, 4),
        out_shape=jax.ShapeDtypeStruct((9, chans, chans), F32),
        in_specs=[anywhere()] * 2 + [vmem()] * 2,
        out_specs=anywhere(),
        scratch_shapes=[
            pltpu.VMEM((ours, wide, group, chans), BF16),
            pltpu.VMEM((ours * lons, chans), F32),
            pltpu.VMEM(state.shape, BF16),
            pltpu.VMEM((9, chans, chans), F32),
            pltpu.SemaphoreType.DMA((2,)),
            pltpu.SemaphoreType.DMA((9,)),
        ],
        compiler_params=params(24),
        cost_estimate=cost(10e9, 8e6),
        name="first_sums",
    )(slope, state, pull, w2t)


def local_kernel(bands, *refs):
    piece_refs, refs = refs[: 2 * bands], refs[2 * bands :]
    slope_ref, adj_ref, w1_ref, w2_ref, grad_ref = refs[:5]
    near_ref, line_ref, shift_ref, pull_ref, sems = refs[5:]
    rows, cols, chans = near_ref.shape[2:]
    span = pull_ref.shape[1]
    copies = nearby_copies(bands, piece_refs, near_ref, sems)
    for copy in copies:
        copy.start()
    for copy in copies:
        copy.wait()
    fill_line(bands, near_ref, line_ref)
    back = jnp.zeros(((rows + 2) * span, chans), F32)
    for b in range(3):
        shift_ref[...] = (
            line_ref[:, 2 - b : 2 - b + span, :].astype(BF16).reshape((rows + 4) * span, chans)
        )
        for a in range(3):
            piece = shift_ref[(2 - a) * span : (2 - a) * span + (rows + 2) * span, :]
            back = back + dot_nt(piece, w2_ref[3 * a + b])
    pull = (back * slope_ref[...]).reshape(rows + 2, span, chans)
    pull_ref[...] = jnp.where(inside_grid(rows, pull.shape, bands), pull, 0.0)
    total = adj_ref[...]
    for b in range(3):
        shift_ref[0 : (rows + 2) * cols, :] = (
            pull_ref[:, 2 - b : 2 - b + cols, :].astype(BF16).reshape((rows + 2) * cols, chans)
        )
        for a in range(3):
            piece = shift_ref[(2 - a) * cols : (2 - a) * cols + rows * cols, :]
            total = total + dot_nt(piece, w1_ref[3 * a + b])
    grad_ref[...] = total


def local_grad(bands, pieces, slope, adjoint, w1, w2):
    half, rows, cols, chans = pieces[0].shape
    return pl.pallas_call(
        functools.partial(local_kernel, bands),
        out_shape=jax.ShapeDtypeStruct((rows * cols, chans), F32),
        in_specs=[anywhere()] * len(pieces) + [vmem()] * 4,
        out_specs=vmem(),
        scratch_shapes=[
            pltpu.VMEM((3, 3, rows, cols, chans), BF16),
            pltpu.VMEM((rows + 4, SPAN + 8, chans), F32),
            pltpu.VMEM(((rows + 4) * SPAN, chans), BF16),
            pltpu.VMEM((rows + 2, SPAN, chans), F32),
            pltpu.SemaphoreType.DMA((3, 3)),
        ],
        compiler_params=params(16),
        cost_estimate=cost(3e9, 4e6),
        name="local_grad",
    )(*pieces, slope, adjoint, w1, w2)


def with_halo(x, sides, width, wrap):
    for axis, dim in sides:
        count, length = (lax.axis_size(axis), x.shape[dim])
        up = [(i, (i + 1) % count) for i in range(count if wrap else count - 1)]
        down = [(j, i) for i, j in up]
        last = lax.slice_in_dim(x, length - width, length, axis=dim)
        first = lax.slice_in_dim(x, 0, width, axis=dim)
        before = lax.ppermute(last, axis, up)
        after = lax.ppermute(first, axis, down)
        x = jnp.concatenate([before, x, after], axis=dim)
    return x


def widen_tile(field):
    across = with_halo(field, (("lon", 1),), 1, True)
    return with_halo(across, (("lat", 0),), 1, False)


def tile_conv(padded, weight, rows, cols, flipped):
    total = jnp.zeros((rows * cols, weight.shape[2]), jnp.float32)
    for first_tap in range(3):
        for second_tap in range(3):
            if flipped:
                piece = padded[
                    2 - first_tap : 2 - first_tap + rows, 2 - second_tap : 2 - second_tap + cols
                ]
                total = total + lax.dot_general(
                    piece.reshape(rows * cols, -1),
                    weight[3 * first_tap + second_tap],
                    (((1,), (1,)), ((), ())),
                    preferred_element_type=jnp.float32,
                )
            else:
                piece = padded[first_tap : first_tap + rows, second_tap : second_tap + cols]
                total = total + jnp.dot(
                    piece.reshape(rows * cols, -1),
                    weight[3 * first_tap + second_tap],
                    preferred_element_type=jnp.float32,
                )
    return total.reshape(rows, cols, -1)


def tile_grads(padded, pullback, rows, cols):
    flat_pull = pullback.reshape(rows * cols, -1)
    result = []
    for first_tap in range(3):
        for second_tap in range(3):
            piece = padded[first_tap : first_tap + rows, second_tap : second_tap + cols].reshape(
                rows * cols, -1
            )
            result.append(
                lax.dot_general(
                    piece, flat_pull, (((0,), (0,)), ((), ())), preferred_element_type=jnp.float32
                )
            )
    return jnp.stack(result)


def route_blocks(obs_owner, obs_cell, obs_level, obs_count, obs_frac, obs_value, obs_weight):
    devices = lax.axis_size(("lat", "lon"))
    blocks, width = obs_value.shape
    slots = max(2, 3 * blocks // (2 * devices))
    owner = obs_owner[:, 0]
    order = lax.broadcasted_iota(jnp.int32, (blocks, blocks), 1) < lax.broadcasted_iota(
        jnp.int32, (blocks, blocks), 0
    )
    earlier = jnp.logical_and(owner[:, None] == owner[None, :], order)
    rank = jnp.sum(earlier.astype(jnp.int32), axis=1)
    target = owner * slots + rank
    valid = (lax.broadcasted_iota(jnp.int32, (blocks, width), 1) < obs_count[:, None]).astype(
        jnp.float32
    )
    packed = jnp.stack(
        [
            obs_frac[:, 0, :],
            obs_frac[:, 1, :],
            obs_value,
            obs_weight,
            obs_cell.astype(jnp.float32),
            obs_level.astype(jnp.float32),
            valid,
        ],
        axis=1,
    )
    outgoing = jnp.zeros((devices * slots, 7, width), jnp.float32).at[target].set(packed)
    return lax.all_to_all(outgoing, ("lat", "lon"), split_axis=0, concat_axis=0, tiled=True)


def observe(corrected, arrived, rows, cols, chans):
    fields = jnp.transpose(arrived, (1, 0, 2)).reshape(7, -1)
    row_total = fields.shape[1]
    span_rows = math.gcd(row_total, 1024)
    fields = jnp.transpose(fields.reshape(7, row_total // span_rows, span_rows), (1, 0, 2))
    grid = corrected.reshape(rows * cols, chans)
    cells = lax.broadcasted_iota(jnp.int32, (1, rows * cols), 1)
    levels = lax.broadcasted_iota(jnp.int32, (1, chans), 1)

    def advance(summed, portion):
        frac_lat = portion[0][:, None]
        frac_lon = portion[1][:, None]
        corner = portion[4].astype(jnp.int32)[:, None]
        level = portion[5].astype(jnp.int32)[:, None]
        weights = (1.0 - frac_lat) * (1.0 - frac_lon) * (cells == corner).astype(jnp.float32)
        weights = weights + (1.0 - frac_lat) * frac_lon * (cells == corner + 1).astype(jnp.float32)
        weights = weights + frac_lat * (1.0 - frac_lon) * (cells == corner + cols).astype(
            jnp.float32
        )
        weights = weights + frac_lat * frac_lon * (cells == corner + cols + 1).astype(jnp.float32)
        onehot = (levels == level).astype(jnp.float32)
        sampled = jnp.dot(
            weights, grid, precision=lax.Precision.HIGHEST, preferred_element_type=jnp.float32
        )
        predicted = jnp.sum(sampled * onehot, axis=1)
        misfit = portion[6] * portion[3] * (predicted - portion[2])
        summed = summed + lax.dot_general(
            weights,
            onehot * misfit[:, None],
            (((0,), (0,)), ((), ())),
            precision=lax.Precision.HIGHEST,
            preferred_element_type=jnp.float32,
        )
        return (summed, None)

    summed, unused = lax.scan(advance, jnp.zeros((rows * cols, chans), jnp.float32), fields)
    return summed.reshape(rows, cols, chans)


def by_tiles(
    state,
    weight_first,
    weight_second,
    obs_owner,
    obs_cell,
    obs_level,
    obs_count,
    obs_frac,
    obs_value,
    obs_weight,
):
    rows, cols, chans = state.shape
    wide_state = widen_tile(state)
    first = tile_conv(wide_state, weight_first, rows, cols, False)
    hidden = jax.nn.silu(first).astype(jnp.bfloat16)
    wide_hidden = widen_tile(hidden)
    corrected = state.astype(jnp.float32) + tile_conv(wide_hidden, weight_second, rows, cols, False)
    arrived = route_blocks(
        obs_owner, obs_cell, obs_level, obs_count, obs_frac, obs_value, obs_weight
    )
    adjoint = observe(corrected, arrived, rows, cols, chans)
    pullback = adjoint.astype(jnp.bfloat16)
    wide_pull = widen_tile(pullback)
    local_second = tile_grads(wide_hidden, pullback, rows, cols)
    back = tile_conv(wide_pull, weight_second, rows, cols, True)
    sig = jax.nn.sigmoid(first)
    pull_first = (back * sig * (1.0 + first * (1.0 - sig))).astype(jnp.bfloat16)
    wide_pull_first = widen_tile(pull_first)
    local_first = tile_grads(wide_state, pull_first, rows, cols)
    state_grad = adjoint + tile_conv(wide_pull_first, weight_first, rows, cols, True)
    grad_first, grad_second = lax.psum((local_first, local_second), ("lat", "lon"))
    return (state_grad, grad_first, grad_second)


def halo_pieces(x):
    bands, tiles = lax.axis_size("lat"), lax.axis_size("lon")
    rows, cols, _ = x.shape
    north = lax.ppermute(x[rows - 2 :], "lat", [(i, i + 1) for i in range(bands - 1)])
    south = lax.ppermute(x[:2], "lat", [(i + 1, i) for i in range(bands - 1)])
    last = jnp.concatenate([p[:, cols - 2 :] for p in (north, x, south)], axis=0)
    first = jnp.concatenate([p[:, :2] for p in (north, x, south)], axis=0)
    west = lax.ppermute(last, "lon", [(i, (i + 1) % tiles) for i in range(tiles)])
    east = lax.ppermute(first, "lon", [((i + 1) % tiles, i) for i in range(tiles)])
    return x, north, south, west, east


def gather_line(copies):
    half = copies.shape[0]
    same = [[2 * q + core for q in range(half)] for core in range(2)]
    return lax.all_to_all(copies, "lon", 0, 0, axis_index_groups=same, tiled=True)


def gather_line_backwards(x):
    tiles = lax.axis_size("lon")
    return jnp.stack(
        [x]
        + [
            lax.ppermute(x, "lon", [(i, (i + step) % tiles) for i in range(tiles)])
            for step in range(2, tiles, 2)
        ]
    )


def gather_bands(line):
    bands = lax.axis_size("lat")
    return [line] + [
        lax.ppermute(line, "lat", [(i, (i + step) % bands) for i in range(bands)])
        for step in range(1, bands)
    ]


def with_other_core(lines):
    swap = [(i, i ^ 1) for i in range(lax.axis_size("lon"))]
    pieces = []
    for line in lines:
        pieces += [line, lax.ppermute(line, "lon", swap)]
    return pieces


def per_device(
    state, weight_first, weight_second, obs_owner, obs_cell, obs_level, obs_count, obs_frac,
    obs_value, obs_weight,
):
    rows, cols, chans = state.shape
    bands = lax.axis_size("lat")
    devices = lax.axis_size(("lat", "lon"))
    if devices * rows * cols > WHOLE_CELLS:
        return by_tiles(
            state, weight_first, weight_second, obs_owner, obs_cell, obs_level, obs_count,
            obs_frac, obs_value, obs_weight,
        )
    slots = max(2, 3 * obs_value.shape[0] // (2 * devices))
    outgoing = route(
        devices, slots, chans, obs_owner, obs_cell, obs_level, obs_count, obs_frac, obs_value,
        obs_weight,
    )
    outgoing, sent = lax.optimization_barrier((outgoing, state))
    pieces = halo_pieces(state)
    got = lax.all_to_all(outgoing, ("lat", "lon"), split_axis=0, concat_axis=0, tiled=True)
    line = gather_line_backwards(sent)
    line, pieces, got = lax.optimization_barrier((line, pieces, got))
    state_lines = gather_bands(line)
    half = lax.axis_size("lon") // 2
    adjoint, pullback, near_slope = forward(
        slots, bands, half, pieces, weight_first, weight_second, got
    )
    state_lines, pullback = lax.optimization_barrier((state_lines, pullback))
    state_pieces = with_other_core(state_lines)
    pull_lines = gather_bands(gather_line(pullback.reshape(half, rows, cols, chans)))
    firsts = whole(bands, state_pieces, weight_first, weight_second)
    pull_lines, firsts = lax.optimization_barrier((pull_lines, firsts))
    slope, hidden, turned, w2t = firsts
    pull_pieces = with_other_core(pull_lines)
    swap = [(i, i ^ 1) for i in range(2 * half)]
    g2, pull = second_sums(bands, pull_pieces, hidden)
    g2_other = lax.ppermute(g2, "lon", swap)
    g1 = first_sums(slope, turned, pull, w2t)
    g1, g2_other = lax.optimization_barrier((g1, g2_other))
    g1_other = lax.ppermute(g1, "lon", swap)
    grad = local_grad(bands, pull_pieces, near_slope, adjoint, weight_first, weight_second)
    g1, g2 = g1 + g1_other, g2 + g2_other
    return grad.reshape(rows, cols, chans), g1, g2


def solution(mesh):
    both = P(("lat", "lon"), None)
    placed = (
        P("lat", "lon", None),
        P(),
        P(),
        both,
        both,
        both,
        P(("lat", "lon")),
        P(("lat", "lon"), None, None),
        both,
        both,
    )
    return jax.shard_map(
        per_device,
        mesh=mesh,
        in_specs=placed,
        out_specs=(P("lat", "lon", None), P(), P()),
        check_vma=False,
    )
```

```python
import functools
import math

import jax
import jax.numpy as jnp
from jax import lax
from jax.experimental import pallas as pl
from jax.experimental.pallas import tpu as pltpu
from jax.sharding import PartitionSpec as P

F32 = jnp.float32
BF16 = jnp.bfloat16
FIELDS = 5
SPAN = 32
WHOLE_CELLS = 4096


def params(mebibytes):
    return pltpu.CompilerParams(vmem_limit_bytes=mebibytes * 1024 * 1024)


def cost(flops, moved):
    return pl.CostEstimate(flops=int(flops), bytes_accessed=int(moved), transcendentals=0)


def vmem():
    return pl.BlockSpec(memory_space=pltpu.VMEM)


def anywhere():
    return pl.BlockSpec(memory_space=pl.ANY)


def iota(shape, dim, dtype=jnp.int32):
    return lax.broadcasted_iota(jnp.int32, shape, dim).astype(dtype)


def dot(x, y, precision=None):
    return jnp.dot(x, y, precision=precision, preferred_element_type=F32)


def dot_nt(x, y, precision=None):
    return lax.dot_general(
        x, y, (((1,), (1,)), ((), ())), precision=precision, preferred_element_type=F32
    )


def slot_layout(slots):
    full, rest = divmod(slots, 4)
    rows = full * FIELDS + (0 if rest == 0 else -(-FIELDS // 2))
    return full, rest, -(-rows // 8) * 8


def route_kernel(
    devices, slots, chans, owner_ref, count_ref, cell_ref, level_ref, frac_ref, value_ref,
    weight_ref, out_ref
):
    width, blocks = value_ref.shape
    owner = owner_ref[...].astype(F32)
    across = jnp.broadcast_to(owner, (blocks, blocks))
    down = across.T
    earlier = iota((blocks, blocks), 0) < iota((blocks, blocks), 1)
    hits = jnp.where(jnp.logical_and(across == down, earlier), 1.0, 0.0)
    rank = jnp.sum(hits, axis=0, keepdims=True)
    target = rank * float(devices) + owner
    places = iota((slots * devices, blocks), 0, F32) == target
    onehot = jnp.where(places, 1.0, 0.0)
    valid = iota((width, blocks), 0) < count_ref[...]
    fields = jnp.concatenate(
        [
            frac_ref[0],
            frac_ref[1],
            value_ref[...],
            jnp.where(valid, weight_ref[...], 0.0),
            (cell_ref[...] * chans + level_ref[...]).astype(F32),
        ],
        axis=0,
    )
    placed = dot_nt(onehot, fields, lax.Precision.HIGHEST)
    full, rest, rows = slot_layout(slots)
    out_ref[...] = jnp.zeros(out_ref.shape, F32)
    for slot in range(slots):
        for field in range(FIELDS):
            piece = placed[
                slot * devices : (slot + 1) * devices, field * width : (field + 1) * width
            ]
            if slot < 4 * full:
                row, lane = (slot // 4) * FIELDS + field, (slot % 4) * width
            else:
                row = full * FIELDS + field // 2
                lane = (field % 2) * 2 * width + (slot - 4 * full) * width
            out_ref[:, row, lane : lane + width] = piece


def route(devices, slots, chans, obs_owner, obs_cell, obs_level, obs_count, obs_frac, obs_value,
          obs_weight):
    blocks = obs_value.shape[0]
    rows = slot_layout(slots)[2]
    return pl.pallas_call(
        functools.partial(route_kernel, devices, slots, chans),
        out_shape=jax.ShapeDtypeStruct((devices, rows, 128), F32),
        in_specs=[vmem()] * 7,
        out_specs=vmem(),
        compiler_params=params(60),
        name="route",
    )(
        obs_owner.reshape(1, blocks),
        obs_count.reshape(1, blocks),
        obs_cell.T,
        obs_level.T,
        jnp.transpose(obs_frac, (1, 2, 0)),
        obs_value.T,
        obs_weight.T,
    )


def silu_parts(first):
    sig = 1.0 / (1.0 + jnp.exp(-first))
    return sig, first * sig


def inside_grid(rows, shape, bands):
    lat = lax.axis_index("lat") * rows + iota(shape, 0) - 1
    return jnp.logical_and(lat >= 0, lat < bands * rows)


def band_copies(bands, piece_refs, all_ref, sems):
    core = lax.axis_index("lon") & 1
    lat = lax.axis_index("lat")
    copies = []
    for offset in range(bands):
        band = (lat + bands - offset) % bands
        for side in range(2):
            copies.append(
                pltpu.make_async_copy(
                    piece_refs[2 * offset + side],
                    all_ref.at[core if side == 0 else 1 - core, band],
                    sems.at[offset, side],
                )
            )
    return copies


def nearby_copies(bands, piece_refs, near_ref, sems):
    half = piece_refs[0].shape[0]
    lon = lax.axis_index("lon")
    west = lax.shift_right_logical((lon + 2 * half - 1) & (2 * half - 1), 1)
    east = lax.shift_right_logical((lon + 1) & (2 * half - 1), 1)
    here = lax.shift_right_logical(lon, 1)
    copies = []
    for down, offset in enumerate((1, 0, bands - 1)):
        mine, other = piece_refs[2 * offset], piece_refs[2 * offset + 1]
        for over, (source, q) in enumerate(((other, west), (mine, here), (other, east))):
            copies.append(
                pltpu.make_async_copy(source.at[q], near_ref.at[down, over], sems.at[down, over])
            )
    return copies


def fill_line(bands, near_ref, line_ref):
    rows, cols, chans = near_ref.shape[2:]
    lat = lax.axis_index("lat")
    for down, (y, height, first) in enumerate(((0, 2, rows - 2), (2, rows, 0), (2 + rows, 2, 0))):
        band = lat + down - 1
        for over, (x, width, left) in enumerate(((0, 2, cols - 2), (2, cols, 0), (2 + cols, 2, 0))):
            part = near_ref[down, over].astype(F32)[
                first : first + height, left : left + width
            ]
            if down != 1:
                part = jnp.where(jnp.logical_and(band >= 0, band < bands), part, 0.0)
            line_ref[y : y + height, x : x + width, :] = part
    line_ref[:, cols + 4 :, :] = jnp.zeros(
        (rows + 4, line_ref.shape[1] - cols - 4, chans), F32
    )


def forward_kernel(slots, bands, group, parts, tile_ref, north_ref, south_ref, west_ref, east_ref,
                   w1_ref, w2_ref, got_ref, adj_ref, pull_ref, slope_ref, line_ref, shift_ref,
                   hid_ref, obs_ref, sum_ref):
    rows, cols, chans = tile_ref.shape
    span = hid_ref.shape[1]
    line_ref[0:2, 2 : 2 + cols, :] = north_ref[...].astype(F32)
    line_ref[2 : 2 + rows, 2 : 2 + cols, :] = tile_ref[...].astype(F32)
    line_ref[2 + rows :, 2 : 2 + cols, :] = south_ref[...].astype(F32)
    line_ref[:, 0:2, :] = west_ref[...].astype(F32)
    line_ref[:, 2 + cols : 4 + cols, :] = east_ref[...].astype(F32)
    line_ref[:, cols + 4 :, :] = jnp.zeros(
        (rows + 4, line_ref.shape[1] - cols - 4, chans), F32
    )
    first = jnp.zeros(((rows + 2) * span, chans), F32)
    for b in range(3):
        shift_ref[...] = (
            line_ref[:, b : b + span, :].astype(BF16).reshape((rows + 4) * span, chans)
        )
        for a in range(3):
            first = first + dot(
                shift_ref[a * span : a * span + (rows + 2) * span, :], w1_ref[3 * a + b]
            )
    sig, hidden = silu_parts(first)
    slope_ref[...] = sig * (1.0 + first * (1.0 - sig))
    hidden = hidden.astype(BF16).astype(F32).reshape(rows + 2, span, chans)
    hidden = jnp.where(inside_grid(rows, hidden.shape, bands), hidden, 0.0)
    hid_ref[...] = hidden
    total = line_ref[2 : 2 + rows, 2 : 2 + cols, :].reshape(rows * cols, chans)
    for b in range(3):
        shift_ref[0 : (rows + 2) * cols, :] = (
            hid_ref[:, b : b + cols, :].astype(BF16).reshape((rows + 2) * cols, chans)
        )
        for a in range(3):
            total = total + dot(
                shift_ref[a * cols : a * cols + rows * cols, :], w2_ref[3 * a + b]
            )
    cells = rows * cols
    turned = total.T
    grid_high = turned.astype(BF16)
    grid_low = (turned - grid_high.astype(F32)).astype(BF16)
    grid_both = jnp.concatenate([grid_high, grid_low], axis=1)

    devices = got_ref.shape[0]
    full, rest, _ = slot_layout(slots)
    half = devices // 2
    for field in range(FIELDS):
        for part in range(full):
            obs_ref[field, part * devices : (part + 1) * devices, :] = got_ref[
                :, part * FIELDS + field, :
            ]
        if rest:
            tail = got_ref[:, full * FIELDS + field // 2, :]
            low, high = tail[:half], tail[half:]
            if field % 2 == 0:
                high = pltpu.roll(high, 64, 1)
            else:
                low = pltpu.roll(low, 64, 1)
            obs_ref[field, full * devices : full * devices + half, :] = jnp.where(
                iota((half, 128), 1) < 64, low, high
            )
    code = obs_ref[4].astype(jnp.int32)
    shift = chans.bit_length() - 1
    cell = lax.shift_right_logical(code, shift)
    obs_ref[4] = (code & (chans - 1)).astype(F32)
    obs_ref[0] = obs_ref[0] + lax.shift_right_logical(cell, 4).astype(F32)
    obs_ref[1] = obs_ref[1] + (cell & (cols - 1)).astype(F32)

    sum_ref[...] = jnp.zeros(sum_ref.shape, F32)
    count = obs_ref.shape[1] // (group * parts)
    row_ids = iota((rows, 128), 0, F32)
    col_ids = iota((cols, 128), 0, F32)
    level_ids = iota((chans, 128), 0, F32)

    def add_group(start):
        high, low, masks, marks = [], [], [], []
        for piece in range(group):
            mark = [obs_ref[field, pl.ds(start + piece, 1), :] for field in range(FIELDS)]
            up = jnp.maximum(0.0, 1.0 - jnp.abs(row_ids - mark[0]))
            along = jnp.maximum(0.0, 1.0 - jnp.abs(col_ids - mark[1]))
            weights = (up[:, None, :] * along[None, :, :]).reshape(cells, 128)
            weights_high = weights.astype(BF16)
            high.append(weights_high)
            low.append((weights - weights_high.astype(F32)).astype(BF16))
            masks.append(level_ids == mark[4])
            marks.append(mark)
        high = jnp.concatenate(high, axis=1)
        low = jnp.concatenate(low, axis=1)
        sampled = dot(grid_both, jnp.concatenate([high, high], axis=0)) + dot(grid_high, low)
        hot_high, hot_low = [], []
        for piece in range(group):
            mine = sampled[:, piece * 128 : (piece + 1) * 128]
            predicted = jnp.sum(jnp.where(masks[piece], mine, 0.0), axis=0, keepdims=True)
            misfit = marks[piece][3] * (predicted - marks[piece][2])
            misfit_high = misfit.astype(BF16).astype(F32)
            hot_high.append(jnp.where(masks[piece], misfit_high, 0.0).astype(BF16))
            hot_low.append(jnp.where(masks[piece], misfit - misfit_high, 0.0).astype(BF16))
        hot_high = jnp.concatenate(hot_high, axis=1)
        hot_low = jnp.concatenate(hot_low, axis=1)
        mixed = dot_nt(
            jnp.concatenate([hot_high, hot_low], axis=0), jnp.concatenate([high, low], axis=0)
        )
        return mixed[:chans, :cells] + (mixed[chans:, :cells] + mixed[:chans, cells:])

    def step(index, carry):
        total = sum_ref[...]
        for part in range(parts):
            total = total + add_group((index * parts + part) * group)
        sum_ref[...] = total
        return carry

    lax.fori_loop(0, count, step, 0)
    adjoint = sum_ref[...].T
    adj_ref[...] = adjoint
    for copy in range(pull_ref.shape[0]):
        pull_ref[copy] = adjoint.astype(BF16)


def forward(slots, bands, copies, pieces, w1, w2, got):
    rows, cols, chans = pieces[0].shape
    devices = got.shape[0]
    full, rest, _ = slot_layout(slots)
    groups = full * devices + (devices // 2 if rest else 0)
    return pl.pallas_call(
        functools.partial(forward_kernel, slots, bands, 2, 4),
        out_shape=[
            jax.ShapeDtypeStruct((rows * cols, chans), F32),
            jax.ShapeDtypeStruct((copies, rows * cols, chans), BF16),
            jax.ShapeDtypeStruct(((rows + 2) * SPAN, chans), F32),
        ],
        in_specs=[vmem()] * 8,
        out_specs=[vmem()] * 3,
        scratch_shapes=[
            pltpu.VMEM((rows + 4, SPAN + 8, chans), F32),
            pltpu.VMEM(((rows + 4) * SPAN, chans), BF16),
            pltpu.VMEM((rows + 2, SPAN, chans), F32),
            pltpu.VMEM((FIELDS, groups, 128), F32),
            pltpu.VMEM((chans, rows * cols), F32),
        ],
        compiler_params=params(46),
        cost_estimate=cost(4e9, 4e6),
        name="forward",
    )(*pieces, w1, w2, got)


def spread_matrix(steps, tiles, backwards):
    lons = 16 * steps
    half = tiles // 2
    place = iota(((steps + 2) * 16, lons), 0)
    lon = (place & 15) * steps + lax.shift_right_logical(place, 4) - 1
    lon = jnp.where(lon < 0, lon + lons, jnp.where(lon >= lons, lon - lons, lon))
    column = iota(((steps + 2) * 16, lons), 1)
    chunk = lax.shift_right_logical(column, 4)
    core = lax.shift_right_logical(chunk, half.bit_length() - 1)
    here = lax.shift_right_logical(lax.axis_index("lon"), 1)
    q = chunk & (half - 1)
    if backwards:
        q = (here - q) & (half - 1)
    column = (2 * q + core) * 16 + (column & 15)
    return jnp.where(column == lon, 1.0, 0.0)


def spread(line_of, start, lats, matrix, pad_ref):
    steps = pad_ref.shape[1] - 2
    for row in range(pad_ref.shape[0]):
        lat = start + row
        inside = jnp.logical_and(lat >= 0, lat < lats)
        line = line_of(jnp.clip(lat, 0, lats - 1))
        chosen = jnp.where(inside, matrix, 0.0).astype(BF16)
        pad_ref[row] = dot(chosen, line).astype(BF16).reshape(steps + 2, 16, line.shape[1])


def conv_block(pad_ref, weight_ref, start, rows, flipped):
    steps = pad_ref.shape[1] - 2
    chans = pad_ref.shape[3]
    pieces = []
    for a in range(3):
        for b in range(3):
            da, db = (2 - a, 2 - b) if flipped else (a, b)
            piece = pad_ref[pl.ds(start + da, rows), db : db + steps]
            pieces.append(piece.reshape(rows * steps * 16, chans))
    return dot(jnp.concatenate(pieces, axis=1), weight_ref[...].reshape(9 * chans, chans))


def whole_kernel(block, *refs):
    bands = refs[-2].shape[1]
    piece_refs, refs = refs[: 2 * bands], refs[2 * bands :]
    w1_ref, w2_ref, slope_ref, hidden_ref, state_ref, w2t_ref, pad_ref, all_ref, sems = refs
    _, _, half, rows, group, chans = all_ref.shape
    lats, lons = bands * rows, 2 * half * group
    steps = lons // 16
    size = block * lons
    mine = pad_ref.shape[0] - 4
    base = (lax.axis_index("lon") & 1) * mine
    copies = band_copies(bands, piece_refs, all_ref, sems)
    for copy in copies:
        copy.start()
    matrix = spread_matrix(steps, 2 * half, True)
    for tap in range(9):
        w2t_ref[tap] = w2_ref[tap].T
    for copy in copies:
        copy.wait()
    spread(
        lambda lat: all_ref[:, lat // rows, :, lat % rows].reshape(lons, chans),
        base - 2, lats, matrix, pad_ref,
    )

    def step(index, carry):
        start = index * block
        first = conv_block(pad_ref, w1_ref, start, block, False)
        sig, hidden = silu_parts(first)
        at = pl.ds(pl.multiple_of(index * size, size), size)
        slope_ref[at, :] = sig * (1.0 + first * (1.0 - sig))
        lat = base - 1 + start + lax.shift_right_logical(
            iota((size, chans), 0), lons.bit_length() - 1
        )
        hidden = jnp.where(jnp.logical_and(lat >= 0, lat < lats), hidden, 0.0)
        hidden_ref[:, at] = hidden.astype(BF16).T
        centre = pad_ref[pl.ds(start + 1, block), 1 : 1 + steps].reshape(size, chans)
        state_ref[:, at] = centre.T
        return carry

    lax.fori_loop(0, (mine + 2) // block, step, 0)


def whole(bands, pieces, w1, w2):
    half, rows, group, chans = pieces[0].shape
    lats, lons = bands * rows, 2 * half * group
    mine = lats // 2
    steps = lons // 16
    cells = (mine + 2) * lons
    return pl.pallas_call(
        functools.partial(whole_kernel, 3),
        out_shape=[
            jax.ShapeDtypeStruct((cells, chans), F32),
            jax.ShapeDtypeStruct((chans, cells), BF16),
            jax.ShapeDtypeStruct((chans, cells), BF16),
            jax.ShapeDtypeStruct((9, chans, chans), BF16),
        ],
        in_specs=[anywhere()] * len(pieces) + [vmem()] * 2,
        out_specs=[vmem()] * 4,
        scratch_shapes=[
            pltpu.VMEM((mine + 4, steps + 2, 16, chans), BF16),
            pltpu.VMEM((2, bands) + pieces[0].shape, BF16),
            pltpu.SemaphoreType.DMA((bands, 2)),
        ],
        compiler_params=params(22),
        cost_estimate=cost(6e9, 10e6),
        name="whole",
    )(*pieces, w1, w2)


def tap_sums(turned_ref, pad_ref, first_row, rows, sum_ref, out_ref, sem):
    steps = pad_ref.shape[1] - 2
    chans = pad_ref.shape[3]
    lons = steps * 16

    def step(tap, carry):
        a, b = tap // 3, tap % 3
        piece = pad_ref[first_row : first_row + rows, pl.ds(2 - b, steps)]
        at = pl.ds(pl.multiple_of(a * lons, lons), rows * lons)
        sum_ref[tap] = dot(turned_ref[:, at], piece.reshape(rows * lons, chans))
        pltpu.make_async_copy(sum_ref.at[tap], out_ref.at[tap], sem.at[tap]).start()
        return carry

    lax.fori_loop(0, 9, step, 0)


def second_kernel(bands, *refs):
    piece_refs, refs = refs[: 2 * bands], refs[2 * bands :]
    hidden_hbm, g2_hbm, pull_ref, all_ref, hidden_ref, g2_ref, piece_sems, sem, g2_sems = refs
    steps = pull_ref.shape[1] - 2
    chans = pull_ref.shape[3]
    lons = steps * 16
    _, _, half, rows, _, _ = all_ref.shape
    lats = bands * rows
    mine = lats // 2
    base = (lax.axis_index("lon") & 1) * mine
    copies = band_copies(bands, piece_refs, all_ref, piece_sems)
    hidden_copy = pltpu.make_async_copy(hidden_hbm, hidden_ref, sem)
    for copy in copies:
        copy.start()
    hidden_copy.start()
    matrix = spread_matrix(steps, 2 * half, False)
    for copy in copies:
        copy.wait()
    spread(
        lambda lat: all_ref[:, lat // rows, :, lat % rows].reshape(lons, chans),
        base - 1, lats, matrix, pull_ref,
    )
    hidden_copy.wait()
    tap_sums(hidden_ref, pull_ref, 1, mine, g2_ref, g2_hbm, g2_sems)
    for tap in range(9):
        pltpu.make_async_copy(g2_ref.at[tap], g2_hbm.at[tap], g2_sems.at[tap]).wait()


def second_sums(bands, pieces, hidden):
    half, rows, group, chans = pieces[0].shape
    lats, lons = bands * rows, 2 * half * group
    ours = lats // 2
    return pl.pallas_call(
        functools.partial(second_kernel, bands),
        out_shape=[
            jax.ShapeDtypeStruct((9, chans, chans), F32),
            jax.ShapeDtypeStruct((ours + 2, lons // 16 + 2, 16, chans), BF16),
        ],
        in_specs=[anywhere()] * (len(pieces) + 1),
        out_specs=[anywhere(), vmem()],
        scratch_shapes=[
            pltpu.VMEM((2, bands) + pieces[0].shape, BF16),
            pltpu.VMEM(hidden.shape, BF16),
            pltpu.VMEM((9, chans, chans), F32),
            pltpu.SemaphoreType.DMA((bands, 2)),
            pltpu.SemaphoreType.DMA,
            pltpu.SemaphoreType.DMA((9,)),
        ],
        compiler_params=params(20),
        cost_estimate=cost(5e9, 8e6),
        name="second_sums",
    )(*pieces, hidden)


def first_kernel(block, slope_hbm, state_hbm, pull_ref, w2t_ref, g1_hbm, first_ref, slope_ref,
                 state_ref, g1_ref, sems, g1_sems):
    steps = pull_ref.shape[1] - 2
    chans = pull_ref.shape[3]
    mine = first_ref.shape[0]
    lons = steps * 16
    size = block * lons
    slope_copy = pltpu.make_async_copy(
        slope_hbm.at[pl.ds(lons, mine * lons), :], slope_ref, sems.at[0]
    )
    state_copy = pltpu.make_async_copy(state_hbm, state_ref, sems.at[1])
    slope_copy.start()
    state_copy.start()
    slope_copy.wait()

    def step(index, carry):
        start = index * block
        back = conv_block(pull_ref, w2t_ref, start, block, True)
        at = pl.ds(pl.multiple_of(index * size, size), size)
        pull = (back * slope_ref[at, :]).astype(BF16).astype(F32)
        pull = pull.reshape(block, steps, 16, chans)
        last, head = pull[:, steps - 1], pull[:, 0]
        before = jnp.concatenate([last[:, 15:], last[:, :15]], axis=1)
        after = jnp.concatenate([head[:, 1:], head[:, :1]], axis=1)
        to = pl.ds(start, block)
        first_ref[to, 1 : 1 + steps] = pull.astype(BF16)
        first_ref[to, 0] = before.astype(BF16)
        first_ref[to, steps + 1] = after.astype(BF16)
        return carry

    lax.fori_loop(0, mine // block, step, 0)
    state_copy.wait()
    tap_sums(state_ref, first_ref, 0, mine, g1_ref, g1_hbm, g1_sems)
    for tap in range(9):
        pltpu.make_async_copy(g1_ref.at[tap], g1_hbm.at[tap], g1_sems.at[tap]).wait()


def first_sums(slope, state, pull, w2t):
    ours, wide, group, chans = pull.shape[0] - 2, *pull.shape[1:]
    lons = (wide - 2) * group
    return pl.pallas_call(
        functools.partial(first_kernel, 4),
        out_shape=jax.ShapeDtypeStruct((9, chans, chans), F32),
        in_specs=[anywhere()] * 2 + [vmem()] * 2,
        out_specs=anywhere(),
        scratch_shapes=[
            pltpu.VMEM((ours, wide, group, chans), BF16),
            pltpu.VMEM((ours * lons, chans), F32),
            pltpu.VMEM(state.shape, BF16),
            pltpu.VMEM((9, chans, chans), F32),
            pltpu.SemaphoreType.DMA((2,)),
            pltpu.SemaphoreType.DMA((9,)),
        ],
        compiler_params=params(24),
        cost_estimate=cost(10e9, 8e6),
        name="first_sums",
    )(slope, state, pull, w2t)


def local_kernel(bands, *refs):
    piece_refs, refs = refs[: 2 * bands], refs[2 * bands :]
    slope_ref, adj_ref, w1_ref, w2_ref, grad_ref = refs[:5]
    near_ref, line_ref, shift_ref, pull_ref, sems = refs[5:]
    rows, cols, chans = near_ref.shape[2:]
    span = pull_ref.shape[1]
    copies = nearby_copies(bands, piece_refs, near_ref, sems)
    for copy in copies:
        copy.start()
    for copy in copies:
        copy.wait()
    fill_line(bands, near_ref, line_ref)
    back = jnp.zeros(((rows + 2) * span, chans), F32)
    for b in range(3):
        shift_ref[...] = (
            line_ref[:, 2 - b : 2 - b + span, :].astype(BF16).reshape((rows + 4) * span, chans)
        )
        for a in range(3):
            piece = shift_ref[(2 - a) * span : (2 - a) * span + (rows + 2) * span, :]
            back = back + dot_nt(piece, w2_ref[3 * a + b])
    pull = (back * slope_ref[...]).reshape(rows + 2, span, chans)
    pull_ref[...] = jnp.where(inside_grid(rows, pull.shape, bands), pull, 0.0)
    total = adj_ref[...]
    for b in range(3):
        shift_ref[0 : (rows + 2) * cols, :] = (
            pull_ref[:, 2 - b : 2 - b + cols, :].astype(BF16).reshape((rows + 2) * cols, chans)
        )
        for a in range(3):
            piece = shift_ref[(2 - a) * cols : (2 - a) * cols + rows * cols, :]
            total = total + dot_nt(piece, w1_ref[3 * a + b])
    grad_ref[...] = total


def local_grad(bands, pieces, slope, adjoint, w1, w2):
    half, rows, cols, chans = pieces[0].shape
    return pl.pallas_call(
        functools.partial(local_kernel, bands),
        out_shape=jax.ShapeDtypeStruct((rows * cols, chans), F32),
        in_specs=[anywhere()] * len(pieces) + [vmem()] * 4,
        out_specs=vmem(),
        scratch_shapes=[
            pltpu.VMEM((3, 3, rows, cols, chans), BF16),
            pltpu.VMEM((rows + 4, SPAN + 8, chans), F32),
            pltpu.VMEM(((rows + 4) * SPAN, chans), BF16),
            pltpu.VMEM((rows + 2, SPAN, chans), F32),
            pltpu.SemaphoreType.DMA((3, 3)),
        ],
        compiler_params=params(16),
        cost_estimate=cost(3e9, 4e6),
        name="local_grad",
    )(*pieces, slope, adjoint, w1, w2)


def with_halo(x, sides, width, wrap):
    for axis, dim in sides:
        count, length = (lax.axis_size(axis), x.shape[dim])
        up = [(i, (i + 1) % count) for i in range(count if wrap else count - 1)]
        down = [(j, i) for i, j in up]
        last = lax.slice_in_dim(x, length - width, length, axis=dim)
        first = lax.slice_in_dim(x, 0, width, axis=dim)
        before = lax.ppermute(last, axis, up)
        after = lax.ppermute(first, axis, down)
        x = jnp.concatenate([before, x, after], axis=dim)
    return x


def widen_tile(field):
    across = with_halo(field, (("lon", 1),), 1, True)
    return with_halo(across, (("lat", 0),), 1, False)


def tile_conv(padded, weight, rows, cols, flipped):
    total = jnp.zeros((rows * cols, weight.shape[2]), jnp.float32)
    for first_tap in range(3):
        for second_tap in range(3):
            if flipped:
                piece = padded[
                    2 - first_tap : 2 - first_tap + rows, 2 - second_tap : 2 - second_tap + cols
                ]
                total = total + lax.dot_general(
                    piece.reshape(rows * cols, -1),
                    weight[3 * first_tap + second_tap],
                    (((1,), (1,)), ((), ())),
                    preferred_element_type=jnp.float32,
                )
            else:
                piece = padded[first_tap : first_tap + rows, second_tap : second_tap + cols]
                total = total + jnp.dot(
                    piece.reshape(rows * cols, -1),
                    weight[3 * first_tap + second_tap],
                    preferred_element_type=jnp.float32,
                )
    return total.reshape(rows, cols, -1)


def tile_grads(padded, pullback, rows, cols):
    flat_pull = pullback.reshape(rows * cols, -1)
    result = []
    for first_tap in range(3):
        for second_tap in range(3):
            piece = padded[first_tap : first_tap + rows, second_tap : second_tap + cols].reshape(
                rows * cols, -1
            )
            result.append(
                lax.dot_general(
                    piece, flat_pull, (((0,), (0,)), ((), ())), preferred_element_type=jnp.float32
                )
            )
    return jnp.stack(result)


def route_blocks(obs_owner, obs_cell, obs_level, obs_count, obs_frac, obs_value, obs_weight):
    devices = lax.axis_size(("lat", "lon"))
    blocks, width = obs_value.shape
    slots = max(2, 3 * blocks // (2 * devices))
    owner = obs_owner[:, 0]
    order = lax.broadcasted_iota(jnp.int32, (blocks, blocks), 1) < lax.broadcasted_iota(
        jnp.int32, (blocks, blocks), 0
    )
    earlier = jnp.logical_and(owner[:, None] == owner[None, :], order)
    rank = jnp.sum(earlier.astype(jnp.int32), axis=1)
    target = owner * slots + rank
    valid = (lax.broadcasted_iota(jnp.int32, (blocks, width), 1) < obs_count[:, None]).astype(
        jnp.float32
    )
    packed = jnp.stack(
        [
            obs_frac[:, 0, :],
            obs_frac[:, 1, :],
            obs_value,
            obs_weight,
            obs_cell.astype(jnp.float32),
            obs_level.astype(jnp.float32),
            valid,
        ],
        axis=1,
    )
    outgoing = jnp.zeros((devices * slots, 7, width), jnp.float32).at[target].set(packed)
    return lax.all_to_all(outgoing, ("lat", "lon"), split_axis=0, concat_axis=0, tiled=True)


def observe(corrected, arrived, rows, cols, chans):
    fields = jnp.transpose(arrived, (1, 0, 2)).reshape(7, -1)
    row_total = fields.shape[1]
    span_rows = math.gcd(row_total, 1024)
    fields = jnp.transpose(fields.reshape(7, row_total // span_rows, span_rows), (1, 0, 2))
    grid = corrected.reshape(rows * cols, chans)
    cells = lax.broadcasted_iota(jnp.int32, (1, rows * cols), 1)
    levels = lax.broadcasted_iota(jnp.int32, (1, chans), 1)

    def advance(summed, portion):
        frac_lat = portion[0][:, None]
        frac_lon = portion[1][:, None]
        corner = portion[4].astype(jnp.int32)[:, None]
        level = portion[5].astype(jnp.int32)[:, None]
        weights = (1.0 - frac_lat) * (1.0 - frac_lon) * (cells == corner).astype(jnp.float32)
        weights = weights + (1.0 - frac_lat) * frac_lon * (cells == corner + 1).astype(jnp.float32)
        weights = weights + frac_lat * (1.0 - frac_lon) * (cells == corner + cols).astype(
            jnp.float32
        )
        weights = weights + frac_lat * frac_lon * (cells == corner + cols + 1).astype(jnp.float32)
        onehot = (levels == level).astype(jnp.float32)
        sampled = jnp.dot(
            weights, grid, precision=lax.Precision.HIGHEST, preferred_element_type=jnp.float32
        )
        predicted = jnp.sum(sampled * onehot, axis=1)
        misfit = portion[6] * portion[3] * (predicted - portion[2])
        summed = summed + lax.dot_general(
            weights,
            onehot * misfit[:, None],
            (((0,), (0,)), ((), ())),
            precision=lax.Precision.HIGHEST,
            preferred_element_type=jnp.float32,
        )
        return (summed, None)

    summed, unused = lax.scan(advance, jnp.zeros((rows * cols, chans), jnp.float32), fields)
    return summed.reshape(rows, cols, chans)


def by_tiles(
    state,
    weight_first,
    weight_second,
    obs_owner,
    obs_cell,
    obs_level,
    obs_count,
    obs_frac,
    obs_value,
    obs_weight,
):
    rows, cols, chans = state.shape
    wide_state = widen_tile(state)
    first = tile_conv(wide_state, weight_first, rows, cols, False)
    hidden = jax.nn.silu(first).astype(jnp.bfloat16)
    wide_hidden = widen_tile(hidden)
    corrected = state.astype(jnp.float32) + tile_conv(wide_hidden, weight_second, rows, cols, False)
    arrived = route_blocks(
        obs_owner, obs_cell, obs_level, obs_count, obs_frac, obs_value, obs_weight
    )
    adjoint = observe(corrected, arrived, rows, cols, chans)
    pullback = adjoint.astype(jnp.bfloat16)
    wide_pull = widen_tile(pullback)
    local_second = tile_grads(wide_hidden, pullback, rows, cols)
    back = tile_conv(wide_pull, weight_second, rows, cols, True)
    sig = jax.nn.sigmoid(first)
    pull_first = (back * sig * (1.0 + first * (1.0 - sig))).astype(jnp.bfloat16)
    wide_pull_first = widen_tile(pull_first)
    local_first = tile_grads(wide_state, pull_first, rows, cols)
    state_grad = adjoint + tile_conv(wide_pull_first, weight_first, rows, cols, True)
    grad_first, grad_second = lax.psum((local_first, local_second), ("lat", "lon"))
    return (state_grad, grad_first, grad_second)


def halo_rows(x):
    return x[-2:], x[:2]


def halo_pieces(x, sent):
    bands, tiles = lax.axis_size("lat"), lax.axis_size("lon")
    rows, cols, _ = x.shape
    north = lax.ppermute(sent[0], "lat", [(i, i + 1) for i in range(bands - 1)])
    south = lax.ppermute(sent[1], "lat", [(i + 1, i) for i in range(bands - 1)])
    last = jnp.concatenate([p[:, cols - 2 :] for p in (north, x, south)], axis=0)
    first = jnp.concatenate([p[:, :2] for p in (north, x, south)], axis=0)
    west = lax.ppermute(last, "lon", [(i, (i + 1) % tiles) for i in range(tiles)])
    east = lax.ppermute(first, "lon", [((i + 1) % tiles, i) for i in range(tiles)])
    return x, north, south, west, east


def gather_line(copies):
    half = copies.shape[0]
    same = [[2 * q + core for q in range(half)] for core in range(2)]
    return lax.all_to_all(copies, "lon", 0, 0, axis_index_groups=same, tiled=True)


def gather_line_backwards(x):
    tiles = lax.axis_size("lon")
    return jnp.stack(
        [x]
        + [
            lax.ppermute(x, "lon", [(i, (i + step) % tiles) for i in range(tiles)])
            for step in range(2, tiles, 2)
        ]
    )


def gather_bands(line):
    bands = lax.axis_size("lat")
    return [line] + [
        lax.ppermute(line, "lat", [(i, (i + step) % bands) for i in range(bands)])
        for step in range(1, bands)
    ]


def with_other_core(lines):
    swap = [(i, i ^ 1) for i in range(lax.axis_size("lon"))]
    pieces = []
    for line in lines:
        pieces += [line, lax.ppermute(line, "lon", swap)]
    return pieces


def per_device(
    state, weight_first, weight_second, obs_owner, obs_cell, obs_level, obs_count, obs_frac,
    obs_value, obs_weight,
):
    rows, cols, chans = state.shape
    bands = lax.axis_size("lat")
    devices = lax.axis_size(("lat", "lon"))
    if devices * rows * cols > WHOLE_CELLS:
        return by_tiles(
            state, weight_first, weight_second, obs_owner, obs_cell, obs_level, obs_count,
            obs_frac, obs_value, obs_weight,
        )
    slots = max(2, 3 * obs_value.shape[0] // (2 * devices))
    edges, obs_owner = lax.optimization_barrier((halo_rows(state), obs_owner))
    outgoing = route(
        devices, slots, chans, obs_owner, obs_cell, obs_level, obs_count, obs_frac, obs_value,
        obs_weight,
    )
    outgoing, sent = lax.optimization_barrier((outgoing, state))
    pieces = halo_pieces(state, edges)
    got = lax.all_to_all(outgoing, ("lat", "lon"), split_axis=0, concat_axis=0, tiled=True)
    line = gather_line_backwards(sent)
    line, pieces, got = lax.optimization_barrier((line, pieces, got))
    state_lines = gather_bands(line)
    half = lax.axis_size("lon") // 2
    adjoint, pullback, near_slope = forward(
        slots, bands, half, pieces, weight_first, weight_second, got
    )
    state_lines, pullback = lax.optimization_barrier((state_lines, pullback))
    state_pieces = with_other_core(state_lines)
    pull_lines = gather_bands(gather_line(pullback.reshape(half, rows, cols, chans)))
    firsts = whole(bands, state_pieces, weight_first, weight_second)
    pull_pieces = with_other_core(pull_lines[:1])
    far_lines, firsts = lax.optimization_barrier((pull_lines[1:], firsts))
    slope, hidden, turned, w2t = firsts
    pull_pieces += with_other_core(far_lines)
    swap = [(i, i ^ 1) for i in range(2 * half)]
    g2, pull = second_sums(bands, pull_pieces, hidden)
    g2_other = lax.ppermute(g2, "lon", swap)
    g1 = first_sums(slope, turned, pull, w2t)
    g1, g2_other = lax.optimization_barrier((g1, g2_other))
    g1_other = lax.ppermute(g1, "lon", swap)
    grad = local_grad(bands, pull_pieces, near_slope, adjoint, weight_first, weight_second)
    g1, g2 = g1 + g1_other, g2 + g2_other
    return grad.reshape(rows, cols, chans), g1, g2


def solution(mesh):
    both = P(("lat", "lon"), None)
    placed = (
        P("lat", "lon", None),
        P(),
        P(),
        both,
        both,
        both,
        P(("lat", "lon")),
        P(("lat", "lon"), None, None),
        both,
        both,
    )
    return jax.shard_map(
        per_device,
        mesh=mesh,
        in_specs=placed,
        out_specs=(P("lat", "lon", None), P(), P()),
        check_vma=False,
    )
```

```python
import functools
import math

import jax
import jax.numpy as jnp
from jax import lax
from jax.experimental import pallas as pl
from jax.experimental.pallas import tpu as pltpu
from jax.sharding import PartitionSpec as P

F32 = jnp.float32
BF16 = jnp.bfloat16
FIELDS = 5
SPAN = 32
WHOLE_CELLS = 4096


def params(mebibytes):
    return pltpu.CompilerParams(vmem_limit_bytes=mebibytes * 1024 * 1024)


def cost(flops, moved):
    return pl.CostEstimate(flops=int(flops), bytes_accessed=int(moved), transcendentals=0)


def vmem():
    return pl.BlockSpec(memory_space=pltpu.VMEM)


def anywhere():
    return pl.BlockSpec(memory_space=pl.ANY)


def iota(shape, dim, dtype=jnp.int32):
    return lax.broadcasted_iota(jnp.int32, shape, dim).astype(dtype)


def dot(x, y, precision=None):
    return jnp.dot(x, y, precision=precision, preferred_element_type=F32)


def dot_nt(x, y, precision=None):
    return lax.dot_general(
        x, y, (((1,), (1,)), ((), ())), precision=precision, preferred_element_type=F32
    )


def slot_layout(slots):
    full, rest = divmod(slots, 4)
    rows = full * FIELDS + (0 if rest == 0 else -(-FIELDS // 2))
    return full, rest, -(-rows // 8) * 8


def route_kernel(
    devices, slots, chans, owner_ref, count_ref, cell_ref, level_ref, frac_ref, value_ref,
    weight_ref, out_ref
):
    width, blocks = value_ref.shape
    owner = owner_ref[...].astype(F32)
    across = jnp.broadcast_to(owner, (blocks, blocks))
    down = across.T
    earlier = iota((blocks, blocks), 0) < iota((blocks, blocks), 1)
    hits = jnp.where(jnp.logical_and(across == down, earlier), 1.0, 0.0)
    rank = jnp.sum(hits, axis=0, keepdims=True)
    target = rank * float(devices) + owner
    places = iota((slots * devices, blocks), 0, F32) == target
    onehot = jnp.where(places, 1.0, 0.0)
    valid = iota((width, blocks), 0) < count_ref[...]
    fields = jnp.concatenate(
        [
            frac_ref[0],
            frac_ref[1],
            value_ref[...],
            jnp.where(valid, weight_ref[...], 0.0),
            (cell_ref[...] * chans + level_ref[...]).astype(F32),
        ],
        axis=0,
    )
    placed = dot_nt(onehot, fields, lax.Precision.HIGHEST)
    full, rest, rows = slot_layout(slots)
    out_ref[...] = jnp.zeros(out_ref.shape, F32)
    for slot in range(slots):
        for field in range(FIELDS):
            piece = placed[
                slot * devices : (slot + 1) * devices, field * width : (field + 1) * width
            ]
            if slot < 4 * full:
                row, lane = (slot // 4) * FIELDS + field, (slot % 4) * width
            else:
                row = full * FIELDS + field // 2
                lane = (field % 2) * 2 * width + (slot - 4 * full) * width
            out_ref[:, row, lane : lane + width] = piece


def route(devices, slots, chans, obs_owner, obs_cell, obs_level, obs_count, obs_frac, obs_value,
          obs_weight):
    blocks = obs_value.shape[0]
    rows = slot_layout(slots)[2]
    return pl.pallas_call(
        functools.partial(route_kernel, devices, slots, chans),
        out_shape=jax.ShapeDtypeStruct((devices, rows, 128), F32),
        in_specs=[vmem()] * 7,
        out_specs=vmem(),
        compiler_params=params(60),
        name="route",
    )(
        obs_owner.reshape(1, blocks),
        obs_count.reshape(1, blocks),
        obs_cell.T,
        obs_level.T,
        jnp.transpose(obs_frac, (1, 2, 0)),
        obs_value.T,
        obs_weight.T,
    )


def silu_parts(first):
    sig = 1.0 / (1.0 + jnp.exp(-first))
    return sig, first * sig


def inside_grid(rows, shape, bands):
    lat = lax.axis_index("lat") * rows + iota(shape, 0) - 1
    return jnp.logical_and(lat >= 0, lat < bands * rows)


def band_copies(bands, piece_refs, all_ref, sems):
    core = lax.axis_index("lon") & 1
    lat = lax.axis_index("lat")
    copies = []
    for offset in range(bands):
        band = (lat + bands - offset) % bands
        for side in range(2):
            copies.append(
                pltpu.make_async_copy(
                    piece_refs[2 * offset + side],
                    all_ref.at[core if side == 0 else 1 - core, band],
                    sems.at[offset, side],
                )
            )
    return copies


def nearby_copies(bands, piece_refs, near_ref, sems):
    half = piece_refs[0].shape[0]
    lon = lax.axis_index("lon")
    west = lax.shift_right_logical((lon + 2 * half - 1) & (2 * half - 1), 1)
    east = lax.shift_right_logical((lon + 1) & (2 * half - 1), 1)
    here = lax.shift_right_logical(lon, 1)
    copies = []
    for down, offset in enumerate((1, 0, bands - 1)):
        mine, other = piece_refs[2 * offset], piece_refs[2 * offset + 1]
        for over, (source, q) in enumerate(((other, west), (mine, here), (other, east))):
            copies.append(
                pltpu.make_async_copy(source.at[q], near_ref.at[down, over], sems.at[down, over])
            )
    return copies


def fill_line(bands, near_ref, line_ref):
    rows, cols, chans = near_ref.shape[2:]
    lat = lax.axis_index("lat")
    for down, (y, height, first) in enumerate(((0, 2, rows - 2), (2, rows, 0), (2 + rows, 2, 0))):
        band = lat + down - 1
        for over, (x, width, left) in enumerate(((0, 2, cols - 2), (2, cols, 0), (2 + cols, 2, 0))):
            part = near_ref[down, over].astype(F32)[
                first : first + height, left : left + width
            ]
            if down != 1:
                part = jnp.where(jnp.logical_and(band >= 0, band < bands), part, 0.0)
            line_ref[y : y + height, x : x + width, :] = part
    line_ref[:, cols + 4 :, :] = jnp.zeros(
        (rows + 4, line_ref.shape[1] - cols - 4, chans), F32
    )


def forward_kernel(slots, bands, group, parts, tile_ref, north_ref, south_ref, west_ref, east_ref,
                   w1_hbm, w2_hbm, got_ref, adj_ref, pull_ref, slope_ref, line_ref, shift_ref,
                   hid_ref, obs_ref, sum_ref, w1_ref, w2_ref, sems):
    w1_copy = pltpu.make_async_copy(w1_hbm, w1_ref, sems.at[0])
    w2_copy = pltpu.make_async_copy(w2_hbm, w2_ref, sems.at[1])
    w1_copy.start()
    w2_copy.start()
    rows, cols, chans = tile_ref.shape
    span = hid_ref.shape[1]
    line_ref[0:2, 2 : 2 + cols, :] = north_ref[...].astype(F32)
    line_ref[2 : 2 + rows, 2 : 2 + cols, :] = tile_ref[...].astype(F32)
    line_ref[2 + rows :, 2 : 2 + cols, :] = south_ref[...].astype(F32)
    line_ref[:, 0:2, :] = west_ref[...].astype(F32)
    line_ref[:, 2 + cols : 4 + cols, :] = east_ref[...].astype(F32)
    line_ref[:, cols + 4 :, :] = jnp.zeros(
        (rows + 4, line_ref.shape[1] - cols - 4, chans), F32
    )
    devices = got_ref.shape[0]
    full, rest, _ = slot_layout(slots)
    half = devices // 2
    for field in range(FIELDS):
        for part in range(full):
            obs_ref[field, part * devices : (part + 1) * devices, :] = got_ref[
                :, part * FIELDS + field, :
            ]
        if rest:
            tail = got_ref[:, full * FIELDS + field // 2, :]
            low, high = tail[:half], tail[half:]
            if field % 2 == 0:
                high = pltpu.roll(high, 64, 1)
            else:
                low = pltpu.roll(low, 64, 1)
            obs_ref[field, full * devices : full * devices + half, :] = jnp.where(
                iota((half, 128), 1) < 64, low, high
            )
    code = obs_ref[4].astype(jnp.int32)
    shift = chans.bit_length() - 1
    cell = lax.shift_right_logical(code, shift)
    obs_ref[4] = (code & (chans - 1)).astype(F32)
    obs_ref[0] = obs_ref[0] + lax.shift_right_logical(cell, 4).astype(F32)
    obs_ref[1] = obs_ref[1] + (cell & (cols - 1)).astype(F32)

    w1_copy.wait()
    first = jnp.zeros(((rows + 2) * span, chans), F32)
    for b in range(3):
        shift_ref[...] = (
            line_ref[:, b : b + span, :].astype(BF16).reshape((rows + 4) * span, chans)
        )
        for a in range(3):
            first = first + dot(
                shift_ref[a * span : a * span + (rows + 2) * span, :], w1_ref[3 * a + b]
            )
    sig, hidden = silu_parts(first)
    slope_ref[...] = sig * (1.0 + first * (1.0 - sig))
    hidden = hidden.astype(BF16).astype(F32).reshape(rows + 2, span, chans)
    hidden = jnp.where(inside_grid(rows, hidden.shape, bands), hidden, 0.0)
    hid_ref[...] = hidden
    w2_copy.wait()
    total = line_ref[2 : 2 + rows, 2 : 2 + cols, :].reshape(rows * cols, chans)
    for b in range(3):
        shift_ref[0 : (rows + 2) * cols, :] = (
            hid_ref[:, b : b + cols, :].astype(BF16).reshape((rows + 2) * cols, chans)
        )
        for a in range(3):
            total = total + dot(
                shift_ref[a * cols : a * cols + rows * cols, :], w2_ref[3 * a + b]
            )
    cells = rows * cols
    turned = total.T
    grid_high = turned.astype(BF16)
    grid_low = (turned - grid_high.astype(F32)).astype(BF16)
    grid_both = jnp.concatenate([grid_high, grid_low], axis=1)

    sum_ref[...] = jnp.zeros(sum_ref.shape, F32)
    count = obs_ref.shape[1] // (group * parts)
    row_ids = iota((rows, 128), 0, F32)
    col_ids = iota((cols, 128), 0, F32)
    level_ids = iota((chans, 128), 0, F32)

    def add_group(start):
        high, low, masks, marks = [], [], [], []
        for piece in range(group):
            mark = [obs_ref[field, pl.ds(start + piece, 1), :] for field in range(FIELDS)]
            up = jnp.maximum(0.0, 1.0 - jnp.abs(row_ids - mark[0]))
            along = jnp.maximum(0.0, 1.0 - jnp.abs(col_ids - mark[1]))
            weights = (up[:, None, :] * along[None, :, :]).reshape(cells, 128)
            weights_high = weights.astype(BF16)
            high.append(weights_high)
            low.append((weights - weights_high.astype(F32)).astype(BF16))
            masks.append(level_ids == mark[4])
            marks.append(mark)
        high = jnp.concatenate(high, axis=1)
        low = jnp.concatenate(low, axis=1)
        sampled = dot(grid_both, jnp.concatenate([high, high], axis=0)) + dot(grid_high, low)
        hot_high, hot_low = [], []
        for piece in range(group):
            mine = sampled[:, piece * 128 : (piece + 1) * 128]
            predicted = jnp.sum(jnp.where(masks[piece], mine, 0.0), axis=0, keepdims=True)
            misfit = marks[piece][3] * (predicted - marks[piece][2])
            misfit_high = misfit.astype(BF16).astype(F32)
            hot_high.append(jnp.where(masks[piece], misfit_high, 0.0).astype(BF16))
            hot_low.append(jnp.where(masks[piece], misfit - misfit_high, 0.0).astype(BF16))
        hot_high = jnp.concatenate(hot_high, axis=1)
        hot_low = jnp.concatenate(hot_low, axis=1)
        mixed = dot_nt(
            jnp.concatenate([hot_high, hot_low], axis=0), jnp.concatenate([high, low], axis=0)
        )
        return mixed[:chans, :cells] + (mixed[chans:, :cells] + mixed[:chans, cells:])

    def step(index, carry):
        total = sum_ref[...]
        for part in range(parts):
            total = total + add_group((index * parts + part) * group)
        sum_ref[...] = total
        return carry

    lax.fori_loop(0, count, step, 0)
    adjoint = sum_ref[...].T
    adj_ref[...] = adjoint
    for copy in range(pull_ref.shape[0]):
        pull_ref[copy] = adjoint.astype(BF16)


def forward(slots, bands, copies, pieces, w1, w2, got):
    rows, cols, chans = pieces[0].shape
    devices = got.shape[0]
    full, rest, _ = slot_layout(slots)
    groups = full * devices + (devices // 2 if rest else 0)
    return pl.pallas_call(
        functools.partial(forward_kernel, slots, bands, 2, 8),
        out_shape=[
            jax.ShapeDtypeStruct((rows * cols, chans), F32),
            jax.ShapeDtypeStruct((copies, rows * cols, chans), BF16),
            jax.ShapeDtypeStruct(((rows + 2) * SPAN, chans), F32),
        ],
        in_specs=[vmem()] * 5 + [anywhere()] * 2 + [vmem()],
        out_specs=[vmem()] * 3,
        scratch_shapes=[
            pltpu.VMEM((rows + 4, SPAN + 8, chans), F32),
            pltpu.VMEM(((rows + 4) * SPAN, chans), BF16),
            pltpu.VMEM((rows + 2, SPAN, chans), F32),
            pltpu.VMEM((FIELDS, groups, 128), F32),
            pltpu.VMEM((chans, rows * cols), F32),
            pltpu.VMEM(w1.shape, BF16),
            pltpu.VMEM(w2.shape, BF16),
            pltpu.SemaphoreType.DMA((2,)),
        ],
        compiler_params=params(58),
        cost_estimate=cost(4e9, 4e6),
        name="forward",
    )(*pieces, w1, w2, got)


def spread_matrix(steps, tiles, backwards):
    lons = 16 * steps
    half = tiles // 2
    place = iota(((steps + 2) * 16, lons), 0)
    lon = (place & 15) * steps + lax.shift_right_logical(place, 4) - 1
    lon = jnp.where(lon < 0, lon + lons, jnp.where(lon >= lons, lon - lons, lon))
    column = iota(((steps + 2) * 16, lons), 1)
    chunk = lax.shift_right_logical(column, 4)
    core = lax.shift_right_logical(chunk, half.bit_length() - 1)
    here = lax.shift_right_logical(lax.axis_index("lon"), 1)
    q = chunk & (half - 1)
    if backwards:
        q = (here - q) & (half - 1)
    column = (2 * q + core) * 16 + (column & 15)
    return jnp.where(column == lon, 1.0, 0.0)


def spread(line_of, start, lats, matrix, pad_ref):
    steps = pad_ref.shape[1] - 2
    for row in range(pad_ref.shape[0]):
        lat = start + row
        inside = jnp.logical_and(lat >= 0, lat < lats)
        line = line_of(jnp.clip(lat, 0, lats - 1))
        chosen = jnp.where(inside, matrix, 0.0).astype(BF16)
        pad_ref[row] = dot(chosen, line).astype(BF16).reshape(steps + 2, 16, line.shape[1])


def conv_block(pad_ref, weight_ref, start, rows, flipped):
    steps = pad_ref.shape[1] - 2
    chans = pad_ref.shape[3]
    pieces = []
    for a in range(3):
        for b in range(3):
            da, db = (2 - a, 2 - b) if flipped else (a, b)
            piece = pad_ref[pl.ds(start + da, rows), db : db + steps]
            pieces.append(piece.reshape(rows * steps * 16, chans))
    return dot(jnp.concatenate(pieces, axis=1), weight_ref[...].reshape(9 * chans, chans))


def whole_kernel(block, *refs):
    bands = refs[-2].shape[1]
    piece_refs, refs = refs[: 2 * bands], refs[2 * bands :]
    w1_ref, w2_ref, slope_ref, hidden_ref, state_ref, w2t_ref, pad_ref, all_ref, sems = refs
    _, _, half, rows, group, chans = all_ref.shape
    lats, lons = bands * rows, 2 * half * group
    steps = lons // 16
    size = block * lons
    mine = pad_ref.shape[0] - 4
    base = (lax.axis_index("lon") & 1) * mine
    copies = band_copies(bands, piece_refs, all_ref, sems)
    for copy in copies:
        copy.start()
    matrix = spread_matrix(steps, 2 * half, True)
    for tap in range(9):
        w2t_ref[tap] = w2_ref[tap].T
    for copy in copies:
        copy.wait()
    spread(
        lambda lat: all_ref[:, lat // rows, :, lat % rows].reshape(lons, chans),
        base - 2, lats, matrix, pad_ref,
    )

    def step(index, carry):
        start = index * block
        first = conv_block(pad_ref, w1_ref, start, block, False)
        sig, hidden = silu_parts(first)
        at = pl.ds(pl.multiple_of(index * size, size), size)
        slope_ref[at, :] = sig * (1.0 + first * (1.0 - sig))
        lat = base - 1 + start + lax.shift_right_logical(
            iota((size, chans), 0), lons.bit_length() - 1
        )
        hidden = jnp.where(jnp.logical_and(lat >= 0, lat < lats), hidden, 0.0)
        hidden_ref[:, at] = hidden.astype(BF16).T
        centre = pad_ref[pl.ds(start + 1, block), 1 : 1 + steps].reshape(size, chans)
        state_ref[:, at] = centre.T
        return carry

    lax.fori_loop(0, (mine + 2) // block, step, 0)


def whole(bands, pieces, w1, w2):
    half, rows, group, chans = pieces[0].shape
    lats, lons = bands * rows, 2 * half * group
    mine = lats // 2
    steps = lons // 16
    cells = (mine + 2) * lons
    return pl.pallas_call(
        functools.partial(whole_kernel, 3),
        out_shape=[
            jax.ShapeDtypeStruct((cells, chans), F32),
            jax.ShapeDtypeStruct((chans, cells), BF16),
            jax.ShapeDtypeStruct((chans, cells), BF16),
            jax.ShapeDtypeStruct((9, chans, chans), BF16),
        ],
        in_specs=[anywhere()] * len(pieces) + [vmem()] * 2,
        out_specs=[vmem()] * 4,
        scratch_shapes=[
            pltpu.VMEM((mine + 4, steps + 2, 16, chans), BF16),
            pltpu.VMEM((2, bands) + pieces[0].shape, BF16),
            pltpu.SemaphoreType.DMA((bands, 2)),
        ],
        compiler_params=params(22),
        cost_estimate=cost(6e9, 10e6),
        name="whole",
    )(*pieces, w1, w2)


def tap_sums(turned_ref, pad_ref, first_row, rows, sum_ref, out_ref, sem):
    steps = pad_ref.shape[1] - 2
    chans = pad_ref.shape[3]
    lons = steps * 16

    def step(tap, carry):
        a, b = tap // 3, tap % 3
        piece = pad_ref[first_row : first_row + rows, pl.ds(2 - b, steps)]
        at = pl.ds(pl.multiple_of(a * lons, lons), rows * lons)
        sum_ref[tap] = dot(turned_ref[:, at], piece.reshape(rows * lons, chans))
        pltpu.make_async_copy(sum_ref.at[tap], out_ref.at[tap], sem.at[tap]).start()
        return carry

    lax.fori_loop(0, 9, step, 0)


def second_kernel(bands, *refs):
    piece_refs, refs = refs[: 2 * bands], refs[2 * bands :]
    hidden_hbm, g2_hbm, pull_ref, all_ref, hidden_ref, g2_ref, piece_sems, sem, g2_sems = refs
    steps = pull_ref.shape[1] - 2
    chans = pull_ref.shape[3]
    lons = steps * 16
    _, _, half, rows, _, _ = all_ref.shape
    lats = bands * rows
    mine = lats // 2
    base = (lax.axis_index("lon") & 1) * mine
    copies = band_copies(bands, piece_refs, all_ref, piece_sems)
    hidden_copy = pltpu.make_async_copy(hidden_hbm, hidden_ref, sem)
    for copy in copies:
        copy.start()
    hidden_copy.start()
    matrix = spread_matrix(steps, 2 * half, False)
    for copy in copies:
        copy.wait()
    spread(
        lambda lat: all_ref[:, lat // rows, :, lat % rows].reshape(lons, chans),
        base - 1, lats, matrix, pull_ref,
    )
    hidden_copy.wait()
    tap_sums(hidden_ref, pull_ref, 1, mine, g2_ref, g2_hbm, g2_sems)
    for tap in range(9):
        pltpu.make_async_copy(g2_ref.at[tap], g2_hbm.at[tap], g2_sems.at[tap]).wait()


def second_sums(bands, pieces, hidden):
    half, rows, group, chans = pieces[0].shape
    lats, lons = bands * rows, 2 * half * group
    ours = lats // 2
    return pl.pallas_call(
        functools.partial(second_kernel, bands),
        out_shape=[
            jax.ShapeDtypeStruct((9, chans, chans), F32),
            jax.ShapeDtypeStruct((ours + 2, lons // 16 + 2, 16, chans), BF16),
        ],
        in_specs=[anywhere()] * (len(pieces) + 1),
        out_specs=[anywhere(), vmem()],
        scratch_shapes=[
            pltpu.VMEM((2, bands) + pieces[0].shape, BF16),
            pltpu.VMEM(hidden.shape, BF16),
            pltpu.VMEM((9, chans, chans), F32),
            pltpu.SemaphoreType.DMA((bands, 2)),
            pltpu.SemaphoreType.DMA,
            pltpu.SemaphoreType.DMA((9,)),
        ],
        compiler_params=params(20),
        cost_estimate=cost(5e9, 8e6),
        name="second_sums",
    )(*pieces, hidden)


def first_kernel(block, slope_hbm, state_hbm, pull_ref, w2t_ref, g1_hbm, first_ref, slope_ref,
                 state_ref, g1_ref, sems, g1_sems):
    steps = pull_ref.shape[1] - 2
    chans = pull_ref.shape[3]
    mine = first_ref.shape[0]
    lons = steps * 16
    size = block * lons
    slope_copy = pltpu.make_async_copy(
        slope_hbm.at[pl.ds(lons, mine * lons), :], slope_ref, sems.at[0]
    )
    state_copy = pltpu.make_async_copy(state_hbm, state_ref, sems.at[1])
    slope_copy.start()
    state_copy.start()
    slope_copy.wait()

    def step(index, carry):
        start = index * block
        back = conv_block(pull_ref, w2t_ref, start, block, True)
        at = pl.ds(pl.multiple_of(index * size, size), size)
        pull = (back * slope_ref[at, :]).astype(BF16).astype(F32)
        pull = pull.reshape(block, steps, 16, chans)
        last, head = pull[:, steps - 1], pull[:, 0]
        before = jnp.concatenate([last[:, 15:], last[:, :15]], axis=1)
        after = jnp.concatenate([head[:, 1:], head[:, :1]], axis=1)
        to = pl.ds(start, block)
        first_ref[to, 1 : 1 + steps] = pull.astype(BF16)
        first_ref[to, 0] = before.astype(BF16)
        first_ref[to, steps + 1] = after.astype(BF16)
        return carry

    lax.fori_loop(0, mine // block, step, 0)
    state_copy.wait()
    tap_sums(state_ref, first_ref, 0, mine, g1_ref, g1_hbm, g1_sems)
    for tap in range(9):
        pltpu.make_async_copy(g1_ref.at[tap], g1_hbm.at[tap], g1_sems.at[tap]).wait()


def first_sums(slope, state, pull, w2t):
    ours, wide, group, chans = pull.shape[0] - 2, *pull.shape[1:]
    lons = (wide - 2) * group
    return pl.pallas_call(
        functools.partial(first_kernel, 4),
        out_shape=jax.ShapeDtypeStruct((9, chans, chans), F32),
        in_specs=[anywhere()] * 2 + [vmem()] * 2,
        out_specs=anywhere(),
        scratch_shapes=[
            pltpu.VMEM((ours, wide, group, chans), BF16),
            pltpu.VMEM((ours * lons, chans), F32),
            pltpu.VMEM(state.shape, BF16),
            pltpu.VMEM((9, chans, chans), F32),
            pltpu.SemaphoreType.DMA((2,)),
            pltpu.SemaphoreType.DMA((9,)),
        ],
        compiler_params=params(24),
        cost_estimate=cost(10e9, 8e6),
        name="first_sums",
    )(slope, state, pull, w2t)


def local_kernel(bands, *refs):
    piece_refs, refs = refs[: 2 * bands], refs[2 * bands :]
    slope_ref, adj_ref, w1_ref, w2_ref, grad_ref = refs[:5]
    near_ref, line_ref, shift_ref, pull_ref, sems = refs[5:]
    rows, cols, chans = near_ref.shape[2:]
    span = pull_ref.shape[1]
    copies = nearby_copies(bands, piece_refs, near_ref, sems)
    for copy in copies:
        copy.start()
    for copy in copies:
        copy.wait()
    fill_line(bands, near_ref, line_ref)
    back = jnp.zeros(((rows + 2) * span, chans), F32)
    for b in range(3):
        shift_ref[...] = (
            line_ref[:, 2 - b : 2 - b + span, :].astype(BF16).reshape((rows + 4) * span, chans)
        )
        for a in range(3):
            piece = shift_ref[(2 - a) * span : (2 - a) * span + (rows + 2) * span, :]
            back = back + dot_nt(piece, w2_ref[3 * a + b])
    pull = (back * slope_ref[...]).reshape(rows + 2, span, chans)
    pull_ref[...] = jnp.where(inside_grid(rows, pull.shape, bands), pull, 0.0)
    total = adj_ref[...]
    for b in range(3):
        shift_ref[0 : (rows + 2) * cols, :] = (
            pull_ref[:, 2 - b : 2 - b + cols, :].astype(BF16).reshape((rows + 2) * cols, chans)
        )
        for a in range(3):
            piece = shift_ref[(2 - a) * cols : (2 - a) * cols + rows * cols, :]
            total = total + dot_nt(piece, w1_ref[3 * a + b])
    grad_ref[...] = total


def local_grad(bands, pieces, slope, adjoint, w1, w2):
    half, rows, cols, chans = pieces[0].shape
    return pl.pallas_call(
        functools.partial(local_kernel, bands),
        out_shape=jax.ShapeDtypeStruct((rows * cols, chans), F32),
        in_specs=[anywhere()] * len(pieces) + [vmem()] * 4,
        out_specs=vmem(),
        scratch_shapes=[
            pltpu.VMEM((3, 3, rows, cols, chans), BF16),
            pltpu.VMEM((rows + 4, SPAN + 8, chans), F32),
            pltpu.VMEM(((rows + 4) * SPAN, chans), BF16),
            pltpu.VMEM((rows + 2, SPAN, chans), F32),
            pltpu.SemaphoreType.DMA((3, 3)),
        ],
        compiler_params=params(16),
        cost_estimate=cost(3e9, 4e6),
        name="local_grad",
    )(*pieces, slope, adjoint, w1, w2)


def with_halo(x, sides, width, wrap):
    for axis, dim in sides:
        count, length = (lax.axis_size(axis), x.shape[dim])
        up = [(i, (i + 1) % count) for i in range(count if wrap else count - 1)]
        down = [(j, i) for i, j in up]
        last = lax.slice_in_dim(x, length - width, length, axis=dim)
        first = lax.slice_in_dim(x, 0, width, axis=dim)
        before = lax.ppermute(last, axis, up)
        after = lax.ppermute(first, axis, down)
        x = jnp.concatenate([before, x, after], axis=dim)
    return x


def widen_tile(field):
    across = with_halo(field, (("lon", 1),), 1, True)
    return with_halo(across, (("lat", 0),), 1, False)


def tile_conv(padded, weight, rows, cols, flipped):
    total = jnp.zeros((rows * cols, weight.shape[2]), jnp.float32)
    for first_tap in range(3):
        for second_tap in range(3):
            if flipped:
                piece = padded[
                    2 - first_tap : 2 - first_tap + rows, 2 - second_tap : 2 - second_tap + cols
                ]
                total = total + lax.dot_general(
                    piece.reshape(rows * cols, -1),
                    weight[3 * first_tap + second_tap],
                    (((1,), (1,)), ((), ())),
                    preferred_element_type=jnp.float32,
                )
            else:
                piece = padded[first_tap : first_tap + rows, second_tap : second_tap + cols]
                total = total + jnp.dot(
                    piece.reshape(rows * cols, -1),
                    weight[3 * first_tap + second_tap],
                    preferred_element_type=jnp.float32,
                )
    return total.reshape(rows, cols, -1)


def tile_grads(padded, pullback, rows, cols):
    flat_pull = pullback.reshape(rows * cols, -1)
    result = []
    for first_tap in range(3):
        for second_tap in range(3):
            piece = padded[first_tap : first_tap + rows, second_tap : second_tap + cols].reshape(
                rows * cols, -1
            )
            result.append(
                lax.dot_general(
                    piece, flat_pull, (((0,), (0,)), ((), ())), preferred_element_type=jnp.float32
                )
            )
    return jnp.stack(result)


def route_blocks(obs_owner, obs_cell, obs_level, obs_count, obs_frac, obs_value, obs_weight):
    devices = lax.axis_size(("lat", "lon"))
    blocks, width = obs_value.shape
    slots = max(2, 3 * blocks // (2 * devices))
    owner = obs_owner[:, 0]
    order = lax.broadcasted_iota(jnp.int32, (blocks, blocks), 1) < lax.broadcasted_iota(
        jnp.int32, (blocks, blocks), 0
    )
    earlier = jnp.logical_and(owner[:, None] == owner[None, :], order)
    rank = jnp.sum(earlier.astype(jnp.int32), axis=1)
    target = owner * slots + rank
    valid = (lax.broadcasted_iota(jnp.int32, (blocks, width), 1) < obs_count[:, None]).astype(
        jnp.float32
    )
    packed = jnp.stack(
        [
            obs_frac[:, 0, :],
            obs_frac[:, 1, :],
            obs_value,
            obs_weight,
            obs_cell.astype(jnp.float32),
            obs_level.astype(jnp.float32),
            valid,
        ],
        axis=1,
    )
    outgoing = jnp.zeros((devices * slots, 7, width), jnp.float32).at[target].set(packed)
    return lax.all_to_all(outgoing, ("lat", "lon"), split_axis=0, concat_axis=0, tiled=True)


def observe(corrected, arrived, rows, cols, chans):
    fields = jnp.transpose(arrived, (1, 0, 2)).reshape(7, -1)
    row_total = fields.shape[1]
    span_rows = math.gcd(row_total, 1024)
    fields = jnp.transpose(fields.reshape(7, row_total // span_rows, span_rows), (1, 0, 2))
    grid = corrected.reshape(rows * cols, chans)
    cells = lax.broadcasted_iota(jnp.int32, (1, rows * cols), 1)
    levels = lax.broadcasted_iota(jnp.int32, (1, chans), 1)

    def advance(summed, portion):
        frac_lat = portion[0][:, None]
        frac_lon = portion[1][:, None]
        corner = portion[4].astype(jnp.int32)[:, None]
        level = portion[5].astype(jnp.int32)[:, None]
        weights = (1.0 - frac_lat) * (1.0 - frac_lon) * (cells == corner).astype(jnp.float32)
        weights = weights + (1.0 - frac_lat) * frac_lon * (cells == corner + 1).astype(jnp.float32)
        weights = weights + frac_lat * (1.0 - frac_lon) * (cells == corner + cols).astype(
            jnp.float32
        )
        weights = weights + frac_lat * frac_lon * (cells == corner + cols + 1).astype(jnp.float32)
        onehot = (levels == level).astype(jnp.float32)
        sampled = jnp.dot(
            weights, grid, precision=lax.Precision.HIGHEST, preferred_element_type=jnp.float32
        )
        predicted = jnp.sum(sampled * onehot, axis=1)
        misfit = portion[6] * portion[3] * (predicted - portion[2])
        summed = summed + lax.dot_general(
            weights,
            onehot * misfit[:, None],
            (((0,), (0,)), ((), ())),
            precision=lax.Precision.HIGHEST,
            preferred_element_type=jnp.float32,
        )
        return (summed, None)

    summed, unused = lax.scan(advance, jnp.zeros((rows * cols, chans), jnp.float32), fields)
    return summed.reshape(rows, cols, chans)


def by_tiles(
    state,
    weight_first,
    weight_second,
    obs_owner,
    obs_cell,
    obs_level,
    obs_count,
    obs_frac,
    obs_value,
    obs_weight,
):
    rows, cols, chans = state.shape
    wide_state = widen_tile(state)
    first = tile_conv(wide_state, weight_first, rows, cols, False)
    hidden = jax.nn.silu(first).astype(jnp.bfloat16)
    wide_hidden = widen_tile(hidden)
    corrected = state.astype(jnp.float32) + tile_conv(wide_hidden, weight_second, rows, cols, False)
    arrived = route_blocks(
        obs_owner, obs_cell, obs_level, obs_count, obs_frac, obs_value, obs_weight
    )
    adjoint = observe(corrected, arrived, rows, cols, chans)
    pullback = adjoint.astype(jnp.bfloat16)
    wide_pull = widen_tile(pullback)
    local_second = tile_grads(wide_hidden, pullback, rows, cols)
    back = tile_conv(wide_pull, weight_second, rows, cols, True)
    sig = jax.nn.sigmoid(first)
    pull_first = (back * sig * (1.0 + first * (1.0 - sig))).astype(jnp.bfloat16)
    wide_pull_first = widen_tile(pull_first)
    local_first = tile_grads(wide_state, pull_first, rows, cols)
    state_grad = adjoint + tile_conv(wide_pull_first, weight_first, rows, cols, True)
    grad_first, grad_second = lax.psum((local_first, local_second), ("lat", "lon"))
    return (state_grad, grad_first, grad_second)


def halo_pieces(x):
    bands, tiles = lax.axis_size("lat"), lax.axis_size("lon")
    rows, cols, _ = x.shape
    north = lax.ppermute(x[rows - 2 :], "lat", [(i, i + 1) for i in range(bands - 1)])
    south = lax.ppermute(x[:2], "lat", [(i + 1, i) for i in range(bands - 1)])
    last = jnp.concatenate([p[:, cols - 2 :] for p in (north, x, south)], axis=0)
    first = jnp.concatenate([p[:, :2] for p in (north, x, south)], axis=0)
    west = lax.ppermute(last, "lon", [(i, (i + 1) % tiles) for i in range(tiles)])
    east = lax.ppermute(first, "lon", [((i + 1) % tiles, i) for i in range(tiles)])
    return x, north, south, west, east


def gather_line(copies):
    half = copies.shape[0]
    same = [[2 * q + core for q in range(half)] for core in range(2)]
    return lax.all_to_all(copies, "lon", 0, 0, axis_index_groups=same, tiled=True)


def gather_line_backwards(x):
    tiles = lax.axis_size("lon")
    return jnp.stack(
        [x]
        + [
            lax.ppermute(x, "lon", [(i, (i + step) % tiles) for i in range(tiles)])
            for step in range(2, tiles, 2)
        ]
    )


def gather_bands(line):
    bands = lax.axis_size("lat")
    return [line] + [
        lax.ppermute(line, "lat", [(i, (i + step) % bands) for i in range(bands)])
        for step in range(1, bands)
    ]


def with_other_core(lines):
    swap = [(i, i ^ 1) for i in range(lax.axis_size("lon"))]
    pieces = []
    for line in lines:
        pieces += [line, lax.ppermute(line, "lon", swap)]
    return pieces


def per_device(
    state, weight_first, weight_second, obs_owner, obs_cell, obs_level, obs_count, obs_frac,
    obs_value, obs_weight,
):
    rows, cols, chans = state.shape
    bands = lax.axis_size("lat")
    devices = lax.axis_size(("lat", "lon"))
    if devices * rows * cols > WHOLE_CELLS:
        return by_tiles(
            state, weight_first, weight_second, obs_owner, obs_cell, obs_level, obs_count,
            obs_frac, obs_value, obs_weight,
        )
    slots = max(2, 3 * obs_value.shape[0] // (2 * devices))
    outgoing = route(
        devices, slots, chans, obs_owner, obs_cell, obs_level, obs_count, obs_frac, obs_value,
        obs_weight,
    )
    outgoing, sent = lax.optimization_barrier((outgoing, state))
    pieces = halo_pieces(state)
    got = lax.all_to_all(outgoing, ("lat", "lon"), split_axis=0, concat_axis=0, tiled=True)
    line = gather_line_backwards(sent)
    line, pieces, got = lax.optimization_barrier((line, pieces, got))
    state_lines = gather_bands(line)
    half = lax.axis_size("lon") // 2
    adjoint, pullback, near_slope = forward(
        slots, bands, half, pieces, weight_first, weight_second, got
    )
    state_lines, pullback = lax.optimization_barrier((state_lines, pullback))
    state_pieces = with_other_core(state_lines)
    pull_lines = gather_bands(gather_line(pullback.reshape(half, rows, cols, chans)))
    firsts = whole(bands, state_pieces, weight_first, weight_second)
    pull_lines, firsts = lax.optimization_barrier((pull_lines, firsts))
    slope, hidden, turned, w2t = firsts
    pull_pieces = with_other_core(pull_lines)
    swap = [(i, i ^ 1) for i in range(2 * half)]
    g2, pull = second_sums(bands, pull_pieces, hidden)
    g2_other = lax.ppermute(g2, "lon", swap)
    g1 = first_sums(slope, turned, pull, w2t)
    g1, g2_other = lax.optimization_barrier((g1, g2_other))
    g1_other = lax.ppermute(g1, "lon", swap)
    grad = local_grad(bands, pull_pieces, near_slope, adjoint, weight_first, weight_second)
    g1, g2 = g1 + g1_other, g2 + g2_other
    return grad.reshape(rows, cols, chans), g1, g2


def solution(mesh):
    both = P(("lat", "lon"), None)
    placed = (
        P("lat", "lon", None),
        P(),
        P(),
        both,
        both,
        both,
        P(("lat", "lon")),
        P(("lat", "lon"), None, None),
        both,
        both,
    )
    return jax.shard_map(
        per_device,
        mesh=mesh,
        in_specs=placed,
        out_specs=(P("lat", "lon", None), P(), P()),
        check_vma=False,
    )
```
